32 devices in a mesh: groups: 2 (over y), ep: 4 (over z), tp: 4 (over x, core).
Axes of the slice: x: 2, y: 2, z: 4, core: 2. Of those that a mesh axis runs over, the one named last changes fastest.
Arguments:
- residual: bfloat16 [128, 3072], P(('groups', 'ep'), 'tp'), parts along dimension 0, may hold values from -6 to 6
- queries: bfloat16 [128, 3072], P(('groups', 'ep'), 'tp'), parts along dimension 0, may hold values from -150 to 150
- token_keys: bfloat16 [128, 1024], P(('groups', 'ep'), 'tp'), parts along dimension 0, may hold values from -5 to 5
- token_values: bfloat16 [128, 1024], P(('groups', 'ep'), 'tp'), parts along dimension 0, may hold values from -5 to 5
- stored_keys: bfloat16 [128, 128, 1024], P(('groups', 'ep'), None, 'tp'), parts along dimension 0, may hold values from -5 to 5
- stored_values: bfloat16 [128, 128, 1024], P(('groups', 'ep'), None, 'tp'), parts along dimension 0, may hold values from -5 to 5
- lengths: int32 [128], P(('groups', 'ep')), parts along dimension 0, may hold values from 2 to 128
- norm_gain_vector: float32 [3072], P('tp'), may hold values from 0.1 to 1.9
- router: bfloat16 [3072, 4], P('tp'), may hold values from -0.109375 to 0.109375
- expert_gate_weight: bfloat16 [3072, 32768], P(None, ('ep', 'tp')), may hold values from -0.109375 to 0.109375
- expert_up_weight: bfloat16 [3072, 32768], P(None, ('ep', 'tp')), may hold values from -0.109375 to 0.109375
- expert_down_weight: bfloat16 [32768, 3072], P(('ep', 'tp')), may hold values from -0.0625 to 0.0625
- adapter_down_map: bfloat16 [3072, 512], P('tp'), may hold values from -0.109375 to 0.109375
- adapter_up_map: bfloat16 [128, 32768], P(None, ('ep', 'tp')), may hold values from -0.75 to 0.75
- routes: int32 [128, 2], P(('groups', 'ep')), parts along dimension 0, may hold values from 0 to 3, all different within a row; in each aligned block of 16 rows (0 to 15, 16 to 31, ...) at most 10 rows name the same one
- tenants: int32 [128], P(('groups', 'ep')), parts along dimension 0, may hold values from 0 to 7
Outputs:
- layer_out: bfloat16 [128, 3072], P(('groups', 'ep'), 'tp'), parts along dimension 0
The draws below stay inside these ranges and needn't reach their ends.
There are 2 independent parts, one for each index of `groups`. The reference program is written for one: setup_inputs(seed, part) draws one part's arguments, and reference() takes and returns one part's arrays. A program takes and returns all parts, laid end to end along the dimension named above; an argument that names none is the same for every part. Nothing has to cross between parts.
Inputs may be any that keep to these rules, and one draw needn't show every extreme that they name: `routes`: in the 16 rows of one index of ep no expert is named by more than 10 rows; the two experts of a row differ.
All inputs are finite; a program needn't handle non-finite values.
Results may differ from the reference program's by a relative error of at most 0.0061.
Values may be sent and summed in bfloat16 or wider, within the bound.
No kernel may reach another device: no remote copies, remote signals or barrier semaphores. Data moves between devices by JAX's collectives and lax.ppermute only.
A program may use at most 128 MiB of HBM per device.

```python
import math
import jax
import jax.numpy as jnp
import numpy as np
from jax import lax

HEADS = 24
KVH = 8
HD = 128
MODEL_WIDTH = 3072
EXPERT_COUNT = 4
EXPERT_HIDDEN = 8192
ADAPTER_RANK = 16
TENANT_COUNT = 8
ROW_DEV = 16
CACHE = 128
CAP = 10
ROWS = 64


def cache_base(key):
    return jnp.clip(jax.random.normal(key, (ROWS, CACHE, KVH * HD), jnp.float32), -5.0, 5.0)


def draw_stored_keys(key, part):
    base_keys = cache_base(key)
    return base_keys.astype(jnp.bfloat16)


def draw_queries(key, part):
    key = jax.random.fold_in(key, 7)
    fresh_rows = jnp.clip(jax.random.normal(key, (ROWS, HEADS * HD), jnp.float32), -5.0, 5.0)
    return fresh_rows.astype(jnp.bfloat16)


def with_ends(array, rng, smallest, top_value):
    dims = array.shape
    index_at = [jax.random.randint(jax.random.fold_in(rng, axis), (), 0, dims[axis]) for axis in range(len(dims))]
    array = array.at[tuple(index_at)].set(smallest)
    longest = dims.index(max(dims))
    index_at[longest] = (index_at[longest] + 1) % dims[longest]
    return array.at[tuple(index_at)].set(top_value)


def shard_levels(own_key, shape, cuts, low, top_value):
    factor_of = 1.0
    for dim, parts in cuts:
        draws = jax.random.uniform(jax.random.fold_in(jax.random.fold_in(own_key, 6), dim), (parts,), jnp.float32, low / len(cuts), top_value / len(cuts))
        factor_of = factor_of * jnp.repeat(jnp.exp(draws), shape[dim] // parts).reshape((-1,) + (1,) * (len(shape) - 1 - dim))
    return factor_of


def routed_block(stream_key, own, number, rows, count, top, most, lean):
    ranking = jax.random.permutation(stream_key, count)
    heavy_load, usual = portions_of(count, rows * top, most, lean, True), portions_of(count, rows * top, most, lean, False)
    places = jnp.arange(count)

    def named(sizes, turn):
        used = int((sizes > 0).sum())
        fixed = max(1, used // 4)
        moved = fixed + (places - fixed + turn * (used - fixed)) % max(1, count - fixed)
        return jnp.zeros((count,), jnp.int32).at[ranking[jnp.where(places < fixed, places, moved)]].set(jnp.asarray(sizes, jnp.int32))

    sizes = jnp.where(number % 4 == 0, named(heavy_load, number // 4), named(usual, number - number // 4 - 1))
    mixed = jax.random.permutation(jax.random.fold_in(own, 3), count)
    donor, taker = mixed[0:count // 2 * 2:2], mixed[1:count // 2 * 2:2]
    room = jnp.minimum(sizes[donor] - 1, most - sizes[taker]) // 2
    room = jnp.where((donor == ranking[0]) | (taker == ranking[0]) | (sizes[taker] == 0), 0, jnp.maximum(room, 0))
    moved = jax.random.randint(jax.random.fold_in(own, 4), (count // 2,), 0, 1 << 20) % (room + 1)
    sizes = sizes.at[donor].add(-moved).at[taker].add(moved)
    members = jnp.searchsorted(jnp.cumsum(sizes), jnp.arange(rows * top), side="right").astype(jnp.int32)
    grid = members.reshape(top, rows).T
    grid = grid[jax.random.permutation(jax.random.fold_in(own, 1), rows)]
    turn = jax.random.randint(jax.random.fold_in(own, 2), (rows, 1), 0, top)
    return jnp.take_along_axis(grid, (jnp.arange(top)[None, :] + turn) % top, axis=1)


def portions_of(number_of, total, bound, skew, full):
    loads = [(1 << 20) // math.isqrt(standing ** skew) + 1 for standing in range(1, number_of + 1)]
    largest = bound if full else min(bound, max(-(-total // number_of), total * loads[0] // sum(loads)))
    least = 1 if total - largest >= number_of - 1 else 0
    given, spare = [largest] + [least] * (number_of - 1), total - largest - least * (number_of - 1)
    while spare > 0:
        movable = [i for i in range(1, number_of) if given[i] < largest] or [i for i in range(1, number_of) if given[i] < bound]
        whole, left = sum([loads[i] for i in movable]), spare
        for i in movable:
            addition = min(bound - given[i], max(1, left * loads[i] // whole), spare)
            given[i] = given[i] + addition
            spare = spare - addition
    return np.array(given)


def gaussian(own_key, shape, width, most, shards=(), kind=jnp.bfloat16):
    entries = width * jax.random.normal(own_key, shape, jnp.float32)
    if shards:
        entries = entries * shard_levels(own_key, shape, shards, -0.22, 0.18)
    return jnp.clip(entries, -most, most).astype(kind)


def setup_inputs(seed: int = 0, part: int = 0) -> dict:
    keys = jax.random.split(jax.random.key(seed), 17)
    part_keys = jax.random.split(jax.random.fold_in(keys[16], part), 17)
    residual = gaussian(part_keys[0], (ROWS, MODEL_WIDTH), 1.0, 6.0, ((0, 4), (1, 4)))
    queries = draw_queries(jax.random.fold_in(jax.random.fold_in(keys[16], part), 71), part)
    token_keys = gaussian(part_keys[2], (ROWS, KVH * HD), 1.0, 5.0, ((0, 4), (1, 4)))
    token_values = gaussian(part_keys[3], (ROWS, KVH * HD), 1.0, 5.0, ((0, 4), (1, 4)))
    stored_keys = draw_stored_keys(jax.random.fold_in(jax.random.fold_in(keys[16], part), 71), part)
    stored_values = gaussian(part_keys[5], (ROWS, CACHE, KVH * HD), 1.0, 5.0, ((0, 4), (2, 4)))
    lengths = with_ends(jax.random.randint(part_keys[6], (ROWS,), 2, CACHE + 1), jax.random.fold_in(part_keys[6], 1), 2, CACHE).astype(jnp.int32)
    norm_gain_vector = jnp.clip(1.0 + 0.18 * jax.random.normal(keys[7], (MODEL_WIDTH,), jnp.float32), 0.1, 1.9)
    router = gaussian(keys[8], (MODEL_WIDTH, EXPERT_COUNT), MODEL_WIDTH ** -0.5, 0.109375, ((0, 4),))
    expert_gate_weight = gaussian(keys[9], (MODEL_WIDTH, EXPERT_COUNT * EXPERT_HIDDEN), MODEL_WIDTH ** -0.5, 0.109375, ((1, 16),))
    expert_up_weight = gaussian(keys[10], (MODEL_WIDTH, EXPERT_COUNT * EXPERT_HIDDEN), MODEL_WIDTH ** -0.5, 0.109375, ((1, 16),))
    expert_down_weight = gaussian(keys[11], (EXPERT_COUNT * EXPERT_HIDDEN, MODEL_WIDTH), EXPERT_HIDDEN ** -0.5, 0.0625, ((0, 16),))
    adapter_down_map = gaussian(keys[12], (MODEL_WIDTH, TENANT_COUNT * EXPERT_COUNT * ADAPTER_RANK), MODEL_WIDTH ** -0.5, 0.109375, ((0, 4),))
    adapter_up_map = gaussian(keys[13], (TENANT_COUNT * ADAPTER_RANK, EXPERT_COUNT * EXPERT_HIDDEN), (4 * ADAPTER_RANK) ** -0.5, 0.75, ((1, 16),))
    routes_keys = jax.random.split(jax.random.fold_in(part_keys[14], 1), ROWS // ROW_DEV)
    routes_turns = jax.random.permutation(jax.random.fold_in(part_keys[14], 3), ROWS // ROW_DEV)
    routes = jax.vmap(lambda own, number: routed_block(jax.random.fold_in(part_keys[14], 2), own, number, ROW_DEV, EXPERT_COUNT, 2, CAP, 2))(routes_keys, routes_turns).reshape((ROWS, 2))
    tenants = with_ends(jax.random.randint(part_keys[15], (ROWS,), 0, TENANT_COUNT), jax.random.fold_in(part_keys[15], 1), 0, TENANT_COUNT - 1).astype(jnp.int32)
    return {"residual": residual, "queries": queries, "token_keys": token_keys, "token_values": token_values, "stored_keys": stored_keys, "stored_values": stored_values, "lengths": lengths, "norm_gain_vector": norm_gain_vector, "router": router, "expert_gate_weight": expert_gate_weight, "expert_up_weight": expert_up_weight, "expert_down_weight": expert_down_weight, "adapter_down_map": adapter_down_map, "adapter_up_map": adapter_up_map, "routes": routes, "tenants": tenants}


def reference(residual, queries, token_keys, token_values, stored_keys, stored_values, lengths, norm_gain_vector, router, expert_gate_weight, expert_up_weight, expert_down_weight, adapter_down_map, adapter_up_map, routes, tenants):
    count_of_rows = residual.shape[0]
    group_heads = HEADS // KVH
    score_scale = HD ** (-0.5)
    query_heads = queries.astype(jnp.float32).reshape(count_of_rows, KVH, group_heads, HD)
    key_heads = stored_keys.astype(jnp.float32).reshape(count_of_rows, CACHE, KVH, HD)
    value_heads = stored_values.astype(jnp.float32).reshape(count_of_rows, CACHE, KVH, HD)
    fresh_keys = token_keys.astype(jnp.float32).reshape(count_of_rows, KVH, HD)
    fresh_values = token_values.astype(jnp.float32).reshape(count_of_rows, KVH, HD)
    cache_scores = jnp.einsum('rgjd,rpgd->rgjp', query_heads, key_heads) * score_scale
    fresh_scores = jnp.einsum('rgjd,rgd->rgj', query_heads, fresh_keys) * score_scale
    positions = lax.broadcasted_iota(jnp.int32, (count_of_rows, CACHE), 1)
    visible = positions < lengths[:, None]
    cache_scores = jnp.where(visible[:, None, None, :], cache_scores, -jnp.inf)
    largest = jnp.maximum(lax.optimization_barrier(jnp.max(cache_scores, axis=3)), fresh_scores)
    cache_exp = jnp.exp(cache_scores - largest[..., None])
    fresh_exp = jnp.exp(fresh_scores - largest)
    denominator = lax.optimization_barrier(jnp.sum(cache_exp, axis=3)) + fresh_exp
    cache_probs = (cache_exp / denominator[..., None]).astype(jnp.bfloat16)
    fresh_probs = (fresh_exp / denominator).astype(jnp.bfloat16)
    attended = jnp.einsum('rgjp,rpgd->rgjd', cache_probs.astype(jnp.float32), value_heads)
    attended = attended + fresh_probs.astype(jnp.float32)[..., None] * fresh_values[:, :, None, :]
    attended = attended.reshape(count_of_rows, HEADS * HD)
    state = (residual.astype(jnp.float32) + attended).astype(jnp.bfloat16)
    state_float = state.astype(jnp.float32)
    inverse_rms = lax.rsqrt(lax.optimization_barrier(jnp.mean(state_float * state_float, axis=1)) + 1e-05)
    normalized_input = (state_float * inverse_rms[:, None] * norm_gain_vector[None, :]).astype(jnp.bfloat16)
    logits = jnp.dot(normalized_input, router, preferred_element_type=jnp.float32)
    chosen = jnp.take_along_axis(logits, routes, axis=1)
    first_weight = jax.nn.sigmoid(chosen[:, 0] - chosen[:, 1])
    route_weights = jnp.stack([first_weight, 1.0 - first_weight], axis=1)
    adapter_total = jnp.dot(normalized_input, adapter_down_map, preferred_element_type=jnp.float32).reshape(count_of_rows, TENANT_COUNT, EXPERT_COUNT, ADAPTER_RANK)
    tenant_rows = jnp.take_along_axis(adapter_total, tenants[:, None, None, None], axis=1)[:, 0]
    lowrank = jnp.take_along_axis(tenant_rows, routes[:, :, None], axis=1).astype(jnp.bfloat16)
    tenant_mask = (tenants[:, None] == jnp.arange(TENANT_COUNT, dtype=jnp.int32)[None, :]).astype(jnp.bfloat16)
    mixture = jnp.zeros((count_of_rows, MODEL_WIDTH), jnp.float32)
    for expert in range(EXPERT_COUNT):
        chosen_here = routes == expert
        weight_here = lax.optimization_barrier(jnp.sum(jnp.where(chosen_here, route_weights, 0.0), axis=1))
        lowrank_here = lax.optimization_barrier(jnp.sum(jnp.where(chosen_here[:, :, None], lowrank.astype(jnp.float32), 0.0), axis=1)).astype(jnp.bfloat16)
        adapter_rows = (tenant_mask[:, :, None] * lowrank_here[:, None, :]).reshape(count_of_rows, TENANT_COUNT * ADAPTER_RANK)
        offset_begin = expert * EXPERT_HIDDEN
        gate_value = jnp.dot(normalized_input, expert_gate_weight[:, offset_begin:offset_begin + EXPERT_HIDDEN], preferred_element_type=jnp.float32)
        up_projected = jnp.dot(normalized_input, expert_up_weight[:, offset_begin:offset_begin + EXPERT_HIDDEN], preferred_element_type=jnp.float32)
        up_projected = up_projected + jnp.dot(adapter_rows, adapter_up_map[:, offset_begin:offset_begin + EXPERT_HIDDEN], preferred_element_type=jnp.float32)
        activated = (jax.nn.silu(gate_value) * up_projected).astype(jnp.bfloat16)
        expert_out = jnp.dot(activated, expert_down_weight[offset_begin:offset_begin + EXPERT_HIDDEN, :], preferred_element_type=jnp.float32)
        mixture = mixture + weight_here[:, None] * expert_out
    return (state_float + mixture).astype(jnp.bfloat16)
```

```python
import functools

import jax
import jax.numpy as jnp
from jax import lax
from jax.experimental import pallas as pl
from jax.experimental.pallas import tpu as pltpu
from jax.sharding import PartitionSpec as P

HEADS = 24
KVH = 8
HD = 128
EXPERT_COUNT = 4
ADAPTER_RANK = 16
TENANT_COUNT = 8
LANES = 128
ADAPTER_LANES = EXPERT_COUNT * ADAPTER_RANK
DIFF_HI, DIFF_LO, SQ_HI, SQ_LO, FIRST, SECOND, TENANT = range(ADAPTER_LANES, ADAPTER_LANES + 7)
F32 = jnp.float32
BF16 = jnp.bfloat16
ANY_LANES = (((1,), (1,)), ((), ()))


def column(values, rows):
    index = lax.broadcasted_iota(jnp.int32, (rows, LANES), 0)
    out = jnp.zeros((rows, LANES), jnp.int32)
    for r in range(rows):
        out = jnp.where(index == r, values(r), out)
    return out


def attend_kernel(
    lengths,
    tenants,
    routes,
    residual,
    queries,
    token_keys,
    token_values,
    stored_keys,
    stored_values,
    gain,
    router,
    adapter_down,
    state_out,
    payload_out,
):
    rows, features = residual.shape
    kv_local = token_keys.shape[1] // HD
    cache = stored_keys.shape[1]
    group = HEADS // KVH
    scale = HD ** (-0.5)
    length_column = column(lambda r: lengths[r], rows)
    stacked_length = jnp.concatenate([length_column[:, :1]] * group, axis=0)
    stacked_row = lax.rem(
        lax.broadcasted_iota(jnp.int32, (group * rows, max(cache, HD)), 0), jnp.int32(rows)
    )
    visible = lax.broadcasted_iota(jnp.int32, (group * rows, cache), 1) < stacked_length
    squares = jnp.zeros((rows, 1), F32)
    for g in range(kv_local):
        key_lanes = slice(g * HD, (g + 1) * HD)
        query = jnp.concatenate(
            [queries[:, (g * group + j) * HD : (g * group + j + 1) * HD] for j in range(group)],
            axis=0,
        )
        scores = jnp.zeros((group * rows, cache), F32)
        for r in range(rows):
            every = lax.dot_general(
                query, stored_keys[r, :, key_lanes], ANY_LANES, preferred_element_type=F32
            )
            scores = jnp.where(stacked_row[:, :cache] == r, every, scores)
        scores = jnp.where(visible, scores * scale, -jnp.inf)
        fresh_key = jnp.concatenate([token_keys[:, key_lanes].astype(F32)] * group, axis=0)
        fresh = jnp.sum(query.astype(F32) * fresh_key, axis=1, keepdims=True) * scale
        largest = jnp.maximum(jnp.max(scores, axis=1, keepdims=True), fresh)
        cache_exp = jnp.exp(scores - largest)
        fresh_exp = jnp.exp(fresh - largest)
        denominator = jnp.sum(cache_exp, axis=1, keepdims=True) + fresh_exp
        probs = (cache_exp / denominator).astype(BF16)
        fresh_prob = (fresh_exp / denominator).astype(BF16).astype(F32)
        attended = jnp.zeros((group * rows, HD), F32)
        for r in range(rows):
            every = jnp.dot(probs, stored_values[r, :, key_lanes], preferred_element_type=F32)
            attended = jnp.where(stacked_row[:, :HD] == r, every, attended)
        fresh_value = jnp.concatenate([token_values[:, key_lanes].astype(F32)] * group, axis=0)
        attended = attended + fresh_prob * fresh_value
        for j in range(group):
            lanes = slice((g * group + j) * HD, (g * group + j + 1) * HD)
            state = (
                residual[:, lanes].astype(F32) + attended[j * rows : (j + 1) * rows]
            ).astype(BF16)
            state_out[:, lanes] = state
            state = state.astype(F32)
            squares = squares + jnp.sum(state * state, axis=1, keepdims=True)
            payload_out[:, lanes] = (state * gain[:, lanes]).astype(BF16)
    scaled = payload_out[:, :features]
    logits = lax.dot_general(scaled, router[...], ANY_LANES, preferred_element_type=F32)
    first = column(lambda r: routes[0, r], rows)
    second = column(lambda r: routes[1, r], rows)
    tenant = column(lambda r: tenants[r], rows)
    expert = lax.broadcasted_iota(jnp.int32, logits.shape, 1)
    chosen = jnp.where(expert == first[:, :EXPERT_COUNT], logits, 0.0) - jnp.where(
        expert == second[:, :EXPERT_COUNT], logits, 0.0
    )
    diff = jnp.sum(chosen, axis=1, keepdims=True)
    adapter = jnp.dot(scaled, adapter_down[...], preferred_element_type=F32)
    lane = lax.broadcasted_iota(jnp.int32, (rows, LANES), 1)
    tail = jnp.zeros((rows, LANES), F32)
    for start in range(0, adapter.shape[1], LANES):
        owner = (lane + start) // ADAPTER_LANES
        tail = tail + jnp.where(owner == tenant, adapter[:, start : start + LANES], 0.0)
    tail = tail + pltpu.roll(tail, ADAPTER_LANES, 1)
    diff_hi = diff.astype(BF16).astype(F32)
    squares_hi = squares.astype(BF16).astype(F32)
    for place, value in (
        (DIFF_HI, diff_hi),
        (DIFF_LO, diff - diff_hi),
        (SQ_HI, squares_hi),
        (SQ_LO, squares - squares_hi),
        (FIRST, first.astype(F32)),
        (SECOND, second.astype(F32)),
        (TENANT, tenant.astype(F32)),
    ):
        tail = jnp.where(lane == place, value, tail)
    payload_out[:, features:] = tail.astype(BF16)


def attend(args):
    rows, features = args[3].shape
    smem = pl.BlockSpec(memory_space=pltpu.SMEM)
    vmem = pl.BlockSpec(memory_space=pltpu.VMEM)
    return pl.pallas_call(
        attend_kernel,
        out_shape=(
            jax.ShapeDtypeStruct((rows, features), BF16),
            jax.ShapeDtypeStruct((rows, features + LANES), BF16),
        ),
        in_specs=[smem] * 3 + [vmem] * 9,
        out_specs=(vmem, vmem),
        compiler_params=pltpu.CompilerParams(vmem_limit_bytes=12 * 2**20),
        cost_estimate=pl.CostEstimate(
            flops=200_000_000, bytes_accessed=3_000_000, transcendentals=20_000
        ),
        name="attend",
    )(*args)


def expert_kernel(
    order, replicas, gathered, gate_weight, up_weight, down_weight, adapter_up, kept, sent, active
):
    tensor_devices, rows, width = gathered.shape
    features = width - LANES
    hidden = gate_weight.shape[1]
    mine = lax.axis_index("tp")
    expert = lax.axis_index("ep") // replicas
    tail = jnp.zeros((rows, LANES), F32)
    for i in range(tensor_devices):
        tail = tail + gathered[i, :, features:].astype(F32)
    place = lambda k: tail[:, k : k + 1]
    here = gathered[0, :, features:].astype(F32)
    inverse_rms = lax.rsqrt(
        (place(SQ_HI) + place(SQ_LO)) / (features * tensor_devices) + 1e-05
    )
    diff = (place(DIFF_HI) + place(DIFF_LO)) * inverse_rms
    expert_float = expert.astype(F32)
    is_first = here[:, FIRST : FIRST + 1] == expert_float
    is_second = here[:, SECOND : SECOND + 1] == expert_float
    weight = jnp.where(
        is_first, jax.nn.sigmoid(diff), jnp.where(is_second, jax.nn.sigmoid(-diff), 0.0)
    )
    lowrank = (tail * inverse_rms).astype(BF16)
    spread_shape = (LANES, TENANT_COUNT * ADAPTER_RANK)
    source = lax.broadcasted_iota(jnp.int32, spread_shape, 0)
    target = lax.broadcasted_iota(jnp.int32, spread_shape, 1)
    spread = jnp.where(
        source == expert * ADAPTER_RANK + lax.rem(target, jnp.int32(ADAPTER_RANK)), 1.0, 0.0
    ).astype(BF16)
    lane = lax.broadcasted_iota(jnp.int32, (rows, TENANT_COUNT * ADAPTER_RANK), 1)
    own_tenant = (lane // ADAPTER_RANK).astype(F32) == here[:, TENANT : TENANT + 1]
    adapter_rows = jnp.where(
        own_tenant, jnp.dot(lowrank, spread, preferred_element_type=F32), 0.0
    ).astype(BF16)
    tile = min(256, hidden)

    def hidden_tile(n, carry):
        lanes = pl.ds(pl.multiple_of(n * tile, tile), tile)
        gate = jnp.zeros((rows, tile), F32)
        up = jnp.zeros((rows, tile), F32)
        for i in range(tensor_devices):
            start = pl.multiple_of((mine ^ order[i]) * features, features)
            scaled = gathered[i, :, :features]
            gate = gate + jnp.dot(
                scaled, gate_weight[pl.ds(start, features), lanes], preferred_element_type=F32
            )
            up = up + jnp.dot(
                scaled, up_weight[pl.ds(start, features), lanes], preferred_element_type=F32
            )
        gate = gate * inverse_rms
        up = up * inverse_rms + jnp.dot(
            adapter_rows, adapter_up[:, lanes], preferred_element_type=F32
        )
        active[:, lanes] = (gate * jax.nn.sigmoid(gate) * up * weight).astype(BF16)
        return carry

    lax.fori_loop(0, hidden // tile, hidden_tile, 0)
    out_tile = 256 if features % 256 == 0 else LANES
    for i in range(tensor_devices):
        start = (mine ^ i) * features

        def out_tiles(n, carry):
            lanes = pl.ds(pl.multiple_of(start + n * out_tile, LANES), out_tile)
            result = jnp.dot(active[...], down_weight[:, lanes], preferred_element_type=F32)
            to = pl.ds(pl.multiple_of(n * out_tile, out_tile), out_tile)
            if i % 2 == 0:
                kept[i // 2, :, to] = result
            else:
                sent[i // 2, :, to] = result.astype(BF16)
            return carry

        lax.fori_loop(0, features // out_tile, out_tiles, 0)


def experts(gathered, order, replicas, gate_weight, up_weight, down_weight, adapter_up):
    tensor_devices, rows, width = gathered.shape
    features = width - LANES
    vmem = pl.BlockSpec(memory_space=pltpu.VMEM)
    placed = [
        pltpu.with_memory_space_constraint(w, pltpu.VMEM)
        for w in (gate_weight, up_weight, down_weight)
    ]
    return pl.pallas_call(
        functools.partial(expert_kernel, order, replicas),
        out_shape=(
            jax.ShapeDtypeStruct((tensor_devices // 2, rows, features), F32),
            jax.ShapeDtypeStruct((tensor_devices // 2, rows, features), BF16),
        ),
        in_specs=[vmem] * 5,
        out_specs=(vmem, vmem),
        scratch_shapes=[pltpu.VMEM((rows, gate_weight.shape[1]), BF16)],
        compiler_params=pltpu.CompilerParams(vmem_limit_bytes=16 * 2**20),
        cost_estimate=pl.CostEstimate(
            flops=2 * rows * 3 * gate_weight.size, bytes_accessed=4_000_000, transcendentals=0
        ),
        name="experts",
    )(gathered, *placed, adapter_up)


def swap(x, axis, distance):
    count = lax.axis_size(axis)
    return lax.ppermute(x, axis, [(i, i ^ distance) for i in range(count)])


def bits(count):
    return [1 << b for b in range(count.bit_length() - 1)]


def per_device(
    residual,
    queries,
    token_keys,
    token_values,
    stored_keys,
    stored_values,
    lengths,
    norm_gain_vector,
    router,
    expert_gate_weight,
    expert_up_weight,
    expert_down_weight,
    adapter_down_map,
    adapter_up_map,
    routes,
    tenants,
):
    rows, features = residual.shape
    expert_devices = lax.axis_size("ep")
    tensor_devices = lax.axis_size("tp")
    state, held = attend(
        (
            lengths,
            tenants,
            routes.T,
            residual,
            queries,
            token_keys,
            token_values,
            stored_keys,
            stored_values,
            norm_gain_vector.reshape(1, features),
            router.T,
            adapter_down_map,
        )
    )
    for distance in bits(expert_devices):
        held = jnp.concatenate([held, swap(held, "ep", distance)], axis=0)
    gathered, order = held[None], [0]
    for distance in reversed(bits(tensor_devices)):
        gathered = jnp.concatenate([gathered, swap(gathered, "tp", distance)], axis=0)
        order = order + [at ^ distance for at in order]
    kept, sent = experts(
        gathered,
        tuple(order),
        expert_devices // EXPERT_COUNT,
        expert_gate_weight,
        expert_up_weight,
        expert_down_weight,
        adapter_up_map,
    )
    for distance in bits(tensor_devices):
        if distance > 1:
            kept, sent = kept[0::2], kept[1::2].astype(BF16)
        kept = kept + swap(sent, "tp", distance).astype(F32)
    kept = kept.reshape(expert_devices, rows, features)
    for distance in bits(expert_devices):
        kept, sent = kept[0::2], kept[1::2].astype(BF16)
        kept = kept + swap(sent, "ep", distance).astype(F32)
    return (state.astype(F32) + kept[0]).astype(BF16)


def solution(mesh):
    placed = (
        P(("groups", "ep"), "tp"),
        P(("groups", "ep"), "tp"),
        P(("groups", "ep"), "tp"),
        P(("groups", "ep"), "tp"),
        P(("groups", "ep"), None, "tp"),
        P(("groups", "ep"), None, "tp"),
        P(("groups", "ep")),
        P("tp"),
        P("tp", None),
        P(None, ("ep", "tp")),
        P(None, ("ep", "tp")),
        P(("ep", "tp"), None),
        P("tp", None),
        P(None, ("ep", "tp")),
        P(("groups", "ep"), None),
        P(("groups", "ep")),
    )
    return jax.shard_map(
        per_device, mesh=mesh, in_specs=placed, out_specs=P(("groups", "ep"), "tp"), check_vma=False
    )
```

```python
import functools

import jax
import jax.numpy as jnp
from jax import lax
from jax.experimental import pallas as pl
from jax.experimental.pallas import tpu as pltpu
from jax.sharding import PartitionSpec as P

HEADS = 24
KVH = 8
HD = 128
EXPERT_COUNT = 4
ADAPTER_RANK = 16
TENANT_COUNT = 8
LANES = 128
ADAPTER_LANES = EXPERT_COUNT * ADAPTER_RANK
DIFF_HI, DIFF_LO, SQ_HI, SQ_LO, FIRST, SECOND, TENANT = range(ADAPTER_LANES, ADAPTER_LANES + 7)
F32 = jnp.float32
BF16 = jnp.bfloat16
ANY_LANES = (((1,), (1,)), ((), ()))


def column(values, rows):
    index = lax.broadcasted_iota(jnp.int32, (rows, LANES), 0)
    out = jnp.zeros((rows, LANES), jnp.int32)
    for r in range(rows):
        out = jnp.where(index == r, values(r), out)
    return out


def attend_kernel(*refs):
    count = 12
    sources, outs, buffers, arrived = refs[:count], refs[count:-count - 1], refs[-count - 1:-1], refs[-1]
    copies = [
        pltpu.make_async_copy(source, buffer, arrived.at[i])
        for i, (source, buffer) in enumerate(zip(sources, buffers, strict=True))
    ]
    for i in (7, 4, 0, 5, 8, 6, 3, 9, 1, 2, 10, 11):
        copies[i].start()
    attend_body(*buffers, *outs, wait=lambda *which: [copies[i].wait() for i in which])


def attend_body(
    lengths,
    tenants,
    routes,
    residual,
    queries,
    token_keys,
    token_values,
    stored_keys,
    stored_values,
    gain,
    router,
    adapter_down,
    state_out,
    payload_out,
    *,
    wait,
):
    rows, features = residual.shape
    kv_local = token_keys.shape[1] // HD
    cache = stored_keys.shape[1]
    group = HEADS // KVH
    scale = HD ** (-0.5)
    wait(0, 4, 7)
    length_column = column(lambda r: lengths[r], rows)
    stacked_length = jnp.concatenate([length_column[:, :1]] * group, axis=0)
    stacked_row = lax.rem(
        lax.broadcasted_iota(jnp.int32, (group * rows, max(cache, HD)), 0), jnp.int32(rows)
    )
    visible = lax.broadcasted_iota(jnp.int32, (group * rows, cache), 1) < stacked_length
    squares = jnp.zeros((rows, 1), F32)
    for g in range(kv_local):
        key_lanes = slice(g * HD, (g + 1) * HD)
        query = jnp.concatenate(
            [queries[:, (g * group + j) * HD : (g * group + j + 1) * HD] for j in range(group)],
            axis=0,
        )
        scores = jnp.zeros((group * rows, cache), F32)
        for r in range(rows):
            every = lax.dot_general(
                query, stored_keys[r, :, key_lanes], ANY_LANES, preferred_element_type=F32
            )
            scores = jnp.where(stacked_row[:, :cache] == r, every, scores)
        scores = jnp.where(visible, scores * scale, -jnp.inf)
        if g == 0:
            wait(5)
        fresh_key = jnp.concatenate([token_keys[:, key_lanes].astype(F32)] * group, axis=0)
        fresh = jnp.sum(query.astype(F32) * fresh_key, axis=1, keepdims=True) * scale
        largest = jnp.maximum(jnp.max(scores, axis=1, keepdims=True), fresh)
        cache_exp = jnp.exp(scores - largest)
        fresh_exp = jnp.exp(fresh - largest)
        denominator = jnp.sum(cache_exp, axis=1, keepdims=True) + fresh_exp
        probs = (cache_exp / denominator).astype(BF16)
        fresh_prob = (fresh_exp / denominator).astype(BF16).astype(F32)
        if g == 0:
            wait(8)
        attended = jnp.zeros((group * rows, HD), F32)
        for r in range(rows):
            every = jnp.dot(probs, stored_values[r, :, key_lanes], preferred_element_type=F32)
            attended = jnp.where(stacked_row[:, :HD] == r, every, attended)
        if g == 0:
            wait(3, 6, 9)
        fresh_value = jnp.concatenate([token_values[:, key_lanes].astype(F32)] * group, axis=0)
        attended = attended + fresh_prob * fresh_value
        for j in range(group):
            lanes = slice((g * group + j) * HD, (g * group + j + 1) * HD)
            state = (
                residual[:, lanes].astype(F32) + attended[j * rows : (j + 1) * rows]
            ).astype(BF16)
            state_out[:, lanes] = state
            state = state.astype(F32)
            squares = squares + jnp.sum(state * state, axis=1, keepdims=True)
            payload_out[:, lanes] = (
                state * gain[lanes.start // LANES : lanes.start // LANES + 1, :]
            ).astype(BF16)
    wait(1, 2, 10, 11)
    scaled = payload_out[:, :features]
    logits = lax.dot_general(scaled, router[...], ANY_LANES, preferred_element_type=F32)
    first = column(lambda r: routes[0, r], rows)
    second = column(lambda r: routes[1, r], rows)
    tenant = column(lambda r: tenants[r], rows)
    expert = lax.broadcasted_iota(jnp.int32, logits.shape, 1)
    chosen = jnp.where(expert == first[:, :EXPERT_COUNT], logits, 0.0) - jnp.where(
        expert == second[:, :EXPERT_COUNT], logits, 0.0
    )
    diff = jnp.sum(chosen, axis=1, keepdims=True)
    adapter = jnp.dot(scaled, adapter_down[...], preferred_element_type=F32)
    lane = lax.broadcasted_iota(jnp.int32, (rows, LANES), 1)
    tail = jnp.zeros((rows, LANES), F32)
    for start in range(0, adapter.shape[1], LANES):
        owner = (lane + start) // ADAPTER_LANES
        tail = tail + jnp.where(owner == tenant, adapter[:, start : start + LANES], 0.0)
    tail = tail + pltpu.roll(tail, ADAPTER_LANES, 1)
    diff_hi = diff.astype(BF16).astype(F32)
    squares_hi = squares.astype(BF16).astype(F32)
    for place, value in (
        (DIFF_HI, diff_hi),
        (DIFF_LO, diff - diff_hi),
        (SQ_HI, squares_hi),
        (SQ_LO, squares - squares_hi),
        (FIRST, first.astype(F32)),
        (SECOND, second.astype(F32)),
        (TENANT, tenant.astype(F32)),
    ):
        tail = jnp.where(lane == place, value, tail)
    payload_out[:, features:] = tail.astype(BF16)


def attend(args):
    rows, features = args[3].shape
    vmem = pl.BlockSpec(memory_space=pltpu.VMEM)
    return pl.pallas_call(
        attend_kernel,
        out_shape=(
            jax.ShapeDtypeStruct((rows, features), BF16),
            jax.ShapeDtypeStruct((rows, features + LANES), BF16),
        ),
        in_specs=[pl.BlockSpec(memory_space=pl.ANY)] * len(args),
        out_specs=(vmem, vmem),
        scratch_shapes=[
            (pltpu.SMEM if i < 3 else pltpu.VMEM)(arg.shape, arg.dtype)
            for i, arg in enumerate(args)
        ]
        + [pltpu.SemaphoreType.DMA((len(args),))],
        compiler_params=pltpu.CompilerParams(vmem_limit_bytes=12 * 2**20),
        cost_estimate=pl.CostEstimate(
            flops=200_000_000, bytes_accessed=3_000_000, transcendentals=20_000
        ),
        name="attend",
    )(*[pltpu.with_memory_space_constraint(arg, pltpu.HBM) for arg in args])


def expert_kernel(
    order,
    replicas,
    gathered,
    gate_weight,
    up_weight,
    down_weight,
    adapter_weight,
    kept,
    sent,
    gate_part,
    up_part,
    down_part,
    adapter_up,
    gate_sum,
    up_sum,
    active,
    arrived,
):
    tensor_devices, rows, width = gathered.shape
    features = width - LANES
    mine = lax.axis_index("tp")
    expert = lax.axis_index("ep") // replicas
    copies = []
    for i in range(tensor_devices):
        depth = pl.ds(pl.multiple_of((mine ^ order[i]) * features, features), features)
        copies.append((gate_weight.at[depth, :], gate_part.at[i]))
        copies.append((up_weight.at[depth, :], up_part.at[i]))
    targets = [i for i in range(tensor_devices) if i % 2] + list(range(0, tensor_devices, 2))
    for i in targets:
        lanes = pl.ds(pl.multiple_of((mine ^ i) * features, features), features)
        copies.append((down_weight.at[:, lanes], down_part.at[i]))
    copies = [
        pltpu.make_async_copy(source, part, arrived.at[i])
        for i, (source, part) in enumerate(copies)
    ]
    adapter_copy = pltpu.make_async_copy(adapter_weight, adapter_up, arrived.at[len(copies)])
    ahead = 4
    for copy in copies[:ahead]:
        copy.start()
    adapter_copy.start()

    def wait(i):
        copies[i].wait()
        if i + ahead < len(copies):
            copies[i + ahead].start()

    tail = jnp.zeros((rows, LANES), F32)
    for i in range(tensor_devices):
        tail = tail + gathered[i, :, features:].astype(F32)
    place = lambda k: tail[:, k : k + 1]
    here = gathered[0, :, features:].astype(F32)
    inverse_rms = lax.rsqrt(
        (place(SQ_HI) + place(SQ_LO)) / (features * tensor_devices) + 1e-05
    )
    diff = (place(DIFF_HI) + place(DIFF_LO)) * inverse_rms
    expert_float = expert.astype(F32)
    is_first = here[:, FIRST : FIRST + 1] == expert_float
    is_second = here[:, SECOND : SECOND + 1] == expert_float
    weight = jnp.where(
        is_first, jax.nn.sigmoid(diff), jnp.where(is_second, jax.nn.sigmoid(-diff), 0.0)
    )
    lowrank = (tail * inverse_rms).astype(BF16)
    spread_shape = (LANES, TENANT_COUNT * ADAPTER_RANK)
    source = lax.broadcasted_iota(jnp.int32, spread_shape, 0)
    target = lax.broadcasted_iota(jnp.int32, spread_shape, 1)
    spread = jnp.where(
        source == expert * ADAPTER_RANK + lax.rem(target, jnp.int32(ADAPTER_RANK)), 1.0, 0.0
    ).astype(BF16)
    lane = lax.broadcasted_iota(jnp.int32, (rows, TENANT_COUNT * ADAPTER_RANK), 1)
    own_tenant = (lane // ADAPTER_RANK).astype(F32) == here[:, TENANT : TENANT + 1]
    adapter_rows = jnp.where(
        own_tenant, jnp.dot(lowrank, spread, preferred_element_type=F32), 0.0
    ).astype(BF16)
    for i in range(tensor_devices):
        scaled = gathered[i, :, :features]
        for weight_part, total, which in ((gate_part, gate_sum, 0), (up_part, up_sum, 1)):
            wait(2 * i + which)
            product = jnp.dot(scaled, weight_part[i], preferred_element_type=F32)
            total[...] = product if i == 0 else total[...] + product
    adapter_copy.wait()
    gate = gate_sum[...] * inverse_rms
    up = up_sum[...] * inverse_rms + jnp.dot(
        adapter_rows, adapter_up[...], preferred_element_type=F32
    )
    active[...] = (gate * jax.nn.sigmoid(gate) * up * weight).astype(BF16)
    for place_of, i in enumerate(targets):
        wait(2 * tensor_devices + place_of)
        result = jnp.dot(active[...], down_part[i], preferred_element_type=F32)
        if i % 2 == 0:
            kept[i // 2] = result
        else:
            sent[i // 2] = result.astype(BF16)


def experts(gathered, order, replicas, gate_weight, up_weight, down_weight, adapter_up):
    tensor_devices, rows, width = gathered.shape
    features = width - LANES
    hidden = gate_weight.shape[1]
    vmem = pl.BlockSpec(memory_space=pltpu.VMEM)
    hbm = pl.BlockSpec(memory_space=pl.ANY)
    return pl.pallas_call(
        functools.partial(expert_kernel, order, replicas),
        out_shape=(
            jax.ShapeDtypeStruct((tensor_devices // 2, rows, features), F32),
            jax.ShapeDtypeStruct((tensor_devices // 2, rows, features), BF16),
        ),
        in_specs=[vmem, hbm, hbm, hbm, hbm],
        out_specs=(vmem, vmem),
        scratch_shapes=[
            pltpu.VMEM((tensor_devices, features, hidden), BF16),
            pltpu.VMEM((tensor_devices, features, hidden), BF16),
            pltpu.VMEM((tensor_devices, hidden, features), BF16),
            pltpu.VMEM(adapter_up.shape, BF16),
            pltpu.VMEM((rows, hidden), F32),
            pltpu.VMEM((rows, hidden), F32),
            pltpu.VMEM((rows, hidden), BF16),
            pltpu.SemaphoreType.DMA((3 * tensor_devices + 1,)),
        ],
        compiler_params=pltpu.CompilerParams(vmem_limit_bytes=48 * 2**20),
        cost_estimate=pl.CostEstimate(
            flops=2 * rows * 3 * gate_weight.size,
            bytes_accessed=6 * gate_weight.size,
            transcendentals=0,
        ),
        name="experts",
    )(
        gathered,
        *[
            pltpu.with_memory_space_constraint(weight, pltpu.HBM)
            for weight in (gate_weight, up_weight, down_weight, adapter_up)
        ],
    )


def swap(x, axis, distance):
    count = lax.axis_size(axis)
    return lax.ppermute(x, axis, [(i, i ^ distance) for i in range(count)])


def bits(count):
    return [1 << b for b in range(count.bit_length() - 1)]


def per_device(
    residual,
    queries,
    token_keys,
    token_values,
    stored_keys,
    stored_values,
    lengths,
    norm_gain_vector,
    router,
    expert_gate_weight,
    expert_up_weight,
    expert_down_weight,
    adapter_down_map,
    adapter_up_map,
    routes,
    tenants,
):
    rows, features = residual.shape
    expert_devices = lax.axis_size("ep")
    tensor_devices = lax.axis_size("tp")
    state, held = attend(
        (
            lengths,
            tenants,
            routes.T,
            residual,
            queries,
            token_keys,
            token_values,
            stored_keys,
            stored_values,
            norm_gain_vector.reshape(features // LANES, LANES),
            router.T,
            adapter_down_map,
        )
    )
    for distance in bits(expert_devices):
        held = jnp.concatenate([held, swap(held, "ep", distance)], axis=0)
    gathered, order = held[None], [0]
    for distance in reversed(bits(tensor_devices)):
        gathered = jnp.concatenate([gathered, swap(gathered, "tp", distance)], axis=0)
        order = order + [at ^ distance for at in order]
    kept, sent = experts(
        gathered,
        tuple(order),
        expert_devices // EXPERT_COUNT,
        expert_gate_weight,
        expert_up_weight,
        expert_down_weight,
        adapter_up_map,
    )
    for distance in bits(tensor_devices):
        if distance > 1:
            kept, sent = kept[0::2], kept[1::2].astype(BF16)
        kept = kept + swap(sent, "tp", distance).astype(F32)
    kept = kept.reshape(expert_devices, rows, features)
    for distance in bits(expert_devices):
        kept, sent = kept[0::2], kept[1::2].astype(BF16)
        kept = kept + swap(sent, "ep", distance).astype(F32)
    return (state.astype(F32) + kept[0]).astype(BF16)


def solution(mesh):
    placed = (
        P(("groups", "ep"), "tp"),
        P(("groups", "ep"), "tp"),
        P(("groups", "ep"), "tp"),
        P(("groups", "ep"), "tp"),
        P(("groups", "ep"), None, "tp"),
        P(("groups", "ep"), None, "tp"),
        P(("groups", "ep")),
        P("tp"),
        P("tp", None),
        P(None, ("ep", "tp")),
        P(None, ("ep", "tp")),
        P(("ep", "tp"), None),
        P("tp", None),
        P(None, ("ep", "tp")),
        P(("groups", "ep"), None),
        P(("groups", "ep")),
    )
    return jax.shard_map(
        per_device, mesh=mesh, in_specs=placed, out_specs=P(("groups", "ep"), "tp"), check_vma=False
    )
```

```python
import functools

import jax
import jax.numpy as jnp
from jax import lax
from jax.experimental import pallas as pl
from jax.experimental.pallas import tpu as pltpu
from jax.sharding import PartitionSpec as P

HEADS = 24
KVH = 8
HD = 128
EXPERT_COUNT = 4
ADAPTER_RANK = 16
TENANT_COUNT = 8
LANES = 128
ADAPTER_LANES = EXPERT_COUNT * ADAPTER_RANK
DIFF_HI, DIFF_LO, SQ_HI, SQ_LO, FIRST, SECOND, TENANT = range(ADAPTER_LANES, ADAPTER_LANES + 7)
F32 = jnp.float32
BF16 = jnp.bfloat16
ANY_LANES = (((1,), (1,)), ((), ()))


VMEM = pl.BlockSpec(memory_space=pltpu.VMEM)
HBM = pl.BlockSpec(memory_space=pl.ANY)


def in_hbm(*arrays):
    return [pltpu.with_memory_space_constraint(array, pltpu.HBM) for array in arrays]


def column(values, rows):
    index = lax.broadcasted_iota(jnp.int32, (rows, LANES), 0)
    out = jnp.zeros((rows, LANES), jnp.int32)
    for r in range(rows):
        out = jnp.where(index == r, values(r), out)
    return out


def fetch(gate_weight, up_weight, distance, part, arrived):
    features = part.shape[1]
    start = pl.multiple_of((lax.axis_index("tp") ^ distance) * features, features)
    copies = [
        pltpu.make_async_copy(weight.at[pl.ds(start, features), :], part.at[i], arrived.at[i])
        for i, weight in enumerate((gate_weight, up_weight))
    ]
    for copy in copies:
        copy.start()
    return copies


def attend_kernel(*refs):
    count = 12
    sources, weights = refs[:count], refs[count : count + 2]
    outs, own_weights = refs[count + 2 : count + 4], refs[count + 4]
    buffers, arrived, weights_arrived = refs[count + 5 : -2], refs[-2], refs[-1]
    copies = [
        pltpu.make_async_copy(source, buffer, arrived.at[i])
        for i, (source, buffer) in enumerate(zip(sources, buffers, strict=True))
    ]
    for i in (7, 4, 0, 5, 8, 6, 3, 9, 1, 2, 10, 11):
        copies[i].start()
    fetched = fetch(*weights, 0, own_weights, weights_arrived)
    attend_body(*buffers, *outs, wait=lambda *which: [copies[i].wait() for i in which])
    for copy in fetched:
        copy.wait()


def attend_body(
    lengths,
    tenants,
    routes,
    residual,
    queries,
    token_keys,
    token_values,
    stored_keys,
    stored_values,
    gain,
    router,
    adapter_down,
    state_out,
    payload_out,
    *,
    wait,
):
    rows, features = residual.shape
    kv_local = token_keys.shape[1] // HD
    cache = stored_keys.shape[1]
    group = HEADS // KVH
    scale = HD ** (-0.5)
    wait(0, 4, 7)
    length_column = column(lambda r: lengths[r], rows)
    stacked_length = jnp.concatenate([length_column[:, :1]] * group, axis=0)
    stacked_row = lax.rem(
        lax.broadcasted_iota(jnp.int32, (group * rows, max(cache, HD)), 0), jnp.int32(rows)
    )
    visible = lax.broadcasted_iota(jnp.int32, (group * rows, cache), 1) < stacked_length
    squares = jnp.zeros((rows, 1), F32)
    for g in range(kv_local):
        key_lanes = slice(g * HD, (g + 1) * HD)
        query = jnp.concatenate(
            [queries[:, (g * group + j) * HD : (g * group + j + 1) * HD] for j in range(group)],
            axis=0,
        )
        scores = jnp.zeros((group * rows, cache), F32)
        for r in range(rows):
            every = lax.dot_general(
                query, stored_keys[r, :, key_lanes], ANY_LANES, preferred_element_type=F32
            )
            scores = jnp.where(stacked_row[:, :cache] == r, every, scores)
        scores = jnp.where(visible, scores * scale, -jnp.inf)
        if g == 0:
            wait(5)
        fresh_key = jnp.concatenate([token_keys[:, key_lanes].astype(F32)] * group, axis=0)
        fresh = jnp.sum(query.astype(F32) * fresh_key, axis=1, keepdims=True) * scale
        largest = jnp.maximum(jnp.max(scores, axis=1, keepdims=True), fresh)
        cache_exp = jnp.exp(scores - largest)
        fresh_exp = jnp.exp(fresh - largest)
        denominator = jnp.sum(cache_exp, axis=1, keepdims=True) + fresh_exp
        probs = (cache_exp / denominator).astype(BF16)
        fresh_prob = (fresh_exp / denominator).astype(BF16).astype(F32)
        if g == 0:
            wait(8)
        attended = jnp.zeros((group * rows, HD), F32)
        for r in range(rows):
            every = jnp.dot(probs, stored_values[r, :, key_lanes], preferred_element_type=F32)
            attended = jnp.where(stacked_row[:, :HD] == r, every, attended)
        if g == 0:
            wait(3, 6, 9)
        fresh_value = jnp.concatenate([token_values[:, key_lanes].astype(F32)] * group, axis=0)
        attended = attended + fresh_prob * fresh_value
        for j in range(group):
            lanes = slice((g * group + j) * HD, (g * group + j + 1) * HD)
            state = (
                residual[:, lanes].astype(F32) + attended[j * rows : (j + 1) * rows]
            ).astype(BF16)
            state_out[:, lanes] = state
            state = state.astype(F32)
            squares = squares + jnp.sum(state * state, axis=1, keepdims=True)
            payload_out[:, lanes] = (
                state * gain[lanes.start // LANES : lanes.start // LANES + 1, :]
            ).astype(BF16)
    wait(1, 2, 10, 11)
    scaled = payload_out[:, :features]
    logits = lax.dot_general(scaled, router[...], ANY_LANES, preferred_element_type=F32)
    first = column(lambda r: routes[0, r], rows)
    second = column(lambda r: routes[1, r], rows)
    tenant = column(lambda r: tenants[r], rows)
    expert = lax.broadcasted_iota(jnp.int32, logits.shape, 1)
    chosen = jnp.where(expert == first[:, :EXPERT_COUNT], logits, 0.0) - jnp.where(
        expert == second[:, :EXPERT_COUNT], logits, 0.0
    )
    diff = jnp.sum(chosen, axis=1, keepdims=True)
    adapter = jnp.dot(scaled, adapter_down[...], preferred_element_type=F32)
    lane = lax.broadcasted_iota(jnp.int32, (rows, LANES), 1)
    tail = jnp.zeros((rows, LANES), F32)
    for start in range(0, adapter.shape[1], LANES):
        owner = (lane + start) // ADAPTER_LANES
        tail = tail + jnp.where(owner == tenant, adapter[:, start : start + LANES], 0.0)
    tail = tail + pltpu.roll(tail, ADAPTER_LANES, 1)
    diff_hi = diff.astype(BF16).astype(F32)
    squares_hi = squares.astype(BF16).astype(F32)
    for place, value in (
        (DIFF_HI, diff_hi),
        (DIFF_LO, diff - diff_hi),
        (SQ_HI, squares_hi),
        (SQ_LO, squares - squares_hi),
        (FIRST, first.astype(F32)),
        (SECOND, second.astype(F32)),
        (TENANT, tenant.astype(F32)),
    ):
        tail = jnp.where(lane == place, value, tail)
    payload_out[:, features:] = tail.astype(BF16)


def attend(args, gate_weight, up_weight):
    rows, features = args[3].shape
    return pl.pallas_call(
        attend_kernel,
        out_shape=(
            jax.ShapeDtypeStruct((rows, features), BF16),
            jax.ShapeDtypeStruct((rows, features + LANES), BF16),
            jax.ShapeDtypeStruct((2, features, gate_weight.shape[1]), BF16),
        ),
        in_specs=[HBM] * (len(args) + 2),
        out_specs=(VMEM, VMEM, VMEM),
        scratch_shapes=[
            (pltpu.SMEM if i < 3 else pltpu.VMEM)(arg.shape, arg.dtype)
            for i, arg in enumerate(args)
        ]
        + [pltpu.SemaphoreType.DMA((len(args),)), pltpu.SemaphoreType.DMA((2,))],
        compiler_params=pltpu.CompilerParams(vmem_limit_bytes=12 * 2**20),
        cost_estimate=pl.CostEstimate(
            flops=200_000_000, bytes_accessed=10_000_000, transcendentals=20_000
        ),
        name="attend",
    )(*in_hbm(*args, gate_weight, up_weight))


def load_kernel(distance, gate_weight, up_weight, after, part, arrived):
    for copy in fetch(gate_weight, up_weight, distance, part, arrived):
        copy.wait()


def load(gate_weight, up_weight, distance, features, after):
    shape = (2, features, gate_weight.shape[1])
    return pl.pallas_call(
        functools.partial(load_kernel, distance),
        out_shape=jax.ShapeDtypeStruct(shape, BF16),
        in_specs=[HBM] * 3,
        out_specs=VMEM,
        scratch_shapes=[pltpu.SemaphoreType.DMA((2,))],
        compiler_params=pltpu.CompilerParams(vmem_limit_bytes=2**20),
        cost_estimate=pl.CostEstimate(
            flops=0, bytes_accessed=4 * features * gate_weight.shape[1], transcendentals=0
        ),
        name="load",
    )(*in_hbm(gate_weight, up_weight), after)


def partial_kernel(distance, block, part, *refs):
    features = part.shape[1]
    fetched = []
    if distance is not None:
        gate_weight, up_weight, *refs = refs
        *refs, next_part, arrived = refs
        fetched = fetch(gate_weight, up_weight, distance, next_part, arrived)
    sums, totals = refs[:-1], refs[-1]
    scaled = block[:, :features]
    for i in range(2):
        product = jnp.dot(scaled, part[i], preferred_element_type=F32)
        totals[i] = sums[0][i] + product if sums else product
    for copy in fetched:
        copy.wait()


def partial(block, part, sums, gate_weight, up_weight, distance):
    rows, width = block.shape
    features = width - LANES
    hidden = part.shape[2]
    fetching = distance is not None
    totals = jax.ShapeDtypeStruct((2, rows, hidden), F32)
    given = (block, part) + (tuple(in_hbm(gate_weight, up_weight)) if fetching else ())
    given = given + ((sums,) if sums is not None else ())
    return pl.pallas_call(
        functools.partial(partial_kernel, distance),
        out_shape=(totals, jax.ShapeDtypeStruct(part.shape, BF16)) if fetching else (totals,),
        in_specs=[VMEM, VMEM] + [HBM] * (2 * fetching) + [VMEM] * (sums is not None),
        out_specs=(VMEM,) * (1 + fetching),
        scratch_shapes=[pltpu.SemaphoreType.DMA((2,))] * fetching,
        compiler_params=pltpu.CompilerParams(vmem_limit_bytes=8 * 2**20),
        cost_estimate=pl.CostEstimate(
            flops=4 * rows * features * hidden,
            bytes_accessed=4 * features * hidden,
            transcendentals=0,
        ),
        name="partial",
    )(*given)


def expert_kernel(replicas, targets, known, count, sums, *refs):
    tensor_devices = known + count
    blocks, parts = refs[:tensor_devices], refs[tensor_devices : tensor_devices + count]
    down_weight, adapter_weight, out, active, down_part, adapter_up, arrived = refs[
        tensor_devices + count :
    ]
    rows, width = blocks[0].shape
    features = width - LANES
    copies = [pltpu.make_async_copy(adapter_weight, adapter_up, arrived.at[len(targets)])]
    copies += down_copies(down_weight, targets, down_part, arrived)
    for copy in copies:
        copy.start()
    expert = lax.axis_index("ep") // replicas
    tail = jnp.zeros((rows, LANES), F32)
    for block in blocks:
        tail = tail + block[:, features:].astype(F32)
    place = lambda k: tail[:, k : k + 1]
    here = blocks[0][:, features:].astype(F32)
    inverse_rms = lax.rsqrt(
        (place(SQ_HI) + place(SQ_LO)) / (features * tensor_devices) + 1e-05
    )
    diff = (place(DIFF_HI) + place(DIFF_LO)) * inverse_rms
    expert_float = expert.astype(F32)
    is_first = here[:, FIRST : FIRST + 1] == expert_float
    is_second = here[:, SECOND : SECOND + 1] == expert_float
    weight = jnp.where(
        is_first, jax.nn.sigmoid(diff), jnp.where(is_second, jax.nn.sigmoid(-diff), 0.0)
    )
    lowrank = (tail * inverse_rms).astype(BF16)
    spread_shape = (LANES, TENANT_COUNT * ADAPTER_RANK)
    source = lax.broadcasted_iota(jnp.int32, spread_shape, 0)
    target = lax.broadcasted_iota(jnp.int32, spread_shape, 1)
    spread = jnp.where(
        source == expert * ADAPTER_RANK + lax.rem(target, jnp.int32(ADAPTER_RANK)), 1.0, 0.0
    ).astype(BF16)
    lane = lax.broadcasted_iota(jnp.int32, (rows, TENANT_COUNT * ADAPTER_RANK), 1)
    own_tenant = (lane // ADAPTER_RANK).astype(F32) == here[:, TENANT : TENANT + 1]
    adapter_rows = jnp.where(
        own_tenant, jnp.dot(lowrank, spread, preferred_element_type=F32), 0.0
    ).astype(BF16)
    copies[0].wait()
    hidden = active.shape[1]
    tile = min(512, hidden)
    for start in range(0, hidden, tile):
        lanes = slice(start, start + tile)
        gate, up = sums[0, :, lanes], sums[1, :, lanes]
        for block, part in zip(blocks[known:], parts, strict=True):
            scaled = block[:, :features]
            gate = gate + jnp.dot(scaled, part[0, :, lanes], preferred_element_type=F32)
            up = up + jnp.dot(scaled, part[1, :, lanes], preferred_element_type=F32)
        gate = gate * inverse_rms
        up = up * inverse_rms + jnp.dot(
            adapter_rows, adapter_up[:, lanes], preferred_element_type=F32
        )
        active[:, lanes] = (gate * jax.nn.sigmoid(gate) * up * weight).astype(BF16)
    down_products(active, copies[1:], down_part, out)


def down_copies(down_weight, targets, down_part, arrived):
    features = down_part.shape[2]
    return [
        pltpu.make_async_copy(
            down_weight.at[
                :, pl.ds(pl.multiple_of((lax.axis_index("tp") ^ k) * features, features), features)
            ],
            down_part.at[i],
            arrived.at[i],
        )
        for i, k in enumerate(targets)
    ]


def down_products(active, copies, down_part, out):
    for i, copy in enumerate(copies):
        copy.wait()
        out[i] = jnp.dot(active[...], down_part[i], preferred_element_type=F32).astype(out.dtype)


def experts(replicas, targets, sums, known, blocks, parts, down_weight, adapter_up):
    rows, width = blocks[0].shape
    features, hidden = width - LANES, sums.shape[2]
    return pl.pallas_call(
        functools.partial(expert_kernel, replicas, targets, known, len(parts)),
        out_shape=(
            jax.ShapeDtypeStruct((len(targets), rows, features), BF16),
            jax.ShapeDtypeStruct((rows, hidden), BF16),
        ),
        in_specs=[VMEM] * (1 + len(blocks) + len(parts)) + [HBM] * 2,
        out_specs=(VMEM, VMEM),
        scratch_shapes=[
            pltpu.VMEM((len(targets), hidden, features), BF16),
            pltpu.VMEM(adapter_up.shape, BF16),
            pltpu.SemaphoreType.DMA((len(targets) + 1,)),
        ],
        compiler_params=pltpu.CompilerParams(vmem_limit_bytes=16 * 2**20),
        cost_estimate=pl.CostEstimate(
            flops=2 * rows * hidden * features * (2 * len(parts) + len(targets)),
            bytes_accessed=2 * len(targets) * hidden * features,
            transcendentals=0,
        ),
        name="experts",
    )(sums, *blocks, *parts, *in_hbm(down_weight, adapter_up))


def down_kernel(targets, active, down_weight, after, out, down_part, arrived):
    copies = down_copies(down_weight, targets, down_part, arrived)
    for copy in copies:
        copy.start()
    down_products(active, copies, down_part, out)


def down(targets, active, down_weight, features, after):
    rows, hidden = active.shape
    return pl.pallas_call(
        functools.partial(down_kernel, targets),
        out_shape=jax.ShapeDtypeStruct((len(targets), rows, features), F32),
        in_specs=[VMEM, HBM, HBM],
        out_specs=VMEM,
        scratch_shapes=[
            pltpu.VMEM((len(targets), hidden, features), BF16),
            pltpu.SemaphoreType.DMA((len(targets),)),
        ],
        compiler_params=pltpu.CompilerParams(vmem_limit_bytes=16 * 2**20),
        cost_estimate=pl.CostEstimate(
            flops=2 * rows * hidden * features * len(targets),
            bytes_accessed=2 * len(targets) * hidden * features,
            transcendentals=0,
        ),
        name="down",
    )(active, *in_hbm(down_weight), after)


def join_kernel(first, second, after, out):
    count = first.shape[0]
    out[:count] = first[...]
    out[count:] = second[...]


def join(first, second, after):
    return pl.pallas_call(
        join_kernel,
        out_shape=jax.ShapeDtypeStruct((2 * first.shape[0], *first.shape[1:]), first.dtype),
        in_specs=[VMEM, VMEM, HBM],
        out_specs=VMEM,
        compiler_params=pltpu.CompilerParams(vmem_limit_bytes=4 * 2**20),
        name="join",
    )(first, second, after)


def tie_kernel(array, after, out):
    pass


def tie(array, after):
    return pl.pallas_call(
        tie_kernel,
        out_shape=jax.ShapeDtypeStruct(array.shape, array.dtype),
        in_specs=[HBM, HBM],
        out_specs=HBM,
        input_output_aliases={0: 0},
        compiler_params=pltpu.CompilerParams(vmem_limit_bytes=2**20),
        name="tie",
    )(array, after)


def swap(x, axis, distance):
    count = lax.axis_size(axis)
    return lax.ppermute(x, axis, [(i, i ^ distance) for i in range(count)])


def bits(count):
    return [1 << b for b in range(count.bit_length() - 1)]


def per_device(
    residual,
    queries,
    token_keys,
    token_values,
    stored_keys,
    stored_values,
    lengths,
    norm_gain_vector,
    router,
    expert_gate_weight,
    expert_up_weight,
    expert_down_weight,
    adapter_down_map,
    adapter_up_map,
    routes,
    tenants,
):
    rows, features = residual.shape
    expert_devices = lax.axis_size("ep")
    tensor_devices = lax.axis_size("tp")
    weights = (expert_gate_weight, expert_up_weight)
    state, held, part = attend(
        (
            lengths,
            tenants,
            routes.T,
            residual,
            queries,
            token_keys,
            token_values,
            stored_keys,
            stored_values,
            norm_gain_vector.reshape(features // LANES, LANES),
            router.T,
            adapter_down_map,
        ),
        *weights,
    )
    order = [0]
    for distance in reversed(bits(tensor_devices)):
        order += [at ^ distance for at in order]
    parts = [part]
    for distance in bits(expert_devices):
        other = swap(held, "ep", distance)
        if len(parts) < tensor_devices - 1:
            parts.append(load(*weights, order[len(parts)], features, held))
        held = join(held, other, parts[-1])
    blocks, known, sums = [held], 0, None
    for distance in reversed(bits(tensor_devices)):
        others = [swap(block, "tp", distance) for block in blocks]
        for block in blocks[known:]:
            fetching = len(parts) < tensor_devices
            sums, *more = partial(
                block, parts[known], sums, *weights, order[len(parts)] if fetching else None
            )
            parts += more
            known += 1
        blocks = blocks + [tie(block, sums) if distance > 1 else block for block in others]
    while len(parts) < tensor_devices:
        parts.append(load(*weights, order[len(parts)], features, held))
    steps = bits(tensor_devices)
    groups = [tuple(k for k in range(tensor_devices) if k & -k == step) for step in steps] + [(0,)]
    sent, active = experts(
        expert_devices // EXPERT_COUNT,
        groups[0],
        sums,
        known,
        blocks,
        parts[known:],
        expert_down_weight,
        adapter_up_map,
    )
    received = {k: [] for k in range(tensor_devices)}
    for step, group, following in zip(steps, groups[:-1], groups[1:], strict=True):
        arriving = swap(sent, "tp", step)
        made = down(following, active, expert_down_weight, features, sent)
        for i, k in enumerate(group):
            received[k ^ step].append(arriving[i])
        kept = [
            sum((block.astype(F32) for block in received[k]), made[i])
            for i, k in enumerate(following)
        ]
        if following != (0,):
            sent = jnp.stack([block.astype(BF16) for block in kept])
    kept = kept[0].reshape(expert_devices, rows, features)
    for distance in bits(expert_devices):
        kept, sent = kept[0::2], kept[1::2].astype(BF16)
        kept = kept + swap(sent, "ep", distance).astype(F32)
    return (state.astype(F32) + kept[0]).astype(BF16)


def solution(mesh):
    placed = (
        P(("groups", "ep"), "tp"),
        P(("groups", "ep"), "tp"),
        P(("groups", "ep"), "tp"),
        P(("groups", "ep"), "tp"),
        P(("groups", "ep"), None, "tp"),
        P(("groups", "ep"), None, "tp"),
        P(("groups", "ep")),
        P("tp"),
        P("tp", None),
        P(None, ("ep", "tp")),
        P(None, ("ep", "tp")),
        P(("ep", "tp"), None),
        P("tp", None),
        P(None, ("ep", "tp")),
        P(("groups", "ep"), None),
        P(("groups", "ep")),
    )
    return jax.shard_map(
        per_device, mesh=mesh, in_specs=placed, out_specs=P(("groups", "ep"), "tp"), check_vma=False
    )
```

```python
import functools

import jax
import jax.numpy as jnp
from jax import lax
from jax.experimental import pallas as pl
from jax.experimental.pallas import tpu as pltpu
from jax.sharding import PartitionSpec as P

HEADS = 24
KVH = 8
HD = 128
EXPERT_COUNT = 4
ADAPTER_RANK = 16
TENANT_COUNT = 8
LANES = 128
ADAPTER_LANES = EXPERT_COUNT * ADAPTER_RANK
DIFF_HI, DIFF_LO, SQ_HI, SQ_LO, FIRST, SECOND, TENANT = range(ADAPTER_LANES, ADAPTER_LANES + 7)
F32 = jnp.float32
BF16 = jnp.bfloat16
ANY_LANES = (((1,), (1,)), ((), ()))


VMEM = pl.BlockSpec(memory_space=pltpu.VMEM)
HBM = pl.BlockSpec(memory_space=pl.ANY)


def in_hbm(*arrays):
    return [pltpu.with_memory_space_constraint(array, pltpu.HBM) for array in arrays]


def column(values, rows):
    index = lax.broadcasted_iota(jnp.int32, (rows, LANES), 0)
    out = jnp.zeros((rows, LANES), jnp.int32)
    for r in range(rows):
        out = jnp.where(index == r, values(r), out)
    return out


def fetch(weights, items, parts, arrived):
    copies = []
    for i, ((distance, which), part) in enumerate(zip(items, parts, strict=True)):
        features = part.shape[0]
        start = pl.multiple_of((lax.axis_index("tp") ^ distance) * features, features)
        copies.append(
            pltpu.make_async_copy(
                weights[which].at[pl.ds(start, features), :], part, arrived.at[i]
            )
        )
        copies[-1].start()
    return copies


def attend_kernel(*refs):
    count = 12
    sources, weights = refs[:count], refs[count : count + 2]
    outs, parts = refs[count + 2 : count + 4], refs[count + 4 : count + 6]
    buffers, arrived, weights_arrived = refs[count + 6 : -2], refs[-2], refs[-1]
    copies = [
        pltpu.make_async_copy(source, buffer, arrived.at[i])
        for i, (source, buffer) in enumerate(zip(sources, buffers, strict=True))
    ]
    for i in (7, 4, 0, 5, 8, 6, 3, 9, 1, 2, 10, 11):
        copies[i].start()
    fetched = fetch(weights, ((0, 0), (0, 1)), parts, weights_arrived)
    attend_body(*buffers, *outs, wait=lambda *which: [copies[i].wait() for i in which])
    for copy in fetched:
        copy.wait()


def attend_body(
    lengths,
    tenants,
    routes,
    residual,
    queries,
    token_keys,
    token_values,
    stored_keys,
    stored_values,
    gain,
    router,
    adapter_down,
    state_out,
    payload_out,
    *,
    wait,
):
    rows, features = residual.shape
    kv_local = token_keys.shape[1] // HD
    cache = stored_keys.shape[1]
    group = HEADS // KVH
    scale = HD ** (-0.5)
    wait(0, 4, 7)
    heads = kv_local * group
    together = 2 if rows % 2 == 0 else 1
    length_column = column(lambda r: lengths[r], rows)
    stacked_length = jnp.concatenate([length_column[:, :1]] * heads, axis=0)
    stacked_row = lax.rem(
        lax.broadcasted_iota(jnp.int32, (heads * rows, cache), 0), jnp.int32(rows)
    )
    visible = lax.broadcasted_iota(jnp.int32, (heads * rows, cache), 1) < stacked_length

    def stacked(get):
        return jnp.concatenate([get(g, j) for g in range(kv_local) for j in range(group)], axis=0)

    def head_lanes(g, j=None):
        h = g if j is None else g * group + j
        return slice(h * HD, (h + 1) * HD)

    query = stacked(lambda g, j: queries[:, head_lanes(g, j)])
    wide = jnp.concatenate([query] * kv_local, axis=1)
    lane_head = lax.broadcasted_iota(jnp.int32, wide.shape, 1) // HD
    row_head = lax.broadcasted_iota(jnp.int32, wide.shape, 0) // (group * rows)
    wide = jnp.where(lane_head == row_head, wide.astype(F32), 0.0).astype(BF16)
    scores = jnp.zeros((heads * rows, cache), F32)
    for r in range(0, rows, together):
        keys = stored_keys[r : r + together].reshape(together * cache, kv_local * HD)
        every = lax.dot_general(wide, keys, ANY_LANES, preferred_element_type=F32)
        for i in range(together):
            scores = jnp.where(
                stacked_row == r + i, every[:, i * cache : (i + 1) * cache], scores
            )
    scores = jnp.where(visible, scores * scale, -jnp.inf)
    wait(5)
    fresh_key = stacked(lambda g, j: token_keys[:, head_lanes(g)].astype(F32))
    fresh = jnp.sum(query.astype(F32) * fresh_key, axis=1, keepdims=True) * scale
    largest = jnp.maximum(jnp.max(scores, axis=1, keepdims=True), fresh)
    cache_exp = jnp.exp(scores - largest)
    fresh_exp = jnp.exp(fresh - largest)
    denominator = jnp.sum(cache_exp, axis=1, keepdims=True) + fresh_exp
    probs = cache_exp / denominator
    fresh_prob = (fresh_exp / denominator).astype(BF16).astype(F32)
    wait(8)
    every = jnp.zeros((heads * rows, kv_local * HD), F32)
    for r in range(0, rows, together):
        values = stored_values[r : r + together].reshape(together * cache, kv_local * HD)
        own = [jnp.where(stacked_row == r + i, probs, 0.0).astype(BF16) for i in range(together)]
        every = every + jnp.dot(
            jnp.concatenate(own, axis=1), values, preferred_element_type=F32
        )
    wait(3, 6, 9)
    squares = jnp.zeros((rows, 1), F32)
    for g in range(kv_local):
        fresh_value = token_values[:, head_lanes(g)].astype(F32)
        for j in range(group):
            lanes = head_lanes(g, j)
            place = slice((g * group + j) * rows, (g * group + j + 1) * rows)
            attended = every[place, head_lanes(g)] + fresh_prob[place] * fresh_value
            state = (residual[:, lanes].astype(F32) + attended).astype(BF16)
            state_out[:, lanes] = state
            state = state.astype(F32)
            squares = squares + jnp.sum(state * state, axis=1, keepdims=True)
            payload_out[:, lanes] = (
                state * gain[lanes.start // LANES : lanes.start // LANES + 1, :]
            ).astype(BF16)
    wait(1, 2, 10, 11)
    scaled = payload_out[:, :features]
    logits = lax.dot_general(scaled, router[...], ANY_LANES, preferred_element_type=F32)
    first = column(lambda r: routes[0, r], rows)
    second = column(lambda r: routes[1, r], rows)
    tenant = column(lambda r: tenants[r], rows)
    expert = lax.broadcasted_iota(jnp.int32, logits.shape, 1)
    chosen = jnp.where(expert == first[:, :EXPERT_COUNT], logits, 0.0) - jnp.where(
        expert == second[:, :EXPERT_COUNT], logits, 0.0
    )
    diff = jnp.sum(chosen, axis=1, keepdims=True)
    adapter = jnp.dot(scaled, adapter_down[...], preferred_element_type=F32)
    lane = lax.broadcasted_iota(jnp.int32, (rows, LANES), 1)
    tail = jnp.zeros((rows, LANES), F32)
    for start in range(0, adapter.shape[1], LANES):
        owner = (lane + start) // ADAPTER_LANES
        tail = tail + jnp.where(owner == tenant, adapter[:, start : start + LANES], 0.0)
    tail = tail + pltpu.roll(tail, ADAPTER_LANES, 1)
    diff_hi = diff.astype(BF16).astype(F32)
    squares_hi = squares.astype(BF16).astype(F32)
    for place, value in (
        (DIFF_HI, diff_hi),
        (DIFF_LO, diff - diff_hi),
        (SQ_HI, squares_hi),
        (SQ_LO, squares - squares_hi),
        (FIRST, first.astype(F32)),
        (SECOND, second.astype(F32)),
        (TENANT, tenant.astype(F32)),
    ):
        tail = jnp.where(lane == place, value, tail)
    payload_out[:, features:] = tail.astype(BF16)


def attend(args, gate_weight, up_weight):
    rows, features = args[3].shape
    return pl.pallas_call(
        attend_kernel,
        out_shape=(
            jax.ShapeDtypeStruct((rows, features), BF16),
            jax.ShapeDtypeStruct((rows, features + LANES), BF16),
            *[jax.ShapeDtypeStruct((features, gate_weight.shape[1]), BF16)] * 2,
        ),
        in_specs=[HBM] * (len(args) + 2),
        out_specs=(VMEM,) * 4,
        scratch_shapes=[
            (pltpu.SMEM if i < 3 else pltpu.VMEM)(arg.shape, arg.dtype)
            for i, arg in enumerate(args)
        ]
        + [pltpu.SemaphoreType.DMA((len(args),)), pltpu.SemaphoreType.DMA((2,))],
        compiler_params=pltpu.CompilerParams(vmem_limit_bytes=12 * 2**20),
        cost_estimate=pl.CostEstimate(
            flops=200_000_000, bytes_accessed=10_000_000, transcendentals=20_000
        ),
        name="attend",
    )(*in_hbm(*args, gate_weight, up_weight))


def load_kernel(item, gate_weight, up_weight, after, part, arrived):
    for copy in fetch((gate_weight, up_weight), (item,), (part,), arrived):
        copy.wait()


def load(weights, item, features, after):
    hidden = weights[0].shape[1]
    return pl.pallas_call(
        functools.partial(load_kernel, item),
        out_shape=jax.ShapeDtypeStruct((features, hidden), BF16),
        in_specs=[HBM] * 3,
        out_specs=VMEM,
        scratch_shapes=[pltpu.SemaphoreType.DMA((1,))],
        compiler_params=pltpu.CompilerParams(vmem_limit_bytes=2**20),
        cost_estimate=pl.CostEstimate(
            flops=0, bytes_accessed=2 * features * hidden, transcendentals=0
        ),
        name="load",
    )(*in_hbm(*weights), after)


def partial_kernel(items, first, block, gate_part, up_part, *refs):
    features = gate_part.shape[0]
    sums, refs = (None, refs) if first else (refs[0], refs[1:])
    weights, totals = refs[:2], refs[2]
    fetched = fetch(weights, items, refs[3 : 3 + len(items)], refs[-1])

    def tile(n, carry):
        for i, part in enumerate((gate_part, up_part)):
            width = part.shape[1] // 2
            lanes = pl.ds(pl.multiple_of(n * width, LANES if width % LANES == 0 else width), width)
            product = jnp.dot(
                block[:, :features], part[:, lanes], preferred_element_type=F32
            )
            totals[i, :, lanes] = product if first else sums[i, :, lanes] + product
        return carry

    if gate_part.shape[1] % (2 * LANES) == 0:
        lax.fori_loop(0, 2, tile, 0)
    else:
        for i, part in enumerate((gate_part, up_part)):
            product = jnp.dot(block[:, :features], part[...], preferred_element_type=F32)
            totals[i] = product if first else sums[i] + product
    for copy in fetched:
        copy.wait()


def partial(block, parts, sums, weights, items):
    rows, width = block.shape
    features = width - LANES
    hidden = weights[0].shape[1]
    first = sums is None
    return pl.pallas_call(
        functools.partial(partial_kernel, items, first),
        out_shape=(
            jax.ShapeDtypeStruct((2, rows, hidden), F32),
            *[jax.ShapeDtypeStruct((features, hidden), BF16)] * len(items),
        ),
        in_specs=[VMEM] * (3 if first else 4) + [HBM] * 2,
        out_specs=(VMEM,) * (1 + len(items)),
        scratch_shapes=[pltpu.SemaphoreType.DMA((max(1, len(items)),))],
        compiler_params=pltpu.CompilerParams(vmem_limit_bytes=8 * 2**20),
        cost_estimate=pl.CostEstimate(
            flops=4 * rows * features * hidden,
            bytes_accessed=2 * len(items) * features * hidden,
            transcendentals=0,
        ),
        name="partial",
    )(block, *parts, *(() if first else (sums,)), *in_hbm(*weights))


def expert_kernel(replicas, targets, known, tensor_devices, items, sums, *refs):
    blocks, refs = refs[:tensor_devices], refs[tensor_devices:]
    present = 2 * (tensor_devices - known) - len(items)
    parts, refs = list(refs[:present]), refs[present:]
    weights, down_weight, adapter_weight, out, active, totals = refs[:2], *refs[2:7]
    late, refs = refs[7 : 7 + len(items)], refs[7 + len(items) :]
    down_part, adapter_up, late_arrived, arrived = refs
    rows, width = blocks[0].shape
    features = width - LANES
    hidden = active.shape[1]
    fetched = fetch(weights, items, late, late_arrived)
    adapter_copy = pltpu.make_async_copy(adapter_weight, adapter_up, arrived.at[len(targets)])
    adapter_copy.start()
    parts += late
    pairs = [
        (block, parts[2 * i], parts[2 * i + 1]) for i, block in enumerate(blocks[known:])
    ]
    early = present // 2
    tile = hidden // 2 if hidden % (2 * LANES) == 0 else hidden

    def products(n, which, some, total):
        lanes = pl.ds(pl.multiple_of(n * tile, tile), tile)
        total = total[which, :, lanes]
        for pair in some:
            total = total + jnp.dot(
                pair[0][:, :features], pair[1 + which][:, lanes], preferred_element_type=F32
            )
        return lanes, total

    def first_pass(n, carry):
        for which in range(2):
            lanes, total = products(n, which, pairs[:early], sums)
            totals[which, :, lanes] = total
        return carry

    lax.fori_loop(0, hidden // tile, first_pass, 0)
    expert = lax.axis_index("ep") // replicas
    tail = jnp.zeros((rows, LANES), F32)
    for block in blocks:
        tail = tail + block[:, features:].astype(F32)
    place = lambda k: tail[:, k : k + 1]
    here = blocks[0][:, features:].astype(F32)
    inverse_rms = lax.rsqrt(
        (place(SQ_HI) + place(SQ_LO)) / (features * tensor_devices) + 1e-05
    )
    diff = (place(DIFF_HI) + place(DIFF_LO)) * inverse_rms
    expert_float = expert.astype(F32)
    is_first = here[:, FIRST : FIRST + 1] == expert_float
    is_second = here[:, SECOND : SECOND + 1] == expert_float
    weight = jnp.where(
        is_first, jax.nn.sigmoid(diff), jnp.where(is_second, jax.nn.sigmoid(-diff), 0.0)
    )
    lowrank = (tail * inverse_rms).astype(BF16)
    spread_shape = (LANES, TENANT_COUNT * ADAPTER_RANK)
    source = lax.broadcasted_iota(jnp.int32, spread_shape, 0)
    target = lax.broadcasted_iota(jnp.int32, spread_shape, 1)
    spread = jnp.where(
        source == expert * ADAPTER_RANK + lax.rem(target, jnp.int32(ADAPTER_RANK)), 1.0, 0.0
    ).astype(BF16)
    lane = lax.broadcasted_iota(jnp.int32, (rows, TENANT_COUNT * ADAPTER_RANK), 1)
    own_tenant = (lane // ADAPTER_RANK).astype(F32) == here[:, TENANT : TENANT + 1]
    adapter_rows = jnp.where(
        own_tenant, jnp.dot(lowrank, spread, preferred_element_type=F32), 0.0
    ).astype(BF16)
    adapter_copy.wait()
    copies = down_copies(down_weight, targets, down_part, arrived)
    for i, copy in enumerate(fetched):
        copy.wait()
        if i < len(copies):
            copies[i].start()
    for copy in copies[len(fetched) :]:
        copy.start()

    def second_pass(n, carry):
        lanes, gate = products(n, 0, pairs[early:], totals)
        _, up = products(n, 1, pairs[early:], totals)
        gate = gate * inverse_rms
        up = up * inverse_rms + jnp.dot(
            adapter_rows, adapter_up[:, lanes], preferred_element_type=F32
        )
        active[:, lanes] = (gate * jax.nn.sigmoid(gate) * up * weight).astype(BF16)
        return carry

    lax.fori_loop(0, hidden // tile, second_pass, 0)
    down_products(active, copies, down_part, out)


def experts(replicas, targets, sums, known, blocks, parts, weights, items, down_weight, adapter_up):
    rows, width = blocks[0].shape
    features, hidden = width - LANES, sums.shape[2]
    missing = len(blocks) - known
    return pl.pallas_call(
        functools.partial(expert_kernel, replicas, targets, known, len(blocks), items),
        out_shape=(
            jax.ShapeDtypeStruct((len(targets), rows, features), BF16),
            jax.ShapeDtypeStruct((rows, hidden), BF16),
        ),
        in_specs=[VMEM] * (1 + len(blocks) + len(parts)) + [HBM] * 4,
        out_specs=(VMEM, VMEM),
        scratch_shapes=[
            pltpu.VMEM(sums.shape, F32),
            *[pltpu.VMEM((features, hidden), BF16)] * len(items),
            pltpu.VMEM((len(targets), hidden, features), BF16),
            pltpu.VMEM(adapter_up.shape, BF16),
            pltpu.SemaphoreType.DMA((max(1, len(items)),)),
            pltpu.SemaphoreType.DMA((len(targets) + 1,)),
        ],
        compiler_params=pltpu.CompilerParams(vmem_limit_bytes=20 * 2**20),
        cost_estimate=pl.CostEstimate(
            flops=2 * rows * hidden * features * (2 * missing + len(targets)),
            bytes_accessed=2 * (len(items) + len(targets)) * hidden * features,
            transcendentals=0,
        ),
        name="experts",
    )(sums, *blocks, *parts, *in_hbm(*weights, down_weight, adapter_up))


def down_copies(down_weight, targets, down_part, arrived):
    features = down_part.shape[2]
    return [
        pltpu.make_async_copy(
            down_weight.at[
                :, pl.ds(pl.multiple_of((lax.axis_index("tp") ^ k) * features, features), features)
            ],
            down_part.at[i],
            arrived.at[i],
        )
        for i, k in enumerate(targets)
    ]


def down_products(active, copies, down_part, out):
    for i, copy in enumerate(copies):
        copy.wait()
        out[i] = jnp.dot(active[...], down_part[i], preferred_element_type=F32).astype(out.dtype)


def down_kernel(targets, active, down_weight, after, out, down_part, arrived):
    copies = down_copies(down_weight, targets, down_part, arrived)
    for copy in copies:
        copy.start()
    down_products(active, copies, down_part, out)


def down(targets, active, down_weight, features, after):
    rows, hidden = active.shape
    return pl.pallas_call(
        functools.partial(down_kernel, targets),
        out_shape=jax.ShapeDtypeStruct((len(targets), rows, features), F32),
        in_specs=[VMEM, HBM, HBM],
        out_specs=VMEM,
        scratch_shapes=[
            pltpu.VMEM((len(targets), hidden, features), BF16),
            pltpu.SemaphoreType.DMA((len(targets),)),
        ],
        compiler_params=pltpu.CompilerParams(vmem_limit_bytes=16 * 2**20),
        cost_estimate=pl.CostEstimate(
            flops=2 * rows * hidden * features * len(targets),
            bytes_accessed=2 * len(targets) * hidden * features,
            transcendentals=0,
        ),
        name="down",
    )(active, *in_hbm(down_weight), after)


def join_kernel(first, second, after, out):
    count = first.shape[0]
    out[:count] = first[...]
    out[count:] = second[...]


def join(first, second, after):
    return pl.pallas_call(
        join_kernel,
        out_shape=jax.ShapeDtypeStruct((2 * first.shape[0], *first.shape[1:]), first.dtype),
        in_specs=[VMEM, VMEM, HBM],
        out_specs=VMEM,
        compiler_params=pltpu.CompilerParams(vmem_limit_bytes=4 * 2**20),
        name="join",
    )(first, second, after)


def tie_kernel(array, after, out):
    pass


def tie(array, after):
    return pl.pallas_call(
        tie_kernel,
        out_shape=jax.ShapeDtypeStruct(array.shape, array.dtype),
        in_specs=[HBM, HBM],
        out_specs=HBM,
        input_output_aliases={0: 0},
        compiler_params=pltpu.CompilerParams(vmem_limit_bytes=2**20),
        name="tie",
    )(array, after)


def swap(x, axis, distance):
    count = lax.axis_size(axis)
    return lax.ppermute(x, axis, [(i, i ^ distance) for i in range(count)])


def bits(count):
    return [1 << b for b in range(count.bit_length() - 1)]


def per_device(
    residual,
    queries,
    token_keys,
    token_values,
    stored_keys,
    stored_values,
    lengths,
    norm_gain_vector,
    router,
    expert_gate_weight,
    expert_up_weight,
    expert_down_weight,
    adapter_down_map,
    adapter_up_map,
    routes,
    tenants,
):
    rows, features = residual.shape
    expert_devices = lax.axis_size("ep")
    tensor_devices = lax.axis_size("tp")
    weights = (expert_gate_weight, expert_up_weight)
    state, held, *parts = attend(
        (
            lengths,
            tenants,
            routes.T,
            residual,
            queries,
            token_keys,
            token_values,
            stored_keys,
            stored_values,
            norm_gain_vector.reshape(features // LANES, LANES),
            router.T,
            adapter_down_map,
        ),
        *weights,
    )
    order = [0]
    for distance in reversed(bits(tensor_devices)):
        order += [at ^ distance for at in order]
    items = [(at, which) for at in order[1:] for which in range(2)]
    for distance in bits(expert_devices):
        other = swap(held, "ep", distance)
        if items:
            parts.append(load(weights, items.pop(0), features, held))
        held = join(held, other, parts[-1])
    blocks, known, sums = [held], 0, None
    for distance in reversed(bits(tensor_devices)):
        others = [swap(block, "tp", distance) for block in blocks]
        for block in blocks[known:]:
            some = tuple(items[:2]) if distance > 1 else ()
            items = items[len(some) :]
            sums, *more = partial(
                block, parts[2 * known : 2 * known + 2], sums, weights, some
            )
            parts += more
            known += 1
        blocks = blocks + [tie(block, sums) if distance > 1 else block for block in others]
    half = tensor_devices // 2
    sent, active = experts(
        expert_devices // EXPERT_COUNT,
        tuple(range(half, tensor_devices)),
        sums,
        known,
        blocks,
        parts[2 * known :],
        weights,
        tuple(items),
        expert_down_weight,
        adapter_up_map,
    )
    kept = None
    while half:
        other = swap(sent, "tp", half)
        if kept is None:
            kept = down(tuple(range(half)), active, expert_down_weight, features, sent)
        kept = kept + other.astype(F32)
        half //= 2
        if half:
            kept, sent = kept[:half], kept[half:].astype(BF16)
    kept = kept[0].reshape(expert_devices, rows, features)
    for distance in bits(expert_devices):
        kept, sent = kept[0::2], kept[1::2].astype(BF16)
        kept = kept + swap(sent, "ep", distance).astype(F32)
    return (state.astype(F32) + kept[0]).astype(BF16)


def solution(mesh):
    placed = (
        P(("groups", "ep"), "tp"),
        P(("groups", "ep"), "tp"),
        P(("groups", "ep"), "tp"),
        P(("groups", "ep"), "tp"),
        P(("groups", "ep"), None, "tp"),
        P(("groups", "ep"), None, "tp"),
        P(("groups", "ep")),
        P("tp"),
        P("tp", None),
        P(None, ("ep", "tp")),
        P(None, ("ep", "tp")),
        P(("ep", "tp"), None),
        P("tp", None),
        P(None, ("ep", "tp")),
        P(("groups", "ep"), None),
        P(("groups", "ep")),
    )
    return jax.shard_map(
        per_device, mesh=mesh, in_specs=placed, out_specs=P(("groups", "ep"), "tp"), check_vma=False
    )
```

```python
import functools

import jax
import jax.numpy as jnp
from jax import lax
from jax.experimental import pallas as pl
from jax.experimental.pallas import tpu as pltpu
from jax.sharding import PartitionSpec as P

HEADS = 24
KVH = 8
HD = 128
EXPERT_COUNT = 4
ADAPTER_RANK = 16
TENANT_COUNT = 8
LANES = 128
ADAPTER_LANES = EXPERT_COUNT * ADAPTER_RANK
DIFF_HI, DIFF_LO, SQ_HI, SQ_LO, FIRST, SECOND, TENANT = range(ADAPTER_LANES, ADAPTER_LANES + 7)
F32 = jnp.float32
BF16 = jnp.bfloat16
ANY_LANES = (((1,), (1,)), ((), ()))


VMEM = pl.BlockSpec(memory_space=pltpu.VMEM)
HBM = pl.BlockSpec(memory_space=pl.ANY)


def in_hbm(*arrays):
    return [pltpu.with_memory_space_constraint(array, pltpu.HBM) for array in arrays]


def column(values, rows):
    index = lax.broadcasted_iota(jnp.int32, (rows, LANES), 0)
    out = jnp.zeros((rows, LANES), jnp.int32)
    for r in range(rows):
        out = jnp.where(index == r, values(r), out)
    return out


def at_distance(distance, size):
    return pl.ds(pl.multiple_of((lax.axis_index("tp") ^ distance) * size, size), size)


def fetch(gate_weight, distance, part, arrived):
    copy = pltpu.make_async_copy(
        gate_weight.at[at_distance(distance, part.shape[0]), :], part, arrived
    )
    copy.start()
    return copy


def attend_kernel(*refs):
    count = 12
    sources, gate_weight, outs, part = refs[:count], refs[count], refs[count + 1 : count + 3], refs[count + 3]
    buffers, arrived, part_arrived = refs[count + 4 : -2], refs[-2], refs[-1]
    copies = [
        pltpu.make_async_copy(source, buffer, arrived.at[i])
        for i, (source, buffer) in enumerate(zip(sources, buffers, strict=True))
    ]
    for i in (7, 4, 0, 5, 8, 6, 3, 9, 1, 2, 10, 11):
        copies[i].start()
    fetched = fetch(gate_weight, 0, part, part_arrived)
    attend_body(*buffers, *outs, wait=lambda *which: [copies[i].wait() for i in which])
    fetched.wait()


def attend_body(
    lengths,
    tenants,
    routes,
    residual,
    queries,
    token_keys,
    token_values,
    stored_keys,
    stored_values,
    gain,
    router,
    adapter_down,
    state_out,
    payload_out,
    *,
    wait,
):
    rows, features = residual.shape
    kv_local = token_keys.shape[1] // HD
    cache = stored_keys.shape[1]
    group = HEADS // KVH
    scale = HD ** (-0.5)
    wait(0, 4, 7)
    heads = kv_local * group
    together = 2 if rows % 2 == 0 else 1
    length_column = column(lambda r: lengths[r], rows)
    stacked_length = jnp.concatenate([length_column[:, :1]] * heads, axis=0)
    stacked_row = lax.rem(
        lax.broadcasted_iota(jnp.int32, (heads * rows, cache), 0), jnp.int32(rows)
    )
    visible = lax.broadcasted_iota(jnp.int32, (heads * rows, cache), 1) < stacked_length

    def stacked(get):
        return jnp.concatenate([get(g, j) for g in range(kv_local) for j in range(group)], axis=0)

    def head_lanes(g, j=None):
        h = g if j is None else g * group + j
        return slice(h * HD, (h + 1) * HD)

    query = stacked(lambda g, j: queries[:, head_lanes(g, j)])
    wide = jnp.concatenate([query] * kv_local, axis=1)
    lane_head = lax.broadcasted_iota(jnp.int32, wide.shape, 1) // HD
    row_head = lax.broadcasted_iota(jnp.int32, wide.shape, 0) // (group * rows)
    wide = jnp.where(lane_head == row_head, wide.astype(F32), 0.0).astype(BF16)
    scores = jnp.zeros((heads * rows, cache), F32)
    for r in range(0, rows, together):
        keys = stored_keys[r : r + together].reshape(together * cache, kv_local * HD)
        every = lax.dot_general(wide, keys, ANY_LANES, preferred_element_type=F32)
        for i in range(together):
            scores = jnp.where(
                stacked_row == r + i, every[:, i * cache : (i + 1) * cache], scores
            )
    scores = jnp.where(visible, scores * scale, -jnp.inf)
    wait(5)
    fresh_key = stacked(lambda g, j: token_keys[:, head_lanes(g)].astype(F32))
    fresh = jnp.sum(query.astype(F32) * fresh_key, axis=1, keepdims=True) * scale
    largest = jnp.maximum(jnp.max(scores, axis=1, keepdims=True), fresh)
    cache_exp = jnp.exp(scores - largest)
    fresh_exp = jnp.exp(fresh - largest)
    denominator = jnp.sum(cache_exp, axis=1, keepdims=True) + fresh_exp
    probs = cache_exp / denominator
    fresh_prob = (fresh_exp / denominator).astype(BF16).astype(F32)
    wait(8)
    every = jnp.zeros((heads * rows, kv_local * HD), F32)
    for r in range(0, rows, together):
        values = stored_values[r : r + together].reshape(together * cache, kv_local * HD)
        own = [jnp.where(stacked_row == r + i, probs, 0.0).astype(BF16) for i in range(together)]
        every = every + jnp.dot(
            jnp.concatenate(own, axis=1), values, preferred_element_type=F32
        )
    wait(3, 6, 9)
    squares = jnp.zeros((rows, 1), F32)
    for g in range(kv_local):
        fresh_value = token_values[:, head_lanes(g)].astype(F32)
        for j in range(group):
            lanes = head_lanes(g, j)
            place = slice((g * group + j) * rows, (g * group + j + 1) * rows)
            attended = every[place, head_lanes(g)] + fresh_prob[place] * fresh_value
            state = (residual[:, lanes].astype(F32) + attended).astype(BF16)
            state_out[:, lanes] = state
            state = state.astype(F32)
            squares = squares + jnp.sum(state * state, axis=1, keepdims=True)
            payload_out[:, lanes] = (
                state * gain[lanes.start // LANES : lanes.start // LANES + 1, :]
            ).astype(BF16)
    wait(1, 2, 10, 11)
    scaled = payload_out[:, :features]
    logits = lax.dot_general(scaled, router[...], ANY_LANES, preferred_element_type=F32)
    first = column(lambda r: routes[0, r], rows)
    second = column(lambda r: routes[1, r], rows)
    tenant = column(lambda r: tenants[r], rows)
    expert = lax.broadcasted_iota(jnp.int32, logits.shape, 1)
    chosen = jnp.where(expert == first[:, :EXPERT_COUNT], logits, 0.0) - jnp.where(
        expert == second[:, :EXPERT_COUNT], logits, 0.0
    )
    diff = jnp.sum(chosen, axis=1, keepdims=True)
    adapter = jnp.dot(scaled, adapter_down[...], preferred_element_type=F32)
    lane = lax.broadcasted_iota(jnp.int32, (rows, LANES), 1)
    tail = jnp.zeros((rows, LANES), F32)
    for start in range(0, adapter.shape[1], LANES):
        owner = (lane + start) // ADAPTER_LANES
        tail = tail + jnp.where(owner == tenant, adapter[:, start : start + LANES], 0.0)
    tail = tail + pltpu.roll(tail, ADAPTER_LANES, 1)
    diff_hi = diff.astype(BF16).astype(F32)
    squares_hi = squares.astype(BF16).astype(F32)
    for place, value in (
        (DIFF_HI, diff_hi),
        (DIFF_LO, diff - diff_hi),
        (SQ_HI, squares_hi),
        (SQ_LO, squares - squares_hi),
        (FIRST, first.astype(F32)),
        (SECOND, second.astype(F32)),
        (TENANT, tenant.astype(F32)),
    ):
        tail = jnp.where(lane == place, value, tail)
    payload_out[:, features:] = tail.astype(BF16)


def attend(args, gate_weight):
    rows, features = args[3].shape
    return pl.pallas_call(
        attend_kernel,
        out_shape=(
            jax.ShapeDtypeStruct((rows, features), BF16),
            jax.ShapeDtypeStruct((rows, features + LANES), BF16),
            jax.ShapeDtypeStruct((features, gate_weight.shape[1]), BF16),
        ),
        in_specs=[HBM] * (len(args) + 1),
        out_specs=(VMEM,) * 3,
        scratch_shapes=[
            (pltpu.SMEM if i < 3 else pltpu.VMEM)(arg.shape, arg.dtype)
            for i, arg in enumerate(args)
        ]
        + [pltpu.SemaphoreType.DMA((len(args),)), pltpu.SemaphoreType.DMA],
        compiler_params=pltpu.CompilerParams(vmem_limit_bytes=12 * 2**20),
        cost_estimate=pl.CostEstimate(
            flops=200_000_000, bytes_accessed=6_000_000, transcendentals=20_000
        ),
        name="attend",
    )(*in_hbm(*args, gate_weight))


def load_kernel(distance, gate_weight, after, part, arrived):
    fetch(gate_weight, distance, part, arrived).wait()


def load(gate_weight, distance, features, after):
    hidden = gate_weight.shape[1]
    return pl.pallas_call(
        functools.partial(load_kernel, distance),
        out_shape=jax.ShapeDtypeStruct((features, hidden), BF16),
        in_specs=[HBM] * 2,
        out_specs=VMEM,
        scratch_shapes=[pltpu.SemaphoreType.DMA],
        compiler_params=pltpu.CompilerParams(vmem_limit_bytes=2**20),
        cost_estimate=pl.CostEstimate(
            flops=0, bytes_accessed=2 * features * hidden, transcendentals=0
        ),
        name="load",
    )(*in_hbm(gate_weight), after)


def halves(hidden):
    return hidden // 2 if hidden % (2 * LANES) == 0 else hidden


def partial_kernel(distance, fetched, first, soon, block, gate_part, up_weight, *refs):
    features, hidden = gate_part.shape
    sums, refs = (None, refs) if first else (refs[0], refs[1:])
    gate_weight, totals = refs[0], refs[1 + soon]
    copy = None if fetched is None else fetch(gate_weight, fetched, refs[2 + soon], refs[-1])
    tile = halves(hidden)
    depth = at_distance(distance, features)

    def products(n, carry):
        lanes = pl.ds(pl.multiple_of(n * tile, tile), tile)
        for i, part in enumerate((gate_part[:, lanes], up_weight[depth, lanes])):
            product = jnp.dot(block[:, :features], part, preferred_element_type=F32)
            totals[i, :, lanes] = product if first else sums[i, :, lanes] + product
        return carry

    lax.fori_loop(0, hidden // tile, products, 0)
    if copy is not None:
        copy.wait()


def partial(block, distance, part, sums, gate_weight, up_weight, fetched, soon):
    rows, width = block.shape
    features = width - LANES
    hidden = gate_weight.shape[1]
    first = sums is None
    more = int(fetched is not None)
    return pl.pallas_call(
        functools.partial(partial_kernel, distance, fetched, first, len(soon)),
        out_shape=(
            jax.ShapeDtypeStruct((2, rows, hidden), F32),
            *[jax.ShapeDtypeStruct((features, hidden), BF16)] * more,
        ),
        in_specs=[VMEM] * (3 if first else 4) + [HBM] * (1 + len(soon)),
        out_specs=(VMEM,) * (1 + more),
        scratch_shapes=[pltpu.SemaphoreType.DMA],
        compiler_params=pltpu.CompilerParams(vmem_limit_bytes=6 * 2**20),
        cost_estimate=pl.CostEstimate(
            flops=4 * rows * features * hidden,
            bytes_accessed=2 * features * hidden,
            transcendentals=0,
        ),
        name="partial",
    )(block, part, up_weight, *(() if first else (sums,)), *in_hbm(gate_weight), *soon)


def expert_kernel(replicas, targets, order, known, sums, *refs):
    tensor_devices = len(order)
    blocks, parts = refs[:tensor_devices], refs[tensor_devices : 2 * tensor_devices - known]
    up_weight, down_weight, adapter_weight, out, active, adapter_up, arrived = refs[
        2 * tensor_devices - known :
    ]
    rows, width = blocks[0].shape
    features = width - LANES
    hidden = active.shape[1]
    adapter_copy = pltpu.make_async_copy(adapter_weight, adapter_up, arrived)
    adapter_copy.start()
    expert = lax.axis_index("ep") // replicas
    tail = jnp.zeros((rows, LANES), F32)
    for block in blocks:
        tail = tail + block[:, features:].astype(F32)
    place = lambda k: tail[:, k : k + 1]
    here = blocks[0][:, features:].astype(F32)
    inverse_rms = lax.rsqrt(
        (place(SQ_HI) + place(SQ_LO)) / (features * tensor_devices) + 1e-05
    )
    diff = (place(DIFF_HI) + place(DIFF_LO)) * inverse_rms
    expert_float = expert.astype(F32)
    is_first = here[:, FIRST : FIRST + 1] == expert_float
    is_second = here[:, SECOND : SECOND + 1] == expert_float
    weight = jnp.where(
        is_first, jax.nn.sigmoid(diff), jnp.where(is_second, jax.nn.sigmoid(-diff), 0.0)
    )
    lowrank = (tail * inverse_rms).astype(BF16)
    spread_shape = (LANES, TENANT_COUNT * ADAPTER_RANK)
    source = lax.broadcasted_iota(jnp.int32, spread_shape, 0)
    target = lax.broadcasted_iota(jnp.int32, spread_shape, 1)
    spread = jnp.where(
        source == expert * ADAPTER_RANK + lax.rem(target, jnp.int32(ADAPTER_RANK)), 1.0, 0.0
    ).astype(BF16)
    lane = lax.broadcasted_iota(jnp.int32, (rows, TENANT_COUNT * ADAPTER_RANK), 1)
    own_tenant = (lane // ADAPTER_RANK).astype(F32) == here[:, TENANT : TENANT + 1]
    adapter_rows = jnp.where(
        own_tenant, jnp.dot(lowrank, spread, preferred_element_type=F32), 0.0
    ).astype(BF16)
    adapter_copy.wait()
    tile = halves(hidden)

    def products(n, carry):
        lanes = pl.ds(pl.multiple_of(n * tile, tile), tile)
        gate, up = sums[0, :, lanes], sums[1, :, lanes]
        for block, part, distance in zip(blocks[known:], parts, order[known:], strict=True):
            scaled = block[:, :features]
            gate = gate + jnp.dot(scaled, part[:, lanes], preferred_element_type=F32)
            up = up + jnp.dot(
                scaled,
                up_weight[at_distance(distance, features), lanes],
                preferred_element_type=F32,
            )
        gate = gate * inverse_rms
        up = up * inverse_rms + jnp.dot(
            adapter_rows, adapter_up[:, lanes], preferred_element_type=F32
        )
        active[:, lanes] = (gate * jax.nn.sigmoid(gate) * up * weight).astype(BF16)
        return carry

    lax.fori_loop(0, hidden // tile, products, 0)
    down_products(targets, active, down_weight, out)


def down_products(targets, active, down_weight, out):
    for i, distance in enumerate(targets):
        lanes = at_distance(distance, out.shape[2])
        out[i] = jnp.dot(
            active[...], down_weight[:, lanes], preferred_element_type=F32
        ).astype(out.dtype)


def experts(replicas, targets, order, sums, known, blocks, parts, up_weight, down_weight, adapter_up):
    rows, width = blocks[0].shape
    features, hidden = width - LANES, sums.shape[2]
    return pl.pallas_call(
        functools.partial(expert_kernel, replicas, targets, order, known),
        out_shape=(
            jax.ShapeDtypeStruct((len(targets), rows, features), BF16),
            jax.ShapeDtypeStruct((rows, hidden), BF16),
        ),
        in_specs=[VMEM] * (3 + len(blocks) + len(parts)) + [HBM],
        out_specs=(VMEM, VMEM),
        scratch_shapes=[pltpu.VMEM(adapter_up.shape, BF16), pltpu.SemaphoreType.DMA],
        compiler_params=pltpu.CompilerParams(vmem_limit_bytes=8 * 2**20),
        cost_estimate=pl.CostEstimate(
            flops=2 * rows * hidden * features * (2 * len(parts) + len(targets)),
            bytes_accessed=0,
            transcendentals=0,
        ),
        name="experts",
    )(sums, *blocks, *parts, up_weight, down_weight, *in_hbm(adapter_up))


def down_kernel(targets, active, down_weight, after, out):
    down_products(targets, active, down_weight, out)


def down(targets, active, down_weight, features, after):
    rows, hidden = active.shape
    return pl.pallas_call(
        functools.partial(down_kernel, targets),
        out_shape=jax.ShapeDtypeStruct((len(targets), rows, features), F32),
        in_specs=[VMEM, VMEM, HBM],
        out_specs=VMEM,
        compiler_params=pltpu.CompilerParams(vmem_limit_bytes=4 * 2**20),
        cost_estimate=pl.CostEstimate(
            flops=2 * rows * hidden * features * len(targets),
            bytes_accessed=0,
            transcendentals=0,
        ),
        name="down",
    )(active, down_weight, after)


def join_kernel(first, second, *refs):
    out = refs[-1]
    count = first.shape[0]
    out[:count] = first[...]
    out[count:] = second[...]


def join(first, second, *after):
    return pl.pallas_call(
        join_kernel,
        out_shape=jax.ShapeDtypeStruct((2 * first.shape[0], *first.shape[1:]), first.dtype),
        in_specs=[VMEM, VMEM] + [HBM] * len(after),
        out_specs=VMEM,
        compiler_params=pltpu.CompilerParams(vmem_limit_bytes=4 * 2**20),
        name="join",
    )(first, second, *after)


def tie_kernel(array, after, out):
    pass


def tie(array, after):
    return pl.pallas_call(
        tie_kernel,
        out_shape=jax.ShapeDtypeStruct(array.shape, array.dtype),
        in_specs=[HBM, HBM],
        out_specs=HBM,
        input_output_aliases={0: 0},
        compiler_params=pltpu.CompilerParams(vmem_limit_bytes=2**20),
        name="tie",
    )(array, after)


def swap(x, axis, distance):
    count = lax.axis_size(axis)
    return lax.ppermute(x, axis, [(i, i ^ distance) for i in range(count)])


def bits(count):
    return [1 << b for b in range(count.bit_length() - 1)]


def per_device(
    residual,
    queries,
    token_keys,
    token_values,
    stored_keys,
    stored_values,
    lengths,
    norm_gain_vector,
    router,
    expert_gate_weight,
    expert_up_weight,
    expert_down_weight,
    adapter_down_map,
    adapter_up_map,
    routes,
    tenants,
):
    rows, features = residual.shape
    expert_devices = lax.axis_size("ep")
    tensor_devices = lax.axis_size("tp")
    state, held, *parts = attend(
        (
            lengths,
            tenants,
            routes.T,
            residual,
            queries,
            token_keys,
            token_values,
            stored_keys,
            stored_values,
            norm_gain_vector.reshape(features // LANES, LANES),
            router.T,
            adapter_down_map,
        ),
        expert_gate_weight,
    )
    order = [0]
    for distance in reversed(bits(tensor_devices)):
        order += [at ^ distance for at in order]
    for distance in bits(expert_devices):
        other = swap(held, "ep", distance)
        if len(parts) < tensor_devices:
            parts.append(load(expert_gate_weight, order[len(parts)], features, held))
        last = 2 * distance == expert_devices
        held = join(held, other, parts[-1], *((expert_up_weight,) if last else ()))
    blocks, known, sums = [held], 0, None
    for distance in reversed(bits(tensor_devices)):
        others = [swap(block, "tp", distance) for block in blocks]
        for block in blocks[known:]:
            fetched = order[len(parts)] if len(parts) < tensor_devices else None
            sums, *more = partial(
                block,
                order[known],
                parts[known],
                sums,
                expert_gate_weight,
                expert_up_weight,
                fetched,
                () if known else (expert_down_weight,),
            )
            parts += more
            known += 1
        blocks = blocks + [tie(block, sums) if distance > 1 else block for block in others]
    steps = bits(tensor_devices)
    groups = [tuple(k for k in range(tensor_devices) if k & -k == step) for step in steps] + [(0,)]
    sent, active = experts(
        expert_devices // EXPERT_COUNT,
        groups[0],
        tuple(order),
        sums,
        known,
        blocks,
        parts[known:],
        expert_up_weight,
        expert_down_weight,
        adapter_up_map,
    )
    received = {k: [] for k in range(tensor_devices)}
    for step, group, following in zip(steps, groups[:-1], groups[1:], strict=True):
        arriving = swap(sent, "tp", step)
        made = down(following, active, expert_down_weight, features, sent)
        for i, k in enumerate(group):
            received[k ^ step].append(arriving[i])
        kept = [
            sum((block.astype(F32) for block in received[k]), made[i])
            for i, k in enumerate(following)
        ]
        if following != (0,):
            sent = jnp.stack([block.astype(BF16) for block in kept])
    kept = kept[0].reshape(expert_devices, rows, features)
    for distance in bits(expert_devices):
        kept, sent = kept[0::2], kept[1::2].astype(BF16)
        kept = kept + swap(sent, "ep", distance).astype(F32)
    return (state.astype(F32) + kept[0]).astype(BF16)


def solution(mesh):
    placed = (
        P(("groups", "ep"), "tp"),
        P(("groups", "ep"), "tp"),
        P(("groups", "ep"), "tp"),
        P(("groups", "ep"), "tp"),
        P(("groups", "ep"), None, "tp"),
        P(("groups", "ep"), None, "tp"),
        P(("groups", "ep")),
        P("tp"),
        P("tp", None),
        P(None, ("ep", "tp")),
        P(None, ("ep", "tp")),
        P(("ep", "tp"), None),
        P("tp", None),
        P(None, ("ep", "tp")),
        P(("groups", "ep"), None),
        P(("groups", "ep")),
    )
    return jax.shard_map(
        per_device, mesh=mesh, in_specs=placed, out_specs=P(("groups", "ep"), "tp"), check_vma=False
    )
```

```python
import functools

import jax
import jax.numpy as jnp
from jax import lax
from jax.experimental import pallas as pl
from jax.experimental.pallas import tpu as pltpu
from jax.sharding import PartitionSpec as P

HEADS = 24
KVH = 8
HD = 128
EXPERT_COUNT = 4
ADAPTER_RANK = 16
TENANT_COUNT = 8
LANES = 128
ADAPTER_LANES = EXPERT_COUNT * ADAPTER_RANK
DIFF_HI, DIFF_LO, SQ_HI, SQ_LO, FIRST, SECOND, TENANT = range(ADAPTER_LANES, ADAPTER_LANES + 7)
F32 = jnp.float32
BF16 = jnp.bfloat16
ANY_LANES = (((1,), (1,)), ((), ()))


VMEM = pl.BlockSpec(memory_space=pltpu.VMEM)
HBM = pl.BlockSpec(memory_space=pl.ANY)


def in_hbm(*arrays):
    return [pltpu.with_memory_space_constraint(array, pltpu.HBM) for array in arrays]


def column(values, rows):
    index = lax.broadcasted_iota(jnp.int32, (rows, LANES), 0)
    out = jnp.zeros((rows, LANES), jnp.int32)
    for r in range(rows):
        out = jnp.where(index == r, values(r), out)
    return out


def at_distance(distance, size):
    return pl.ds(pl.multiple_of((lax.axis_index("tp") ^ distance) * size, size), size)


def fetch(gate_weight, distance, part, arrived):
    copy = pltpu.make_async_copy(
        gate_weight.at[at_distance(distance, part.shape[0]), :], part, arrived
    )
    copy.start()
    return copy


def attend_kernel(*refs):
    count = 12
    sources, gate_weight, outs, part = refs[:count], refs[count], refs[count + 1 : count + 3], refs[count + 3]
    buffers, arrived, part_arrived = refs[count + 4 : -2], refs[-2], refs[-1]
    copies = [
        pltpu.make_async_copy(source, buffer, arrived.at[i])
        for i, (source, buffer) in enumerate(zip(sources, buffers, strict=True))
    ]
    for i in (7, 4, 0, 5, 8, 6, 3, 9, 1, 2, 10, 11):
        copies[i].start()
    fetched = fetch(gate_weight, 0, part, part_arrived)
    attend_body(*buffers, *outs, wait=lambda *which: [copies[i].wait() for i in which])
    fetched.wait()


def attend_body(
    lengths,
    tenants,
    routes,
    residual,
    queries,
    token_keys,
    token_values,
    stored_keys,
    stored_values,
    gain,
    router,
    adapter_down,
    state_out,
    payload_out,
    *,
    wait,
):
    rows, features = residual.shape
    kv_local = token_keys.shape[1] // HD
    cache = stored_keys.shape[1]
    group = HEADS // KVH
    scale = HD ** (-0.5)
    wait(0, 4, 7)
    heads = kv_local * group
    together = 2 if rows % 2 == 0 else 1
    length_column = column(lambda r: lengths[r], rows)
    stacked_length = jnp.concatenate([length_column[:, :1]] * heads, axis=0)
    stacked_row = lax.rem(
        lax.broadcasted_iota(jnp.int32, (heads * rows, cache), 0), jnp.int32(rows)
    )
    visible = lax.broadcasted_iota(jnp.int32, (heads * rows, cache), 1) < stacked_length

    def stacked(get):
        return jnp.concatenate([get(g, j) for g in range(kv_local) for j in range(group)], axis=0)

    def head_lanes(g, j=None):
        h = g if j is None else g * group + j
        return slice(h * HD, (h + 1) * HD)

    query = stacked(lambda g, j: queries[:, head_lanes(g, j)])
    wide = jnp.concatenate([query] * kv_local, axis=1)
    lane_head = lax.broadcasted_iota(jnp.int32, wide.shape, 1) // HD
    row_head = lax.broadcasted_iota(jnp.int32, wide.shape, 0) // (group * rows)
    wide = jnp.where(lane_head == row_head, wide.astype(F32), 0.0).astype(BF16)
    scores = jnp.zeros((heads * rows, cache), F32)
    for r in range(0, rows, together):
        keys = stored_keys[r : r + together].reshape(together * cache, kv_local * HD)
        every = lax.dot_general(wide, keys, ANY_LANES, preferred_element_type=F32)
        for i in range(together):
            scores = jnp.where(
                stacked_row == r + i, every[:, i * cache : (i + 1) * cache], scores
            )
    scores = jnp.where(visible, scores * scale, -jnp.inf)
    wait(5)
    fresh_key = stacked(lambda g, j: token_keys[:, head_lanes(g)].astype(F32))
    fresh = jnp.sum(query.astype(F32) * fresh_key, axis=1, keepdims=True) * scale
    largest = jnp.maximum(jnp.max(scores, axis=1, keepdims=True), fresh)
    cache_exp = jnp.exp(scores - largest)
    fresh_exp = jnp.exp(fresh - largest)
    denominator = jnp.sum(cache_exp, axis=1, keepdims=True) + fresh_exp
    probs = cache_exp / denominator
    fresh_prob = (fresh_exp / denominator).astype(BF16).astype(F32)
    wait(8)
    every = jnp.zeros((heads * rows, kv_local * HD), F32)
    for r in range(0, rows, together):
        values = stored_values[r : r + together].reshape(together * cache, kv_local * HD)
        own = [jnp.where(stacked_row == r + i, probs, 0.0).astype(BF16) for i in range(together)]
        every = every + jnp.dot(
            jnp.concatenate(own, axis=1), values, preferred_element_type=F32
        )
    wait(3, 6, 9)
    squares = jnp.zeros((rows, 1), F32)
    for g in range(kv_local):
        fresh_value = token_values[:, head_lanes(g)].astype(F32)
        for j in range(group):
            lanes = head_lanes(g, j)
            place = slice((g * group + j) * rows, (g * group + j + 1) * rows)
            attended = every[place, head_lanes(g)] + fresh_prob[place] * fresh_value
            state = (residual[:, lanes].astype(F32) + attended).astype(BF16)
            state_out[:, lanes] = state
            state = state.astype(F32)
            squares = squares + jnp.sum(state * state, axis=1, keepdims=True)
            payload_out[:, lanes] = (
                state * gain[lanes.start // LANES : lanes.start // LANES + 1, :]
            ).astype(BF16)
    wait(1, 2, 10, 11)
    scaled = payload_out[:, :features]
    logits = lax.dot_general(scaled, router[...], ANY_LANES, preferred_element_type=F32)
    first = column(lambda r: routes[0, r], rows)
    second = column(lambda r: routes[1, r], rows)
    tenant = column(lambda r: tenants[r], rows)
    expert = lax.broadcasted_iota(jnp.int32, logits.shape, 1)
    chosen = jnp.where(expert == first[:, :EXPERT_COUNT], logits, 0.0) - jnp.where(
        expert == second[:, :EXPERT_COUNT], logits, 0.0
    )
    diff = jnp.sum(chosen, axis=1, keepdims=True)
    adapter = jnp.dot(scaled, adapter_down[...], preferred_element_type=F32)
    lane = lax.broadcasted_iota(jnp.int32, (rows, LANES), 1)
    tail = jnp.zeros((rows, LANES), F32)
    for start in range(0, adapter.shape[1], LANES):
        owner = (lane + start) // ADAPTER_LANES
        tail = tail + jnp.where(owner == tenant, adapter[:, start : start + LANES], 0.0)
    tail = tail + pltpu.roll(tail, ADAPTER_LANES, 1)
    diff_hi = diff.astype(BF16).astype(F32)
    squares_hi = squares.astype(BF16).astype(F32)
    for place, value in (
        (DIFF_HI, diff_hi),
        (DIFF_LO, diff - diff_hi),
        (SQ_HI, squares_hi),
        (SQ_LO, squares - squares_hi),
        (FIRST, first.astype(F32)),
        (SECOND, second.astype(F32)),
        (TENANT, tenant.astype(F32)),
    ):
        tail = jnp.where(lane == place, value, tail)
    payload_out[:, features:] = tail.astype(BF16)


def attend(args, gate_weight):
    rows, features = args[3].shape
    return pl.pallas_call(
        attend_kernel,
        out_shape=(
            jax.ShapeDtypeStruct((rows, features), BF16),
            jax.ShapeDtypeStruct((rows, features + LANES), BF16),
            jax.ShapeDtypeStruct((features, gate_weight.shape[1]), BF16),
        ),
        in_specs=[HBM] * (len(args) + 1),
        out_specs=(VMEM,) * 3,
        scratch_shapes=[
            (pltpu.SMEM if i < 3 else pltpu.VMEM)(arg.shape, arg.dtype)
            for i, arg in enumerate(args)
        ]
        + [pltpu.SemaphoreType.DMA((len(args),)), pltpu.SemaphoreType.DMA],
        compiler_params=pltpu.CompilerParams(vmem_limit_bytes=6 * 2**20),
        cost_estimate=pl.CostEstimate(
            flops=200_000_000, bytes_accessed=6_000_000, transcendentals=20_000
        ),
        name="attend",
    )(*in_hbm(*args, gate_weight))


def load_kernel(distance, gate_weight, after, part, arrived):
    fetch(gate_weight, distance, part, arrived).wait()


def load(gate_weight, distance, features, after):
    hidden = gate_weight.shape[1]
    return pl.pallas_call(
        functools.partial(load_kernel, distance),
        out_shape=jax.ShapeDtypeStruct((features, hidden), BF16),
        in_specs=[HBM] * 2,
        out_specs=VMEM,
        scratch_shapes=[pltpu.SemaphoreType.DMA],
        compiler_params=pltpu.CompilerParams(vmem_limit_bytes=2**20),
        cost_estimate=pl.CostEstimate(
            flops=0, bytes_accessed=2 * features * hidden, transcendentals=0
        ),
        name="load",
    )(*in_hbm(gate_weight), after)


def halves(hidden):
    return hidden // 2 if hidden % (2 * LANES) == 0 else hidden


def partial_kernel(distance, fetched, first, soon, block, gate_part, up_weight, *refs):
    features, hidden = gate_part.shape
    sums, refs = (None, refs) if first else (refs[0], refs[1:])
    gate_weight, totals = refs[0], refs[1 + soon]
    copy = None if fetched is None else fetch(gate_weight, fetched, refs[2 + soon], refs[-1])
    tile = halves(hidden)
    depth = at_distance(distance, features)

    def products(n, carry):
        lanes = pl.ds(pl.multiple_of(n * tile, tile), tile)
        for i, part in enumerate((gate_part[:, lanes], up_weight[depth, lanes])):
            product = jnp.dot(block[:, :features], part, preferred_element_type=F32)
            totals[i, :, lanes] = product if first else sums[i, :, lanes] + product
        return carry

    lax.fori_loop(0, hidden // tile, products, 0)
    if copy is not None:
        copy.wait()


def partial(block, distance, part, sums, gate_weight, up_weight, fetched, soon):
    rows, width = block.shape
    features = width - LANES
    hidden = gate_weight.shape[1]
    first = sums is None
    more = int(fetched is not None)
    return pl.pallas_call(
        functools.partial(partial_kernel, distance, fetched, first, len(soon)),
        out_shape=(
            jax.ShapeDtypeStruct((2, rows, hidden), F32),
            *[jax.ShapeDtypeStruct((features, hidden), BF16)] * more,
        ),
        in_specs=[VMEM] * (3 if first else 4) + [HBM] * (1 + len(soon)),
        out_specs=(VMEM,) * (1 + more),
        scratch_shapes=[pltpu.SemaphoreType.DMA],
        compiler_params=pltpu.CompilerParams(vmem_limit_bytes=3 * 2**20),
        cost_estimate=pl.CostEstimate(
            flops=4 * rows * features * hidden,
            bytes_accessed=2 * features * hidden,
            transcendentals=0,
        ),
        name="partial",
    )(block, part, up_weight, *(() if first else (sums,)), *in_hbm(gate_weight), *soon)


def expert_kernel(replicas, targets, order, known, sums, *refs):
    tensor_devices = len(order)
    blocks, parts = refs[:tensor_devices], refs[tensor_devices : 2 * tensor_devices - known]
    up_weight, down_weight, adapter_up, out, active = refs[2 * tensor_devices - known :]
    rows, width = blocks[0].shape
    features = width - LANES
    hidden = active.shape[1]
    expert = lax.axis_index("ep") // replicas
    tail = jnp.zeros((rows, LANES), F32)
    for block in blocks:
        tail = tail + block[:, features:].astype(F32)
    place = lambda k: tail[:, k : k + 1]
    here = blocks[0][:, features:].astype(F32)
    inverse_rms = lax.rsqrt(
        (place(SQ_HI) + place(SQ_LO)) / (features * tensor_devices) + 1e-05
    )
    diff = (place(DIFF_HI) + place(DIFF_LO)) * inverse_rms
    expert_float = expert.astype(F32)
    is_first = here[:, FIRST : FIRST + 1] == expert_float
    is_second = here[:, SECOND : SECOND + 1] == expert_float
    weight = jnp.where(
        is_first, jax.nn.sigmoid(diff), jnp.where(is_second, jax.nn.sigmoid(-diff), 0.0)
    )
    lowrank = (tail * inverse_rms).astype(BF16)
    spread_shape = (LANES, TENANT_COUNT * ADAPTER_RANK)
    source = lax.broadcasted_iota(jnp.int32, spread_shape, 0)
    target = lax.broadcasted_iota(jnp.int32, spread_shape, 1)
    spread = jnp.where(
        source == expert * ADAPTER_RANK + lax.rem(target, jnp.int32(ADAPTER_RANK)), 1.0, 0.0
    ).astype(BF16)
    lane = lax.broadcasted_iota(jnp.int32, (rows, TENANT_COUNT * ADAPTER_RANK), 1)
    own_tenant = (lane // ADAPTER_RANK).astype(F32) == here[:, TENANT : TENANT + 1]
    adapter_rows = jnp.where(
        own_tenant, jnp.dot(lowrank, spread, preferred_element_type=F32), 0.0
    ).astype(BF16)
    tile = halves(hidden)
    for start in range(0, hidden, tile):
        lanes = slice(start, start + tile)
        gate, up = sums[0, :, lanes], sums[1, :, lanes]
        for block, part, distance in zip(blocks[known:], parts, order[known:], strict=True):
            scaled = block[:, :features]
            gate = gate + jnp.dot(scaled, part[:, lanes], preferred_element_type=F32)
            up = up + jnp.dot(
                scaled,
                up_weight[at_distance(distance, features), lanes],
                preferred_element_type=F32,
            )
        gate = gate * inverse_rms
        up = up * inverse_rms + jnp.dot(
            adapter_rows, adapter_up[:, lanes], preferred_element_type=F32
        )
        active[:, lanes] = (gate * jax.nn.sigmoid(gate) * up * weight).astype(BF16)
    down_products(targets, active, down_weight, out)


def down_products(targets, active, down_weight, out):
    for i, distance in enumerate(targets):
        lanes = at_distance(distance, out.shape[2])
        out[i] = jnp.dot(
            active[...], down_weight[:, lanes], preferred_element_type=F32
        ).astype(out.dtype)


def experts(replicas, targets, order, sums, known, blocks, parts, up_weight, down_weight, adapter_up):
    rows, width = blocks[0].shape
    features, hidden = width - LANES, sums.shape[2]
    return pl.pallas_call(
        functools.partial(expert_kernel, replicas, targets, order, known),
        out_shape=(
            jax.ShapeDtypeStruct((len(targets), rows, features), BF16),
            jax.ShapeDtypeStruct((rows, hidden), BF16),
        ),
        in_specs=[VMEM] * (4 + len(blocks) + len(parts)),
        out_specs=(VMEM, VMEM),
        compiler_params=pltpu.CompilerParams(vmem_limit_bytes=4 * 2**20),
        cost_estimate=pl.CostEstimate(
            flops=2 * rows * hidden * features * (2 * len(parts) + len(targets)),
            bytes_accessed=0,
            transcendentals=0,
        ),
        name="experts",
    )(sums, *blocks, *parts, up_weight, down_weight, adapter_up)


def down_kernel(targets, active, down_weight, after, out):
    down_products(targets, active, down_weight, out)


def down(targets, active, down_weight, features, after):
    rows, hidden = active.shape
    return pl.pallas_call(
        functools.partial(down_kernel, targets),
        out_shape=jax.ShapeDtypeStruct((len(targets), rows, features), F32),
        in_specs=[VMEM, VMEM, HBM],
        out_specs=VMEM,
        compiler_params=pltpu.CompilerParams(vmem_limit_bytes=4 * 2**20),
        cost_estimate=pl.CostEstimate(
            flops=2 * rows * hidden * features * len(targets),
            bytes_accessed=0,
            transcendentals=0,
        ),
        name="down",
    )(active, down_weight, after)


def join_kernel(first, second, *refs):
    out = refs[-1]
    count = first.shape[0]
    out[:count] = first[...]
    out[count:] = second[...]


def join(first, second, *after):
    return pl.pallas_call(
        join_kernel,
        out_shape=jax.ShapeDtypeStruct((2 * first.shape[0], *first.shape[1:]), first.dtype),
        in_specs=[VMEM, VMEM] + [HBM] * len(after),
        out_specs=VMEM,
        compiler_params=pltpu.CompilerParams(vmem_limit_bytes=1 * 2**20),
        name="join",
    )(first, second, *after)


def tie_kernel(array, after, out):
    pass


def tie(array, after):
    return pl.pallas_call(
        tie_kernel,
        out_shape=jax.ShapeDtypeStruct(array.shape, array.dtype),
        in_specs=[HBM, HBM],
        out_specs=HBM,
        input_output_aliases={0: 0},
        compiler_params=pltpu.CompilerParams(vmem_limit_bytes=2**20),
        name="tie",
    )(array, after)


def swap(x, axis, distance):
    count = lax.axis_size(axis)
    return lax.ppermute(x, axis, [(i, i ^ distance) for i in range(count)])


def bits(count):
    return [1 << b for b in range(count.bit_length() - 1)]


def per_device(
    residual,
    queries,
    token_keys,
    token_values,
    stored_keys,
    stored_values,
    lengths,
    norm_gain_vector,
    router,
    expert_gate_weight,
    expert_up_weight,
    expert_down_weight,
    adapter_down_map,
    adapter_up_map,
    routes,
    tenants,
):
    rows, features = residual.shape
    expert_devices = lax.axis_size("ep")
    tensor_devices = lax.axis_size("tp")
    state, held, *parts = attend(
        (
            lengths,
            tenants,
            routes.T,
            residual,
            queries,
            token_keys,
            token_values,
            stored_keys,
            stored_values,
            norm_gain_vector.reshape(features // LANES, LANES),
            router.T,
            adapter_down_map,
        ),
        expert_gate_weight,
    )
    order = [0]
    for distance in reversed(bits(tensor_devices)):
        order += [at ^ distance for at in order]
    for distance in bits(expert_devices):
        other = swap(held, "ep", distance)
        if len(parts) < tensor_devices:
            parts.append(load(expert_gate_weight, order[len(parts)], features, held))
        last = 2 * distance == expert_devices
        held = join(held, other, parts[-1], *((expert_up_weight,) if last else ()))
    blocks, known, sums = [held], 0, None
    for distance in reversed(bits(tensor_devices)):
        others = [swap(block, "tp", distance) for block in blocks]
        for block in blocks[known:]:
            fetched = order[len(parts)] if len(parts) < tensor_devices else None
            sums, *more = partial(
                block,
                order[known],
                parts[known],
                sums,
                expert_gate_weight,
                expert_up_weight,
                fetched,
                (adapter_up_map, expert_down_weight) if not known else (),
            )
            parts += more
            known += 1
        blocks = blocks + [tie(block, sums) if distance > 1 else block for block in others]
    steps = bits(tensor_devices)
    groups = [tuple(k for k in range(tensor_devices) if k & -k == step) for step in steps] + [(0,)]
    sent, active = experts(
        expert_devices // EXPERT_COUNT,
        groups[0],
        tuple(order),
        sums,
        known,
        blocks,
        parts[known:],
        expert_up_weight,
        expert_down_weight,
        adapter_up_map,
    )
    received = {k: [] for k in range(tensor_devices)}
    for step, group, following in zip(steps, groups[:-1], groups[1:], strict=True):
        arriving = swap(sent, "tp", step)
        made = down(following, active, expert_down_weight, features, sent)
        for i, k in enumerate(group):
            received[k ^ step].append(arriving[i])
        kept = [
            sum((block.astype(F32) for block in received[k]), made[i])
            for i, k in enumerate(following)
        ]
        if following != (0,):
            sent = jnp.stack([block.astype(BF16) for block in kept])
    kept = kept[0].reshape(expert_devices, rows, features)
    for distance in bits(expert_devices):
        kept, sent = kept[0::2], kept[1::2].astype(BF16)
        kept = kept + swap(sent, "ep", distance).astype(F32)
    return (state.astype(F32) + kept[0]).astype(BF16)


def solution(mesh):
    placed = (
        P(("groups", "ep"), "tp"),
        P(("groups", "ep"), "tp"),
        P(("groups", "ep"), "tp"),
        P(("groups", "ep"), "tp"),
        P(("groups", "ep"), None, "tp"),
        P(("groups", "ep"), None, "tp"),
        P(("groups", "ep")),
        P("tp"),
        P("tp", None),
        P(None, ("ep", "tp")),
        P(None, ("ep", "tp")),
        P(("ep", "tp"), None),
        P("tp", None),
        P(None, ("ep", "tp")),
        P(("groups", "ep"), None),
        P(("groups", "ep")),
    )
    return jax.shard_map(
        per_device, mesh=mesh, in_specs=placed, out_specs=P(("groups", "ep"), "tp"), check_vma=False
    )
```

```python
import functools

import jax
import jax.numpy as jnp
from jax import lax
from jax.experimental import pallas as pl
from jax.experimental.pallas import tpu as pltpu
from jax.sharding import PartitionSpec as P

HEADS = 24
KVH = 8
HD = 128
EXPERT_COUNT = 4
ADAPTER_RANK = 16
TENANT_COUNT = 8
LANES = 128
ADAPTER_LANES = EXPERT_COUNT * ADAPTER_RANK
DIFF_HI, DIFF_LO, SQ_HI, SQ_LO, FIRST, SECOND, TENANT = range(ADAPTER_LANES, ADAPTER_LANES + 7)
F32 = jnp.float32
BF16 = jnp.bfloat16
ANY_LANES = (((1,), (1,)), ((), ()))


VMEM = pl.BlockSpec(memory_space=pltpu.VMEM)
HBM = pl.BlockSpec(memory_space=pl.ANY)


def in_hbm(*arrays):
    return [pltpu.with_memory_space_constraint(array, pltpu.HBM) for array in arrays]


def column(values, rows):
    index = lax.broadcasted_iota(jnp.int32, (rows, LANES), 0)
    out = jnp.zeros((rows, LANES), jnp.int32)
    for r in range(rows):
        out = jnp.where(index == r, values(r), out)
    return out


def at_distance(distance, size):
    return pl.ds(pl.multiple_of((lax.axis_index("tp") ^ distance) * size, size), size)


def attend_kernel(*refs):
    count = 12
    sources, outs, buffers, arrived = refs[:count], refs[count : count + 2], refs[count + 2 : -1], refs[-1]
    copies = [
        pltpu.make_async_copy(source, buffer, arrived.at[i])
        for i, (source, buffer) in enumerate(zip(sources, buffers, strict=True))
    ]
    for i in (7, 4, 0, 5, 8, 6, 3, 9, 1, 2, 10, 11):
        copies[i].start()
    attend_body(*buffers, *outs, wait=lambda *which: [copies[i].wait() for i in which])


def attend_body(
    lengths,
    tenants,
    routes,
    residual,
    queries,
    token_keys,
    token_values,
    stored_keys,
    stored_values,
    gain,
    router,
    adapter_down,
    state_out,
    payload_out,
    *,
    wait,
):
    rows, features = residual.shape
    kv_local = token_keys.shape[1] // HD
    cache = stored_keys.shape[1]
    group = HEADS // KVH
    scale = HD ** (-0.5)
    wait(0, 4, 7)
    heads = kv_local * group
    together = 2 if rows % 2 == 0 else 1
    length_column = column(lambda r: lengths[r], rows)
    stacked_length = jnp.concatenate([length_column[:, :1]] * heads, axis=0)
    stacked_row = lax.rem(
        lax.broadcasted_iota(jnp.int32, (heads * rows, cache), 0), jnp.int32(rows)
    )
    visible = lax.broadcasted_iota(jnp.int32, (heads * rows, cache), 1) < stacked_length

    def stacked(get):
        return jnp.concatenate([get(g, j) for g in range(kv_local) for j in range(group)], axis=0)

    def head_lanes(g, j=None):
        h = g if j is None else g * group + j
        return slice(h * HD, (h + 1) * HD)

    query = stacked(lambda g, j: queries[:, head_lanes(g, j)])
    wide = jnp.concatenate([query] * kv_local, axis=1)
    lane_head = lax.broadcasted_iota(jnp.int32, wide.shape, 1) // HD
    row_head = lax.broadcasted_iota(jnp.int32, wide.shape, 0) // (group * rows)
    wide = jnp.where(lane_head == row_head, wide.astype(F32), 0.0).astype(BF16)
    scores = jnp.zeros((heads * rows, cache), F32)
    for r in range(0, rows, together):
        keys = stored_keys[r : r + together].reshape(together * cache, kv_local * HD)
        every = lax.dot_general(wide, keys, ANY_LANES, preferred_element_type=F32)
        for i in range(together):
            scores = jnp.where(
                stacked_row == r + i, every[:, i * cache : (i + 1) * cache], scores
            )
    scores = jnp.where(visible, scores * scale, -jnp.inf)
    wait(5)
    fresh_key = stacked(lambda g, j: token_keys[:, head_lanes(g)].astype(F32))
    fresh = jnp.sum(query.astype(F32) * fresh_key, axis=1, keepdims=True) * scale
    largest = jnp.maximum(jnp.max(scores, axis=1, keepdims=True), fresh)
    cache_exp = jnp.exp(scores - largest)
    fresh_exp = jnp.exp(fresh - largest)
    denominator = jnp.sum(cache_exp, axis=1, keepdims=True) + fresh_exp
    probs = cache_exp / denominator
    fresh_prob = (fresh_exp / denominator).astype(BF16).astype(F32)
    wait(8)
    every = jnp.zeros((heads * rows, kv_local * HD), F32)
    for r in range(0, rows, together):
        values = stored_values[r : r + together].reshape(together * cache, kv_local * HD)
        own = [jnp.where(stacked_row == r + i, probs, 0.0).astype(BF16) for i in range(together)]
        every = every + jnp.dot(
            jnp.concatenate(own, axis=1), values, preferred_element_type=F32
        )
    wait(3, 6, 9)
    squares = jnp.zeros((rows, 1), F32)
    for g in range(kv_local):
        fresh_value = token_values[:, head_lanes(g)].astype(F32)
        for j in range(group):
            lanes = head_lanes(g, j)
            place = slice((g * group + j) * rows, (g * group + j + 1) * rows)
            attended = every[place, head_lanes(g)] + fresh_prob[place] * fresh_value
            state = (residual[:, lanes].astype(F32) + attended).astype(BF16)
            state_out[:, lanes] = state
            state = state.astype(F32)
            squares = squares + jnp.sum(state * state, axis=1, keepdims=True)
            payload_out[:, lanes] = (
                state * gain[lanes.start // LANES : lanes.start // LANES + 1, :]
            ).astype(BF16)
    wait(1, 2, 10, 11)
    scaled = payload_out[:, :features]
    logits = lax.dot_general(scaled, router[...], ANY_LANES, preferred_element_type=F32)
    first = column(lambda r: routes[0, r], rows)
    second = column(lambda r: routes[1, r], rows)
    tenant = column(lambda r: tenants[r], rows)
    expert = lax.broadcasted_iota(jnp.int32, logits.shape, 1)
    chosen = jnp.where(expert == first[:, :EXPERT_COUNT], logits, 0.0) - jnp.where(
        expert == second[:, :EXPERT_COUNT], logits, 0.0
    )
    diff = jnp.sum(chosen, axis=1, keepdims=True)
    adapter = jnp.dot(scaled, adapter_down[...], preferred_element_type=F32)
    lane = lax.broadcasted_iota(jnp.int32, (rows, LANES), 1)
    tail = jnp.zeros((rows, LANES), F32)
    for start in range(0, adapter.shape[1], LANES):
        owner = (lane + start) // ADAPTER_LANES
        tail = tail + jnp.where(owner == tenant, adapter[:, start : start + LANES], 0.0)
    tail = tail + pltpu.roll(tail, ADAPTER_LANES, 1)
    diff_hi = diff.astype(BF16).astype(F32)
    squares_hi = squares.astype(BF16).astype(F32)
    for place, value in (
        (DIFF_HI, diff_hi),
        (DIFF_LO, diff - diff_hi),
        (SQ_HI, squares_hi),
        (SQ_LO, squares - squares_hi),
        (FIRST, first.astype(F32)),
        (SECOND, second.astype(F32)),
        (TENANT, tenant.astype(F32)),
    ):
        tail = jnp.where(lane == place, value, tail)
    payload_out[:, features:] = tail.astype(BF16)


def attend(args):
    rows, features = args[3].shape
    return pl.pallas_call(
        attend_kernel,
        out_shape=(
            jax.ShapeDtypeStruct((rows, features), BF16),
            jax.ShapeDtypeStruct((rows, features + LANES), BF16),
        ),
        in_specs=[HBM] * len(args),
        out_specs=(VMEM,) * 2,
        scratch_shapes=[
            (pltpu.SMEM if i < 3 else pltpu.VMEM)(arg.shape, arg.dtype)
            for i, arg in enumerate(args)
        ]
        + [pltpu.SemaphoreType.DMA((len(args),))],
        compiler_params=pltpu.CompilerParams(vmem_limit_bytes=6 * 2**20),
        cost_estimate=pl.CostEstimate(
            flops=200_000_000, bytes_accessed=3_000_000, transcendentals=20_000
        ),
        name="attend",
    )(*in_hbm(*args))


def fetch(down_weight, distances, parts, arrived):
    copies = [
        pltpu.make_async_copy(
            down_weight.at[:, at_distance(distance, part.shape[1])], part, arrived.at[i]
        )
        for i, (distance, part) in enumerate(zip(distances, parts, strict=True))
    ]
    for copy in copies:
        copy.start()
    return copies


def halves(hidden):
    return hidden // 2 if hidden % (2 * LANES) == 0 else hidden


def partial_kernel(distance, fetched, first, soon, block, gate_weight, up_weight, *refs):
    hidden = gate_weight.shape[1]
    features = block.shape[1] - LANES
    sums, refs = (None, refs) if first else (refs[0], refs[1:])
    down_weight, totals = refs[0], refs[1 + soon]
    copies = fetch(down_weight, fetched, refs[2 + soon : -1], refs[-1])
    tile = halves(hidden)
    depth = at_distance(distance, features)

    def products(n, carry):
        lanes = pl.ds(pl.multiple_of(n * tile, tile), tile)
        for i, weight in enumerate((gate_weight, up_weight)):
            product = jnp.dot(
                block[:, :features], weight[depth, lanes], preferred_element_type=F32
            )
            totals[i, :, lanes] = product if first else sums[i, :, lanes] + product
        return carry

    lax.fori_loop(0, hidden // tile, products, 0)
    for copy in copies:
        copy.wait()


def partial(block, distance, sums, gate_weight, up_weight, down_weight, fetched, soon):
    rows, width = block.shape
    features = width - LANES
    hidden = gate_weight.shape[1]
    first = sums is None
    return pl.pallas_call(
        functools.partial(partial_kernel, distance, fetched, first, len(soon)),
        out_shape=(
            jax.ShapeDtypeStruct((2, rows, hidden), F32),
            *[jax.ShapeDtypeStruct((hidden, features), BF16)] * len(fetched),
        ),
        in_specs=[VMEM] * (3 if first else 4) + [HBM] * (1 + len(soon)),
        out_specs=(VMEM,) * (1 + len(fetched)),
        scratch_shapes=[pltpu.SemaphoreType.DMA((max(1, len(fetched)),))],
        compiler_params=pltpu.CompilerParams(vmem_limit_bytes=3 * 2**20),
        cost_estimate=pl.CostEstimate(
            flops=4 * rows * features * hidden,
            bytes_accessed=2 * features * hidden,
            transcendentals=0,
        ),
        name="partial",
    )(block, gate_weight, up_weight, *(() if first else (sums,)), *in_hbm(down_weight), *soon)


def expert_kernel(replicas, late, following, order, known, early, sums, *refs):
    tensor_devices = len(order)
    blocks, refs = refs[:tensor_devices], refs[tensor_devices:]
    gate_weight, up_weight, adapter_up, refs = *refs[:3], refs[3:]
    early_parts, refs = refs[:early], refs[early:]
    down_weight, out, active, refs = *refs[:3], refs[3:]
    next_parts, late_parts, arrived = refs[: len(following)], refs[len(following) : -1], refs[-1]
    rows, width = blocks[0].shape
    features = width - LANES
    hidden = active.shape[1]
    copies = fetch(down_weight, late + following, (*late_parts, *next_parts), arrived)
    tile = halves(hidden)

    @pl.when(lax.axis_index("tp") >= 0)
    def _():
        expert = lax.axis_index("ep") // replicas
        tail = jnp.zeros((rows, LANES), F32)
        for block in blocks:
            tail = tail + block[:, features:].astype(F32)
        place = lambda k: tail[:, k : k + 1]
        here = blocks[0][:, features:].astype(F32)
        inverse_rms = lax.rsqrt(
            (place(SQ_HI) + place(SQ_LO)) / (features * tensor_devices) + 1e-05
        )
        diff = (place(DIFF_HI) + place(DIFF_LO)) * inverse_rms
        expert_float = expert.astype(F32)
        is_first = here[:, FIRST : FIRST + 1] == expert_float
        is_second = here[:, SECOND : SECOND + 1] == expert_float
        weight = jnp.where(
            is_first, jax.nn.sigmoid(diff), jnp.where(is_second, jax.nn.sigmoid(-diff), 0.0)
        )
        lowrank = (tail * inverse_rms).astype(BF16)
        spread_shape = (LANES, TENANT_COUNT * ADAPTER_RANK)
        source = lax.broadcasted_iota(jnp.int32, spread_shape, 0)
        target = lax.broadcasted_iota(jnp.int32, spread_shape, 1)
        spread = jnp.where(
            source == expert * ADAPTER_RANK + lax.rem(target, jnp.int32(ADAPTER_RANK)), 1.0, 0.0
        ).astype(BF16)
        lane = lax.broadcasted_iota(jnp.int32, (rows, TENANT_COUNT * ADAPTER_RANK), 1)
        own_tenant = (lane // ADAPTER_RANK).astype(F32) == here[:, TENANT : TENANT + 1]
        adapter_rows = jnp.where(
            own_tenant, jnp.dot(lowrank, spread, preferred_element_type=F32), 0.0
        ).astype(BF16)
        for start in range(0, hidden, tile):
            lanes = slice(start, start + tile)
            gate, up = sums[0, :, lanes], sums[1, :, lanes]
            for block, distance in zip(blocks[known:], order[known:], strict=True):
                scaled = block[:, :features]
                depth = at_distance(distance, features)
                gate = gate + jnp.dot(
                    scaled, gate_weight[depth, lanes], preferred_element_type=F32
                )
                up = up + jnp.dot(scaled, up_weight[depth, lanes], preferred_element_type=F32)
            gate = gate * inverse_rms
            up = up * inverse_rms + jnp.dot(
                adapter_rows, adapter_up[:, lanes], preferred_element_type=F32
            )
            active[:, lanes] = (gate * jax.nn.sigmoid(gate) * up * weight).astype(BF16)
        for i, part in enumerate((*early_parts, *late_parts)):
            if i >= early:
                copies[i - early].wait()
            out[i] = jnp.dot(active[...], part[...], preferred_element_type=F32).astype(out.dtype)

    for copy in copies[len(late) :]:
        copy.wait()


def experts(
    replicas, late, following, order, sums, known, blocks, gate_weight, up_weight, adapter_up, parts, down_weight
):
    rows, width = blocks[0].shape
    features, hidden = width - LANES, sums.shape[2]
    count = len(parts) + len(late)
    columns = (hidden, features)
    return pl.pallas_call(
        functools.partial(expert_kernel, replicas, late, following, order, known, len(parts)),
        out_shape=(
            jax.ShapeDtypeStruct((count, rows, features), BF16),
            jax.ShapeDtypeStruct((rows, hidden), BF16),
            *[jax.ShapeDtypeStruct(columns, BF16)] * len(following),
        ),
        in_specs=[VMEM] * (4 + len(blocks) + len(parts)) + [HBM],
        out_specs=(VMEM,) * (2 + len(following)),
        scratch_shapes=[pltpu.VMEM(columns, BF16)] * len(late)
        + [pltpu.SemaphoreType.DMA((len(late) + len(following),))],
        compiler_params=pltpu.CompilerParams(vmem_limit_bytes=5 * 2**20),
        cost_estimate=pl.CostEstimate(
            flops=2 * rows * hidden * features * (2 * (len(blocks) - known) + count),
            bytes_accessed=2 * hidden * features * (len(late) + len(following)),
            transcendentals=0,
        ),
        name="experts",
    )(sums, *blocks, gate_weight, up_weight, adapter_up, *parts, *in_hbm(down_weight))


def down_kernel(active, after, *refs):
    *parts, out = refs
    for i, part in enumerate(parts):
        out[i] = jnp.dot(active[...], part[...], preferred_element_type=F32)


def down_fetching_kernel(targets, active, after, down_weight, out, *refs):
    parts, arrived = refs[:-1], refs[-1]
    for i, copy in enumerate(fetch(down_weight, targets, parts, arrived)):
        copy.wait()
        out[i] = jnp.dot(active[...], parts[i][...], preferred_element_type=F32)


def down(targets, active, parts, down_weight, features, after):
    rows, hidden = active.shape
    count = len(targets)
    columns = pltpu.VMEM((hidden, features), BF16)
    scratch = () if parts else (*[columns] * count, pltpu.SemaphoreType.DMA((count,)))
    return pl.pallas_call(
        down_kernel if parts else functools.partial(down_fetching_kernel, targets),
        out_shape=jax.ShapeDtypeStruct((count, rows, features), F32),
        in_specs=[VMEM, HBM] + ([VMEM] * count if parts else [HBM]),
        out_specs=VMEM,
        scratch_shapes=scratch,
        compiler_params=pltpu.CompilerParams(vmem_limit_bytes=5 * 2**20),
        cost_estimate=pl.CostEstimate(
            flops=2 * rows * hidden * features * count,
            bytes_accessed=2 * hidden * features * count,
            transcendentals=0,
        ),
        name="down",
    )(active, after, *(parts if parts else in_hbm(down_weight)))


def join_kernel(first, second, *refs):
    out = refs[-1]
    count = first.shape[0]
    out[:count] = first[...]
    out[count:] = second[...]


def join(first, second, *after):
    return pl.pallas_call(
        join_kernel,
        out_shape=jax.ShapeDtypeStruct((2 * first.shape[0], *first.shape[1:]), first.dtype),
        in_specs=[VMEM, VMEM] + [HBM] * len(after),
        out_specs=VMEM,
        compiler_params=pltpu.CompilerParams(vmem_limit_bytes=1 * 2**20),
        name="join",
    )(first, second, *after)


def mark_kernel(after, weight, out):
    out[...] = jnp.zeros_like(out)


def mark(after, weight):
    return pl.pallas_call(
        mark_kernel,
        out_shape=jax.ShapeDtypeStruct((8, LANES), F32),
        in_specs=[HBM, HBM],
        out_specs=VMEM,
        compiler_params=pltpu.CompilerParams(vmem_limit_bytes=2**20),
        name="mark",
    )(after, *in_hbm(weight))


def tie_kernel(array, after, out):
    pass


def tie(array, after):
    return pl.pallas_call(
        tie_kernel,
        out_shape=jax.ShapeDtypeStruct(array.shape, array.dtype),
        in_specs=[HBM, HBM],
        out_specs=HBM,
        input_output_aliases={0: 0},
        compiler_params=pltpu.CompilerParams(vmem_limit_bytes=2**20),
        name="tie",
    )(array, after)


def swap(x, axis, distance):
    count = lax.axis_size(axis)
    return lax.ppermute(x, axis, [(i, i ^ distance) for i in range(count)])


def bits(count):
    return [1 << b for b in range(count.bit_length() - 1)]


def per_device(
    residual,
    queries,
    token_keys,
    token_values,
    stored_keys,
    stored_values,
    lengths,
    norm_gain_vector,
    router,
    expert_gate_weight,
    expert_up_weight,
    expert_down_weight,
    adapter_down_map,
    adapter_up_map,
    routes,
    tenants,
):
    rows, features = residual.shape
    expert_devices = lax.axis_size("ep")
    tensor_devices = lax.axis_size("tp")
    state, held = attend(
        (
            lengths,
            tenants,
            routes.T,
            residual,
            queries,
            token_keys,
            token_values,
            stored_keys,
            stored_values,
            norm_gain_vector.reshape(features // LANES, LANES),
            router.T,
            adapter_down_map,
        ),
    )
    for distance in bits(expert_devices):
        other = swap(held, "ep", distance)
        last = 2 * distance == expert_devices
        beside = mark(held, expert_down_weight)
        held = join(held, other, beside, *((expert_up_weight,) if last else ()))
    steps = bits(tensor_devices)
    groups = [tuple(k for k in range(tensor_devices) if k & -k == step) for step in steps] + [(0,)]
    early, late = groups[0][-1:], groups[0][:-1]
    blocks, order, known, sums, parts = [held], [0], 0, None, []
    for distance in reversed(steps):
        others = [swap(block, "tp", distance) for block in blocks]
        for block in blocks[known:]:
            sums, *more = partial(
                block,
                order[known],
                sums,
                expert_gate_weight,
                expert_up_weight,
                expert_down_weight,
                () if known else early,
                () if known else (expert_gate_weight, adapter_up_map),
            )
            parts += more
            known += 1
        blocks = blocks + [tie(block, sums) if distance > 1 else block for block in others]
        order = order + [at ^ distance for at in order]
    sent, active, *parts = experts(
        expert_devices // EXPERT_COUNT,
        late,
        groups[1],
        tuple(order),
        sums,
        known,
        blocks,
        expert_gate_weight,
        expert_up_weight,
        adapter_up_map,
        parts,
        expert_down_weight,
    )
    received = {k: [] for k in range(tensor_devices)}
    groups[0] = early + late
    for step, group, following in zip(steps, groups[:-1], groups[1:], strict=True):
        arriving = swap(sent, "tp", step)
        made = down(following, active, parts, expert_down_weight, features, sent)
        parts = []
        for i, k in enumerate(group):
            received[k ^ step].append(arriving[i])
        kept = [
            sum((block.astype(F32) for block in received[k]), made[i])
            for i, k in enumerate(following)
        ]
        if following != (0,):
            sent = jnp.stack([block.astype(BF16) for block in kept])
    kept = kept[0].reshape(expert_devices, rows, features)
    for distance in bits(expert_devices):
        kept, sent = kept[0::2], kept[1::2].astype(BF16)
        kept = kept + swap(sent, "ep", distance).astype(F32)
    return (state.astype(F32) + kept[0]).astype(BF16)


def solution(mesh):
    placed = (
        P(("groups", "ep"), "tp"),
        P(("groups", "ep"), "tp"),
        P(("groups", "ep"), "tp"),
        P(("groups", "ep"), "tp"),
        P(("groups", "ep"), None, "tp"),
        P(("groups", "ep"), None, "tp"),
        P(("groups", "ep")),
        P("tp"),
        P("tp", None),
        P(None, ("ep", "tp")),
        P(None, ("ep", "tp")),
        P(("ep", "tp"), None),
        P("tp", None),
        P(None, ("ep", "tp")),
        P(("groups", "ep"), None),
        P(("groups", "ep")),
    )
    return jax.shard_map(
        per_device, mesh=mesh, in_specs=placed, out_specs=P(("groups", "ep"), "tp"), check_vma=False
    )
```

```python
import functools

import jax
import jax.numpy as jnp
from jax import lax
from jax.experimental import pallas as pl
from jax.experimental.pallas import tpu as pltpu
from jax.sharding import PartitionSpec as P

HEADS = 24
KVH = 8
HD = 128
EXPERT_COUNT = 4
ADAPTER_RANK = 16
TENANT_COUNT = 8
CAP = 10
LANES = 128
ADAPTER_LANES = EXPERT_COUNT * ADAPTER_RANK
DIFF_HI, DIFF_LO, SQ_HI, SQ_LO, FIRST, SECOND, TENANT = range(ADAPTER_LANES, ADAPTER_LANES + 7)
F32 = jnp.float32
BF16 = jnp.bfloat16
ANY_LANES = (((1,), (1,)), ((), ()))


VMEM = pl.BlockSpec(memory_space=pltpu.VMEM)
HBM = pl.BlockSpec(memory_space=pl.ANY)


def in_hbm(*arrays):
    return [pltpu.with_memory_space_constraint(array, pltpu.HBM) for array in arrays]


def column(values, rows):
    index = lax.broadcasted_iota(jnp.int32, (rows, LANES), 0)
    out = jnp.zeros((rows, LANES), jnp.int32)
    for r in range(rows):
        out = jnp.where(index == r, values(r), out)
    return out


def at_distance(distance, size):
    return pl.ds(pl.multiple_of((lax.axis_index("tp") ^ distance) * size, size), size)


def attend_kernel(*refs):
    count = 12
    sources, outs, buffers, arrived = refs[:count], refs[count : count + 2], refs[count + 2 : -1], refs[-1]
    copies = [
        pltpu.make_async_copy(source, buffer, arrived.at[i])
        for i, (source, buffer) in enumerate(zip(sources, buffers, strict=True))
    ]
    for i in (7, 4, 0, 5, 8, 6, 3, 9, 1, 2, 10, 11):
        copies[i].start()
    attend_body(*buffers, *outs, wait=lambda *which: [copies[i].wait() for i in which])


def attend_body(
    lengths,
    tenants,
    routes,
    residual,
    queries,
    token_keys,
    token_values,
    stored_keys,
    stored_values,
    gain,
    router,
    adapter_down,
    state_out,
    payload_out,
    *,
    wait,
):
    rows, features = residual.shape
    kv_local = token_keys.shape[1] // HD
    cache = stored_keys.shape[1]
    group = HEADS // KVH
    scale = HD ** (-0.5)
    wait(0, 4, 7)
    heads = kv_local * group
    together = 2 if rows % 2 == 0 else 1
    length_column = column(lambda r: lengths[r], rows)
    stacked_length = jnp.concatenate([length_column[:, :1]] * heads, axis=0)
    stacked_row = lax.rem(
        lax.broadcasted_iota(jnp.int32, (heads * rows, cache), 0), jnp.int32(rows)
    )
    visible = lax.broadcasted_iota(jnp.int32, (heads * rows, cache), 1) < stacked_length

    def stacked(get):
        return jnp.concatenate([get(g, j) for g in range(kv_local) for j in range(group)], axis=0)

    def head_lanes(g, j=None):
        h = g if j is None else g * group + j
        return slice(h * HD, (h + 1) * HD)

    query = stacked(lambda g, j: queries[:, head_lanes(g, j)])
    wide = jnp.concatenate([query] * kv_local, axis=1)
    lane_head = lax.broadcasted_iota(jnp.int32, wide.shape, 1) // HD
    row_head = lax.broadcasted_iota(jnp.int32, wide.shape, 0) // (group * rows)
    wide = jnp.where(lane_head == row_head, wide.astype(F32), 0.0).astype(BF16)
    scores = jnp.zeros((heads * rows, cache), F32)
    for r in range(0, rows, together):
        keys = stored_keys[r : r + together].reshape(together * cache, kv_local * HD)
        every = lax.dot_general(wide, keys, ANY_LANES, preferred_element_type=F32)
        for i in range(together):
            scores = jnp.where(
                stacked_row == r + i, every[:, i * cache : (i + 1) * cache], scores
            )
    scores = jnp.where(visible, scores * scale, -jnp.inf)
    wait(5)
    fresh_key = stacked(lambda g, j: token_keys[:, head_lanes(g)].astype(F32))
    fresh = jnp.sum(query.astype(F32) * fresh_key, axis=1, keepdims=True) * scale
    largest = jnp.maximum(jnp.max(scores, axis=1, keepdims=True), fresh)
    cache_exp = jnp.exp(scores - largest)
    fresh_exp = jnp.exp(fresh - largest)
    denominator = jnp.sum(cache_exp, axis=1, keepdims=True) + fresh_exp
    probs = cache_exp / denominator
    fresh_prob = (fresh_exp / denominator).astype(BF16).astype(F32)
    wait(8)
    every = jnp.zeros((heads * rows, kv_local * HD), F32)
    for r in range(0, rows, together):
        values = stored_values[r : r + together].reshape(together * cache, kv_local * HD)
        own = [jnp.where(stacked_row == r + i, probs, 0.0).astype(BF16) for i in range(together)]
        every = every + jnp.dot(
            jnp.concatenate(own, axis=1), values, preferred_element_type=F32
        )
    wait(3, 6, 9)
    squares = jnp.zeros((rows, 1), F32)
    for g in range(kv_local):
        fresh_value = token_values[:, head_lanes(g)].astype(F32)
        for j in range(group):
            lanes = head_lanes(g, j)
            place = slice((g * group + j) * rows, (g * group + j + 1) * rows)
            attended = every[place, head_lanes(g)] + fresh_prob[place] * fresh_value
            state = (residual[:, lanes].astype(F32) + attended).astype(BF16)
            state_out[:, lanes] = state
            state = state.astype(F32)
            squares = squares + jnp.sum(state * state, axis=1, keepdims=True)
            payload_out[:, lanes] = (
                state * gain[lanes.start // LANES : lanes.start // LANES + 1, :]
            ).astype(BF16)
    wait(1, 2, 10, 11)
    scaled = payload_out[:, :features]
    logits = lax.dot_general(scaled, router[...], ANY_LANES, preferred_element_type=F32)
    first = column(lambda r: routes[0, r], rows)
    second = column(lambda r: routes[1, r], rows)
    tenant = column(lambda r: tenants[r], rows)
    expert = lax.broadcasted_iota(jnp.int32, logits.shape, 1)
    chosen = jnp.where(expert == first[:, :EXPERT_COUNT], logits, 0.0) - jnp.where(
        expert == second[:, :EXPERT_COUNT], logits, 0.0
    )
    diff = jnp.sum(chosen, axis=1, keepdims=True)
    adapter = jnp.dot(scaled, adapter_down[...], preferred_element_type=F32)
    lane = lax.broadcasted_iota(jnp.int32, (rows, LANES), 1)
    tail = jnp.zeros((rows, LANES), F32)
    for start in range(0, adapter.shape[1], LANES):
        owner = (lane + start) // ADAPTER_LANES
        tail = tail + jnp.where(owner == tenant, adapter[:, start : start + LANES], 0.0)
    tail = tail + pltpu.roll(tail, ADAPTER_LANES, 1)
    diff_hi = diff.astype(BF16).astype(F32)
    squares_hi = squares.astype(BF16).astype(F32)
    for place, value in (
        (DIFF_HI, diff_hi),
        (DIFF_LO, diff - diff_hi),
        (SQ_HI, squares_hi),
        (SQ_LO, squares - squares_hi),
        (FIRST, first.astype(F32)),
        (SECOND, second.astype(F32)),
        (TENANT, tenant.astype(F32)),
    ):
        tail = jnp.where(lane == place, value, tail)
    payload_out[:, features:] = tail.astype(BF16)


def attend(args):
    rows, features = args[3].shape
    return pl.pallas_call(
        attend_kernel,
        out_shape=(
            jax.ShapeDtypeStruct((rows, features), BF16),
            jax.ShapeDtypeStruct((rows, features + LANES), BF16),
        ),
        in_specs=[HBM] * len(args),
        out_specs=(VMEM,) * 2,
        scratch_shapes=[
            (pltpu.SMEM if i < 3 else pltpu.VMEM)(arg.shape, arg.dtype)
            for i, arg in enumerate(args)
        ]
        + [pltpu.SemaphoreType.DMA((len(args),))],
        compiler_params=pltpu.CompilerParams(vmem_limit_bytes=6 * 2**20),
        cost_estimate=pl.CostEstimate(
            flops=200_000_000, bytes_accessed=3_000_000, transcendentals=20_000
        ),
        name="attend",
    )(*in_hbm(*args))


def fetch(down_weight, distances, parts, arrived):
    copies = [
        pltpu.make_async_copy(
            down_weight.at[:, at_distance(distance, part.shape[1])], part, arrived.at[i]
        )
        for i, (distance, part) in enumerate(zip(distances, parts, strict=True))
    ]
    for copy in copies:
        copy.start()
    return copies


def halves(hidden):
    return hidden // 2 if hidden % (2 * LANES) == 0 else hidden


def partial_kernel(distance, fetched, first, soon, block, gate_weight, up_weight, *refs):
    hidden = gate_weight.shape[1]
    features = block.shape[1] - LANES
    sums, refs = (None, refs) if first else (refs[0], refs[1:])
    down_weight, totals = refs[0], refs[1 + soon]
    copies = fetch(down_weight, fetched, refs[2 + soon : -1], refs[-1])
    tile = halves(hidden)
    depth = at_distance(distance, features)

    def products(n, carry):
        lanes = pl.ds(pl.multiple_of(n * tile, tile), tile)
        for i, weight in enumerate((gate_weight, up_weight)):
            product = jnp.dot(
                block[:, :features], weight[depth, lanes], preferred_element_type=F32
            )
            totals[i, :, lanes] = product if first else sums[i, :, lanes] + product
        return carry

    lax.fori_loop(0, hidden // tile, products, 0)
    for copy in copies:
        copy.wait()


def partial(block, distance, sums, gate_weight, up_weight, down_weight, fetched, soon):
    rows, width = block.shape
    features = width - LANES
    hidden = gate_weight.shape[1]
    first = sums is None
    return pl.pallas_call(
        functools.partial(partial_kernel, distance, fetched, first, len(soon)),
        out_shape=(
            jax.ShapeDtypeStruct((2, rows, hidden), F32),
            *[jax.ShapeDtypeStruct((hidden, features), BF16)] * len(fetched),
        ),
        in_specs=[VMEM] * (3 if first else 4) + [HBM] * (1 + len(soon)),
        out_specs=(VMEM,) * (1 + len(fetched)),
        scratch_shapes=[pltpu.SemaphoreType.DMA((max(1, len(fetched)),))],
        compiler_params=pltpu.CompilerParams(vmem_limit_bytes=3 * 2**20),
        cost_estimate=pl.CostEstimate(
            flops=4 * rows * features * hidden,
            bytes_accessed=2 * features * hidden,
            transcendentals=0,
        ),
        name="partial",
    )(block, gate_weight, up_weight, *(() if first else (sums,)), *in_hbm(down_weight), *soon)


def expert_kernel(replicas, late, following, order, known, early, sums, *refs):
    tensor_devices = len(order)
    blocks, refs = refs[:tensor_devices], refs[tensor_devices:]
    gate_weight, up_weight, adapter_up, refs = *refs[:3], refs[3:]
    early_parts, refs = refs[:early], refs[early:]
    down_weight, out, active, refs = *refs[:3], refs[3:]
    next_parts, late_parts, arrived = refs[: len(following)], refs[len(following) : -1], refs[-1]
    rows, width = blocks[0].shape
    features = width - LANES
    hidden = active.shape[1]
    copies = fetch(down_weight, late + following, (*late_parts, *next_parts), arrived)
    tile = halves(hidden)

    @pl.when(lax.axis_index("tp") >= 0)
    def _():
        expert = lax.axis_index("ep") // replicas
        tail = jnp.zeros((rows, LANES), F32)
        for block in blocks:
            tail = tail + block[:, features:].astype(F32)
        place = lambda k: tail[:, k : k + 1]
        here = blocks[0][:, features:].astype(F32)
        inverse_rms = lax.rsqrt(
            (place(SQ_HI) + place(SQ_LO)) / (features * tensor_devices) + 1e-05
        )
        diff = (place(DIFF_HI) + place(DIFF_LO)) * inverse_rms
        expert_float = expert.astype(F32)
        is_first = here[:, FIRST : FIRST + 1] == expert_float
        is_second = here[:, SECOND : SECOND + 1] == expert_float
        weight = jnp.where(
            is_first, jax.nn.sigmoid(diff), jnp.where(is_second, jax.nn.sigmoid(-diff), 0.0)
        )
        lowrank = (tail * inverse_rms).astype(BF16)
        spread_shape = (LANES, TENANT_COUNT * ADAPTER_RANK)
        source = lax.broadcasted_iota(jnp.int32, spread_shape, 0)
        target = lax.broadcasted_iota(jnp.int32, spread_shape, 1)
        spread = jnp.where(
            source == expert * ADAPTER_RANK + lax.rem(target, jnp.int32(ADAPTER_RANK)), 1.0, 0.0
        ).astype(BF16)
        lane = lax.broadcasted_iota(jnp.int32, (rows, TENANT_COUNT * ADAPTER_RANK), 1)
        own_tenant = (lane // ADAPTER_RANK).astype(F32) == here[:, TENANT : TENANT + 1]
        adapter_rows = jnp.where(
            own_tenant, jnp.dot(lowrank, spread, preferred_element_type=F32), 0.0
        ).astype(BF16)
        for start in range(0, hidden, tile):
            lanes = slice(start, start + tile)
            gate, up = sums[0, :, lanes], sums[1, :, lanes]
            for block, distance in zip(blocks[known:], order[known:], strict=True):
                scaled = block[:, :features]
                depth = at_distance(distance, features)
                gate = gate + jnp.dot(
                    scaled, gate_weight[depth, lanes], preferred_element_type=F32
                )
                up = up + jnp.dot(scaled, up_weight[depth, lanes], preferred_element_type=F32)
            gate = gate * inverse_rms
            up = up * inverse_rms + jnp.dot(
                adapter_rows, adapter_up[:, lanes], preferred_element_type=F32
            )
            active[:, lanes] = (gate * jax.nn.sigmoid(gate) * up * weight).astype(BF16)
        for i, part in enumerate((*early_parts, *late_parts)):
            if i >= early:
                copies[i - early].wait()
            out[i] = jnp.dot(active[...], part[...], preferred_element_type=F32).astype(out.dtype)

    for copy in copies[len(late) :]:
        copy.wait()


def experts(
    replicas, late, following, order, sums, known, blocks, gate_weight, up_weight, adapter_up, parts, down_weight
):
    rows, width = blocks[0].shape
    features, hidden = width - LANES, sums.shape[2]
    count = len(parts) + len(late)
    columns = (hidden, features)
    return pl.pallas_call(
        functools.partial(expert_kernel, replicas, late, following, order, known, len(parts)),
        out_shape=(
            jax.ShapeDtypeStruct((count, rows, features), BF16),
            jax.ShapeDtypeStruct((rows, hidden), BF16),
            *[jax.ShapeDtypeStruct(columns, BF16)] * len(following),
        ),
        in_specs=[VMEM] * (4 + len(blocks) + len(parts)) + [HBM],
        out_specs=(VMEM,) * (2 + len(following)),
        scratch_shapes=[pltpu.VMEM(columns, BF16)] * len(late)
        + [pltpu.SemaphoreType.DMA((len(late) + len(following),))],
        compiler_params=pltpu.CompilerParams(vmem_limit_bytes=5 * 2**20),
        cost_estimate=pl.CostEstimate(
            flops=2 * rows * hidden * features * (2 * (len(blocks) - known) + count),
            bytes_accessed=2 * hidden * features * (len(late) + len(following)),
            transcendentals=0,
        ),
        name="experts",
    )(sums, *blocks, gate_weight, up_weight, adapter_up, *parts, *in_hbm(down_weight))


def down_kernel(active, after, *refs):
    *parts, out = refs
    for i, part in enumerate(parts):
        out[i] = jnp.dot(active[...], part[...], preferred_element_type=F32)


def down_fetching_kernel(targets, active, after, down_weight, out, *refs):
    parts, arrived = refs[:-1], refs[-1]
    for i, copy in enumerate(fetch(down_weight, targets, parts, arrived)):
        copy.wait()
        out[i] = jnp.dot(active[...], parts[i][...], preferred_element_type=F32)


def down(targets, active, parts, down_weight, features, after):
    rows, hidden = active.shape
    count = len(targets)
    columns = pltpu.VMEM((hidden, features), BF16)
    scratch = () if parts else (*[columns] * count, pltpu.SemaphoreType.DMA((count,)))
    return pl.pallas_call(
        down_kernel if parts else functools.partial(down_fetching_kernel, targets),
        out_shape=jax.ShapeDtypeStruct((count, rows, features), F32),
        in_specs=[VMEM, HBM] + ([VMEM] * count if parts else [HBM]),
        out_specs=VMEM,
        scratch_shapes=scratch,
        compiler_params=pltpu.CompilerParams(vmem_limit_bytes=5 * 2**20),
        cost_estimate=pl.CostEstimate(
            flops=2 * rows * hidden * features * count,
            bytes_accessed=2 * hidden * features * count,
            transcendentals=0,
        ),
        name="down",
    )(active, after, *(parts if parts else in_hbm(down_weight)))


def join_kernel(first, second, *refs):
    out = refs[-1]
    count = first.shape[0]
    out[:count] = first[...]
    out[count:] = second[...]


def join(first, second, *after):
    return pl.pallas_call(
        join_kernel,
        out_shape=jax.ShapeDtypeStruct((2 * first.shape[0], *first.shape[1:]), first.dtype),
        in_specs=[VMEM, VMEM] + [HBM] * len(after),
        out_specs=VMEM,
        compiler_params=pltpu.CompilerParams(vmem_limit_bytes=1 * 2**20),
        name="join",
    )(first, second, *after)


def pack_kernel(replicas, first, second, *refs):
    packed, place = refs[-2:]
    rows, slots = place.shape
    half = first.shape[0]
    features = first.shape[1] - LANES
    every = jnp.concatenate([first[...], second[...]], axis=0)
    tail = every[:, features:].astype(F32)
    expert = (lax.axis_index("ep") // replicas).astype(F32)
    named = jnp.where(
        (tail[:, FIRST : FIRST + 1] == expert) | (tail[:, SECOND : SECOND + 1] == expert), 1.0, 0.0
    )
    row = lax.broadcasted_iota(jnp.int32, (rows, rows), 0)
    before = jnp.where(lax.broadcasted_iota(jnp.int32, (rows, rows), 1) < row, 1.0, 0.0)
    named = jnp.broadcast_to(named, (rows, slots))
    slot = jnp.dot(before.astype(BF16), named.astype(BF16), preferred_element_type=F32)
    lane = lax.broadcasted_iota(jnp.int32, (rows, slots), 1).astype(F32)
    at = jnp.where(lane == slot, named, 0.0)
    place[...] = at.astype(BF16)
    packed[...] = lax.dot_general(
        at.astype(BF16), every, (((0,), (0,)), ((), ())), preferred_element_type=F32
    ).astype(BF16)


def pack(first, second, replicas, slots, *after):
    rows, width = 2 * first.shape[0], first.shape[1]
    return pl.pallas_call(
        functools.partial(pack_kernel, replicas),
        out_shape=(
            jax.ShapeDtypeStruct((slots, width), BF16),
            jax.ShapeDtypeStruct((rows, slots), BF16),
        ),
        in_specs=[VMEM, VMEM] + [HBM] * len(after),
        out_specs=(VMEM, VMEM),
        compiler_params=pltpu.CompilerParams(vmem_limit_bytes=4 * 2**20),
        name="pack",
    )(first, second, *after)


def unpack_kernel(place, made, *refs):
    *arrived, kept, sent = refs
    total = made[0]
    for block in arrived:
        total = total + block[0].astype(F32)
    high = total.astype(BF16)
    low = (total - high.astype(F32)).astype(BF16)
    at = place[...]
    full = jnp.dot(at, high, preferred_element_type=F32) + jnp.dot(
        at, low, preferred_element_type=F32
    )
    rows = kept.shape[1]
    for j in range(kept.shape[0]):
        kept[j] = full[2 * j * rows : (2 * j + 1) * rows]
        sent[j] = full[(2 * j + 1) * rows : (2 * j + 2) * rows].astype(BF16)


def unpack(place, made, arrived, rows):
    features = made.shape[2]
    pairs = place.shape[0] // (2 * rows)
    return pl.pallas_call(
        unpack_kernel,
        out_shape=(
            jax.ShapeDtypeStruct((pairs, rows, features), F32),
            jax.ShapeDtypeStruct((pairs, rows, features), BF16),
        ),
        in_specs=[VMEM] * (2 + len(arrived)),
        out_specs=(VMEM, VMEM),
        compiler_params=pltpu.CompilerParams(vmem_limit_bytes=4 * 2**20),
        name="unpack",
    )(place, made, *arrived)


def mark_kernel(after, weight, out):
    out[...] = jnp.zeros_like(out)


def mark(after, weight):
    return pl.pallas_call(
        mark_kernel,
        out_shape=jax.ShapeDtypeStruct((8, LANES), F32),
        in_specs=[HBM, HBM],
        out_specs=VMEM,
        compiler_params=pltpu.CompilerParams(vmem_limit_bytes=2**20),
        name="mark",
    )(after, *in_hbm(weight))


def tie_kernel(array, after, out):
    pass


def tie(array, after):
    return pl.pallas_call(
        tie_kernel,
        out_shape=jax.ShapeDtypeStruct(array.shape, array.dtype),
        in_specs=[HBM, HBM],
        out_specs=HBM,
        input_output_aliases={0: 0},
        compiler_params=pltpu.CompilerParams(vmem_limit_bytes=2**20),
        name="tie",
    )(array, after)


def swap(x, axis, distance):
    count = lax.axis_size(axis)
    return lax.ppermute(x, axis, [(i, i ^ distance) for i in range(count)])


def bits(count):
    return [1 << b for b in range(count.bit_length() - 1)]


def per_device(
    residual,
    queries,
    token_keys,
    token_values,
    stored_keys,
    stored_values,
    lengths,
    norm_gain_vector,
    router,
    expert_gate_weight,
    expert_up_weight,
    expert_down_weight,
    adapter_down_map,
    adapter_up_map,
    routes,
    tenants,
):
    rows, features = residual.shape
    expert_devices = lax.axis_size("ep")
    tensor_devices = lax.axis_size("tp")
    state, held = attend(
        (
            lengths,
            tenants,
            routes.T,
            residual,
            queries,
            token_keys,
            token_values,
            stored_keys,
            stored_values,
            norm_gain_vector.reshape(features // LANES, LANES),
            router.T,
            adapter_down_map,
        ),
    )
    replicas = expert_devices // EXPERT_COUNT
    for distance in bits(expert_devices):
        other = swap(held, "ep", distance)
        last = 2 * distance == expert_devices
        beside = mark(held, expert_down_weight)
        if last:
            slots = expert_devices * CAP
            held, place = pack(held, other, replicas, slots, beside, expert_up_weight)
        else:
            held = join(held, other, beside)
    steps = bits(tensor_devices)
    groups = [tuple(k for k in range(tensor_devices) if k & -k == step) for step in steps] + [(0,)]
    early, late = groups[0][-1:], groups[0][:-1]
    blocks, order, known, sums, parts = [held], [0], 0, None, []
    for distance in reversed(steps):
        others = [swap(block, "tp", distance) for block in blocks]
        for block in blocks[known:]:
            sums, *more = partial(
                block,
                order[known],
                sums,
                expert_gate_weight,
                expert_up_weight,
                expert_down_weight,
                () if known else early,
                () if known else (expert_gate_weight, adapter_up_map),
            )
            parts += more
            known += 1
        blocks = blocks + [tie(block, sums) if distance > 1 else block for block in others]
        order = order + [at ^ distance for at in order]
    sent, active, *parts = experts(
        replicas,
        late,
        groups[1],
        tuple(order),
        sums,
        known,
        blocks,
        expert_gate_weight,
        expert_up_weight,
        adapter_up_map,
        parts,
        expert_down_weight,
    )
    received = {k: [] for k in range(tensor_devices)}
    groups[0] = early + late
    for step, group, following in zip(steps, groups[:-1], groups[1:], strict=True):
        arriving = swap(sent, "tp", step)
        made = down(following, active, parts, expert_down_weight, features, sent)
        parts = []
        for i, k in enumerate(group):
            received[k ^ step].append(arriving[i])
        if following != (0,):
            kept = [
                sum((block.astype(F32) for block in received[k]), made[i])
                for i, k in enumerate(following)
            ]
            sent = jnp.stack([block.astype(BF16) for block in kept])
    kept, sent = unpack(place, made, [block[None] for block in received[0]], rows)
    for distance in bits(expert_devices):
        if distance > 1:
            kept, sent = kept[0::2], kept[1::2].astype(BF16)
        kept = kept + swap(sent, "ep", distance).astype(F32)
    return (state.astype(F32) + kept[0]).astype(BF16)


def solution(mesh):
    placed = (
        P(("groups", "ep"), "tp"),
        P(("groups", "ep"), "tp"),
        P(("groups", "ep"), "tp"),
        P(("groups", "ep"), "tp"),
        P(("groups", "ep"), None, "tp"),
        P(("groups", "ep"), None, "tp"),
        P(("groups", "ep")),
        P("tp"),
        P("tp", None),
        P(None, ("ep", "tp")),
        P(None, ("ep", "tp")),
        P(("ep", "tp"), None),
        P("tp", None),
        P(None, ("ep", "tp")),
        P(("groups", "ep"), None),
        P(("groups", "ep")),
    )
    return jax.shard_map(
        per_device, mesh=mesh, in_specs=placed, out_specs=P(("groups", "ep"), "tp"), check_vma=False
    )
```

```python
import functools

import jax
import jax.numpy as jnp
from jax import lax
from jax.experimental import pallas as pl
from jax.experimental.pallas import tpu as pltpu
from jax.sharding import PartitionSpec as P

HEADS = 24
KVH = 8
HD = 128
EXPERT_COUNT = 4
ADAPTER_RANK = 16
TENANT_COUNT = 8
CAP = 10
LANES = 128
ADAPTER_LANES = EXPERT_COUNT * ADAPTER_RANK
DIFF_HI, DIFF_LO, SQ_HI, SQ_LO, FIRST, SECOND, TENANT = range(ADAPTER_LANES, ADAPTER_LANES + 7)
F32 = jnp.float32
BF16 = jnp.bfloat16
ANY_LANES = (((1,), (1,)), ((), ()))


VMEM = pl.BlockSpec(memory_space=pltpu.VMEM)
HBM = pl.BlockSpec(memory_space=pl.ANY)


def in_hbm(*arrays):
    return [pltpu.with_memory_space_constraint(array, pltpu.HBM) for array in arrays]


def column(values, rows):
    index = lax.broadcasted_iota(jnp.int32, (rows, LANES), 0)
    out = jnp.zeros((rows, LANES), jnp.int32)
    for r in range(rows):
        out = jnp.where(index == r, values(r), out)
    return out


def at_distance(distance, size):
    return pl.ds(pl.multiple_of((lax.axis_index("tp") ^ distance) * size, size), size)


def attend_kernel(*refs):
    count = 12
    sources, outs, buffers, arrived = refs[:count], refs[count : count + 2], refs[count + 2 : -1], refs[-1]
    copies = [
        pltpu.make_async_copy(source, buffer, arrived.at[i])
        for i, (source, buffer) in enumerate(zip(sources, buffers, strict=True))
    ]
    for i in (7, 4, 0, 5, 8, 6, 3, 9, 1, 2, 10, 11):
        copies[i].start()
    attend_body(*buffers, *outs, wait=lambda *which: [copies[i].wait() for i in which])


def attend_body(
    lengths,
    tenants,
    routes,
    residual,
    queries,
    token_keys,
    token_values,
    stored_keys,
    stored_values,
    gain,
    router,
    adapter_down,
    state_out,
    payload_out,
    *,
    wait,
):
    rows, features = residual.shape
    kv_local = token_keys.shape[1] // HD
    cache = stored_keys.shape[1]
    group = HEADS // KVH
    scale = HD ** (-0.5)
    wait(0, 4, 7)
    heads = kv_local * group
    together = 2 if rows % 2 == 0 else 1
    length_column = column(lambda r: lengths[r], rows)
    stacked_length = jnp.concatenate([length_column[:, :1]] * heads, axis=0)
    stacked_row = lax.rem(
        lax.broadcasted_iota(jnp.int32, (heads * rows, cache), 0), jnp.int32(rows)
    )
    visible = lax.broadcasted_iota(jnp.int32, (heads * rows, cache), 1) < stacked_length

    def stacked(get):
        return jnp.concatenate([get(g, j) for g in range(kv_local) for j in range(group)], axis=0)

    def head_lanes(g, j=None):
        h = g if j is None else g * group + j
        return slice(h * HD, (h + 1) * HD)

    query = stacked(lambda g, j: queries[:, head_lanes(g, j)])
    wide = jnp.concatenate([query] * kv_local, axis=1)
    lane_head = lax.broadcasted_iota(jnp.int32, wide.shape, 1) // HD
    row_head = lax.broadcasted_iota(jnp.int32, wide.shape, 0) // (group * rows)
    wide = jnp.where(lane_head == row_head, wide.astype(F32), 0.0).astype(BF16)
    scores = jnp.zeros((heads * rows, cache), F32)
    for r in range(0, rows, together):
        keys = stored_keys[r : r + together].reshape(together * cache, kv_local * HD)
        every = lax.dot_general(wide, keys, ANY_LANES, preferred_element_type=F32)
        for i in range(together):
            scores = jnp.where(
                stacked_row == r + i, every[:, i * cache : (i + 1) * cache], scores
            )
    scores = jnp.where(visible, scores * scale, -jnp.inf)
    wait(5)
    fresh_key = stacked(lambda g, j: token_keys[:, head_lanes(g)].astype(F32))
    fresh = jnp.sum(query.astype(F32) * fresh_key, axis=1, keepdims=True) * scale
    largest = jnp.maximum(jnp.max(scores, axis=1, keepdims=True), fresh)
    cache_exp = jnp.exp(scores - largest)
    fresh_exp = jnp.exp(fresh - largest)
    denominator = jnp.sum(cache_exp, axis=1, keepdims=True) + fresh_exp
    probs = cache_exp / denominator
    fresh_prob = (fresh_exp / denominator).astype(BF16).astype(F32)
    wait(8)
    every = jnp.zeros((heads * rows, kv_local * HD), F32)
    for r in range(0, rows, together):
        values = stored_values[r : r + together].reshape(together * cache, kv_local * HD)
        own = [jnp.where(stacked_row == r + i, probs, 0.0).astype(BF16) for i in range(together)]
        every = every + jnp.dot(
            jnp.concatenate(own, axis=1), values, preferred_element_type=F32
        )
    wait(3, 6, 9)
    squares = jnp.zeros((rows, 1), F32)
    for g in range(kv_local):
        fresh_value = token_values[:, head_lanes(g)].astype(F32)
        for j in range(group):
            lanes = head_lanes(g, j)
            place = slice((g * group + j) * rows, (g * group + j + 1) * rows)
            attended = every[place, head_lanes(g)] + fresh_prob[place] * fresh_value
            state = (residual[:, lanes].astype(F32) + attended).astype(BF16)
            state_out[:, lanes] = state
            state = state.astype(F32)
            squares = squares + jnp.sum(state * state, axis=1, keepdims=True)
            payload_out[:, lanes] = (
                state * gain[lanes.start // LANES : lanes.start // LANES + 1, :]
            ).astype(BF16)
    wait(1, 2, 10, 11)
    scaled = payload_out[:, :features]
    logits = lax.dot_general(scaled, router[...], ANY_LANES, preferred_element_type=F32)
    first = column(lambda r: routes[0, r], rows)
    second = column(lambda r: routes[1, r], rows)
    tenant = column(lambda r: tenants[r], rows)
    expert = lax.broadcasted_iota(jnp.int32, logits.shape, 1)
    chosen = jnp.where(expert == first[:, :EXPERT_COUNT], logits, 0.0) - jnp.where(
        expert == second[:, :EXPERT_COUNT], logits, 0.0
    )
    diff = jnp.sum(chosen, axis=1, keepdims=True)
    adapter = jnp.dot(scaled, adapter_down[...], preferred_element_type=F32)
    lane = lax.broadcasted_iota(jnp.int32, (rows, LANES), 1)
    tail = jnp.zeros((rows, LANES), F32)
    for start in range(0, adapter.shape[1], LANES):
        owner = (lane + start) // ADAPTER_LANES
        tail = tail + jnp.where(owner == tenant, adapter[:, start : start + LANES], 0.0)
    tail = tail + pltpu.roll(tail, ADAPTER_LANES, 1)
    diff_hi = diff.astype(BF16).astype(F32)
    squares_hi = squares.astype(BF16).astype(F32)
    for place, value in (
        (DIFF_HI, diff_hi),
        (DIFF_LO, diff - diff_hi),
        (SQ_HI, squares_hi),
        (SQ_LO, squares - squares_hi),
        (FIRST, first.astype(F32)),
        (SECOND, second.astype(F32)),
        (TENANT, tenant.astype(F32)),
    ):
        tail = jnp.where(lane == place, value, tail)
    payload_out[:, features:] = tail.astype(BF16)


def attend(args):
    rows, features = args[3].shape
    return pl.pallas_call(
        attend_kernel,
        out_shape=(
            jax.ShapeDtypeStruct((rows, features), BF16),
            jax.ShapeDtypeStruct((rows, features + LANES), BF16),
        ),
        in_specs=[HBM] * len(args),
        out_specs=(VMEM,) * 2,
        scratch_shapes=[
            (pltpu.SMEM if i < 3 else pltpu.VMEM)(arg.shape, arg.dtype)
            for i, arg in enumerate(args)
        ]
        + [pltpu.SemaphoreType.DMA((len(args),))],
        compiler_params=pltpu.CompilerParams(vmem_limit_bytes=6 * 2**20),
        cost_estimate=pl.CostEstimate(
            flops=200_000_000, bytes_accessed=3_000_000, transcendentals=20_000
        ),
        name="attend",
    )(*in_hbm(*args))


def fetch(down_weight, distances, parts, arrived):
    copies = [
        pltpu.make_async_copy(
            down_weight.at[:, at_distance(distance, part.shape[1])], part, arrived.at[i]
        )
        for i, (distance, part) in enumerate(zip(distances, parts, strict=True))
    ]
    for copy in copies:
        copy.start()
    return copies


def halves(hidden):
    return hidden // 2 if hidden % (2 * LANES) == 0 else hidden


def partial_kernel(distance, fetched, first, soon, block, gate_weight, up_weight, *refs):
    hidden = gate_weight.shape[1]
    features = block.shape[1] - LANES
    sums, refs = (None, refs) if first else (refs[0], refs[1:])
    down_weight, totals = refs[0], refs[1 + soon]
    copies = fetch(down_weight, fetched, refs[2 + soon : -1], refs[-1])
    tile = halves(hidden)
    depth = at_distance(distance, features)

    def products(n, carry):
        lanes = pl.ds(pl.multiple_of(n * tile, tile), tile)
        for i, weight in enumerate((gate_weight, up_weight)):
            product = jnp.dot(
                block[:, :features], weight[depth, lanes], preferred_element_type=F32
            )
            totals[i, :, lanes] = product if first else sums[i, :, lanes] + product
        return carry

    lax.fori_loop(0, hidden // tile, products, 0)
    for copy in copies:
        copy.wait()


def partial(block, distance, sums, gate_weight, up_weight, down_weight, fetched, soon):
    rows, width = block.shape
    features = width - LANES
    hidden = gate_weight.shape[1]
    first = sums is None
    return pl.pallas_call(
        functools.partial(partial_kernel, distance, fetched, first, len(soon)),
        out_shape=(
            jax.ShapeDtypeStruct((2, rows, hidden), F32),
            *[jax.ShapeDtypeStruct((hidden, features), BF16)] * len(fetched),
        ),
        in_specs=[VMEM] * (3 if first else 4) + [HBM] * (1 + len(soon)),
        out_specs=(VMEM,) * (1 + len(fetched)),
        scratch_shapes=[pltpu.SemaphoreType.DMA((max(1, len(fetched)),))],
        compiler_params=pltpu.CompilerParams(vmem_limit_bytes=3 * 2**20),
        cost_estimate=pl.CostEstimate(
            flops=4 * rows * features * hidden,
            bytes_accessed=2 * features * hidden,
            transcendentals=0,
        ),
        name="partial",
    )(block, gate_weight, up_weight, *(() if first else (sums,)), *in_hbm(down_weight), *soon)


def expert_kernel(replicas, late, following, order, known, early, sums, *refs):
    tensor_devices = len(order)
    blocks, refs = refs[:tensor_devices], refs[tensor_devices:]
    gate_weight, up_weight, adapter_up, refs = *refs[:3], refs[3:]
    early_parts, refs = refs[:early], refs[early:]
    down_weight, out, active, refs = *refs[:3], refs[3:]
    next_parts, late_parts, arrived = refs[: len(following)], refs[len(following) : -1], refs[-1]
    rows, width = blocks[0].shape
    features = width - LANES
    hidden = active.shape[1]
    copies = fetch(down_weight, late + following, (*late_parts, *next_parts), arrived)
    tile = halves(hidden)

    @pl.when(lax.axis_index("tp") >= 0)
    def _():
        expert = lax.axis_index("ep") // replicas
        tail = jnp.zeros((rows, LANES), F32)
        for block in blocks:
            tail = tail + block[:, features:].astype(F32)
        place = lambda k: tail[:, k : k + 1]
        here = blocks[0][:, features:].astype(F32)
        inverse_rms = lax.rsqrt(
            (place(SQ_HI) + place(SQ_LO)) / (features * tensor_devices) + 1e-05
        )
        diff = (place(DIFF_HI) + place(DIFF_LO)) * inverse_rms
        expert_float = expert.astype(F32)
        is_first = here[:, FIRST : FIRST + 1] == expert_float
        is_second = here[:, SECOND : SECOND + 1] == expert_float
        weight = jnp.where(
            is_first, jax.nn.sigmoid(diff), jnp.where(is_second, jax.nn.sigmoid(-diff), 0.0)
        )
        lowrank = (tail * inverse_rms).astype(BF16)
        spread_shape = (LANES, TENANT_COUNT * ADAPTER_RANK)
        source = lax.broadcasted_iota(jnp.int32, spread_shape, 0)
        target = lax.broadcasted_iota(jnp.int32, spread_shape, 1)
        spread = jnp.where(
            source == expert * ADAPTER_RANK + lax.rem(target, jnp.int32(ADAPTER_RANK)), 1.0, 0.0
        ).astype(BF16)
        lane = lax.broadcasted_iota(jnp.int32, (rows, TENANT_COUNT * ADAPTER_RANK), 1)
        own_tenant = (lane // ADAPTER_RANK).astype(F32) == here[:, TENANT : TENANT + 1]
        adapter_rows = jnp.where(
            own_tenant, jnp.dot(lowrank, spread, preferred_element_type=F32), 0.0
        ).astype(BF16)
        for start in range(0, hidden, tile):
            lanes = slice(start, start + tile)
            gate, up = sums[0, :, lanes], sums[1, :, lanes]
            for block, distance in zip(blocks[known:], order[known:], strict=True):
                scaled = block[:, :features]
                depth = at_distance(distance, features)
                gate = gate + jnp.dot(
                    scaled, gate_weight[depth, lanes], preferred_element_type=F32
                )
                up = up + jnp.dot(scaled, up_weight[depth, lanes], preferred_element_type=F32)
            gate = gate * inverse_rms
            up = up * inverse_rms + jnp.dot(
                adapter_rows, adapter_up[:, lanes], preferred_element_type=F32
            )
            active[:, lanes] = (gate * jax.nn.sigmoid(gate) * up * weight).astype(BF16)
        for i, part in enumerate((*early_parts, *late_parts)):
            if i >= early:
                copies[i - early].wait()
            out[i] = jnp.dot(active[...], part[...], preferred_element_type=F32).astype(out.dtype)

    for copy in copies[len(late) :]:
        copy.wait()


def experts(
    replicas, late, following, order, sums, known, blocks, gate_weight, up_weight, adapter_up, parts, down_weight
):
    rows, width = blocks[0].shape
    features, hidden = width - LANES, sums.shape[2]
    count = len(parts) + len(late)
    columns = (hidden, features)
    return pl.pallas_call(
        functools.partial(expert_kernel, replicas, late, following, order, known, len(parts)),
        out_shape=(
            jax.ShapeDtypeStruct((count, rows, features), BF16),
            jax.ShapeDtypeStruct((rows, hidden), BF16),
            *[jax.ShapeDtypeStruct(columns, BF16)] * len(following),
        ),
        in_specs=[VMEM] * (4 + len(blocks) + len(parts)) + [HBM],
        out_specs=(VMEM,) * (2 + len(following)),
        scratch_shapes=[pltpu.VMEM(columns, BF16)] * len(late)
        + [pltpu.SemaphoreType.DMA((len(late) + len(following),))],
        compiler_params=pltpu.CompilerParams(vmem_limit_bytes=5 * 2**20),
        cost_estimate=pl.CostEstimate(
            flops=2 * rows * hidden * features * (2 * (len(blocks) - known) + count),
            bytes_accessed=2 * hidden * features * (len(late) + len(following)),
            transcendentals=0,
        ),
        name="experts",
    )(sums, *blocks, gate_weight, up_weight, adapter_up, *parts, *in_hbm(down_weight))


def down_kernel(active, after, *refs):
    *parts, out = refs
    for i, part in enumerate(parts):
        out[i] = jnp.dot(active[...], part[...], preferred_element_type=F32)


def down_fetching_kernel(targets, active, after, down_weight, out, *refs):
    parts, arrived = refs[:-1], refs[-1]
    for i, copy in enumerate(fetch(down_weight, targets, parts, arrived)):
        copy.wait()
        out[i] = jnp.dot(active[...], parts[i][...], preferred_element_type=F32)


def down(targets, active, parts, down_weight, features, after):
    rows, hidden = active.shape
    count = len(targets)
    columns = pltpu.VMEM((hidden, features), BF16)
    scratch = () if parts else (*[columns] * count, pltpu.SemaphoreType.DMA((count,)))
    return pl.pallas_call(
        down_kernel if parts else functools.partial(down_fetching_kernel, targets),
        out_shape=jax.ShapeDtypeStruct((count, rows, features), F32),
        in_specs=[VMEM, HBM] + ([VMEM] * count if parts else [HBM]),
        out_specs=VMEM,
        scratch_shapes=scratch,
        compiler_params=pltpu.CompilerParams(vmem_limit_bytes=5 * 2**20),
        cost_estimate=pl.CostEstimate(
            flops=2 * rows * hidden * features * count,
            bytes_accessed=2 * hidden * features * count,
            transcendentals=0,
        ),
        name="down",
    )(active, after, *(parts if parts else in_hbm(down_weight)))


def join_kernel(first, second, *refs):
    out = refs[-1]
    count = first.shape[0]
    out[:count] = first[...]
    out[count:] = second[...]


def join(first, second, *after):
    return pl.pallas_call(
        join_kernel,
        out_shape=jax.ShapeDtypeStruct((2 * first.shape[0], *first.shape[1:]), first.dtype),
        in_specs=[VMEM, VMEM] + [HBM] * len(after),
        out_specs=VMEM,
        compiler_params=pltpu.CompilerParams(vmem_limit_bytes=1 * 2**20),
        name="join",
    )(first, second, *after)


def pack_kernel(replicas, first, second, *refs):
    packed, place = refs[-2:]
    rows, slots = place.shape
    half = first.shape[0]
    features = first.shape[1] - LANES
    every = jnp.concatenate([first[...], second[...]], axis=0)
    tail = every[:, features:].astype(F32)
    expert = (lax.axis_index("ep") // replicas).astype(F32)
    named = jnp.where(
        (tail[:, FIRST : FIRST + 1] == expert) | (tail[:, SECOND : SECOND + 1] == expert), 1.0, 0.0
    )
    row = lax.broadcasted_iota(jnp.int32, (rows, rows), 0)
    before = jnp.where(lax.broadcasted_iota(jnp.int32, (rows, rows), 1) < row, 1.0, 0.0)
    named = jnp.broadcast_to(named, (rows, slots))
    slot = jnp.dot(before.astype(BF16), named.astype(BF16), preferred_element_type=F32)
    lane = lax.broadcasted_iota(jnp.int32, (rows, slots), 1).astype(F32)
    at = jnp.where(lane == slot, named, 0.0)
    place[...] = at.astype(BF16)
    packed[...] = lax.dot_general(
        at.astype(BF16), every, (((0,), (0,)), ((), ())), preferred_element_type=F32
    ).astype(BF16)


def pack(first, second, replicas, slots, *after):
    rows, width = 2 * first.shape[0], first.shape[1]
    return pl.pallas_call(
        functools.partial(pack_kernel, replicas),
        out_shape=(
            jax.ShapeDtypeStruct((slots, width), BF16),
            jax.ShapeDtypeStruct((rows, slots), BF16),
        ),
        in_specs=[VMEM, VMEM] + [HBM] * len(after),
        out_specs=(VMEM, VMEM),
        compiler_params=pltpu.CompilerParams(vmem_limit_bytes=4 * 2**20),
        name="pack",
    )(first, second, *after)


def unpack_kernel(place, made, *refs):
    *arrived, kept, sent = refs
    total = made[0]
    for block in arrived:
        total = total + block[0].astype(F32)
    high = total.astype(BF16)
    low = (total - high.astype(F32)).astype(BF16)
    at = place[...]
    full = jnp.dot(at, high, preferred_element_type=F32) + jnp.dot(
        at, low, preferred_element_type=F32
    )
    rows = kept.shape[1]
    for j in range(kept.shape[0]):
        kept[j] = full[2 * j * rows : (2 * j + 1) * rows]
        sent[j] = full[(2 * j + 1) * rows : (2 * j + 2) * rows].astype(BF16)


def unpack(place, made, arrived, rows):
    features = made.shape[2]
    pairs = place.shape[0] // (2 * rows)
    return pl.pallas_call(
        unpack_kernel,
        out_shape=(
            jax.ShapeDtypeStruct((pairs, rows, features), F32),
            jax.ShapeDtypeStruct((pairs, rows, features), BF16),
        ),
        in_specs=[VMEM] * (2 + len(arrived)),
        out_specs=(VMEM, VMEM),
        compiler_params=pltpu.CompilerParams(vmem_limit_bytes=4 * 2**20),
        name="unpack",
    )(place, made, *arrived)


def mark_kernel(after, *refs):
    out = refs[-1]
    out[...] = jnp.zeros_like(out)


def mark(after, *weights):
    return pl.pallas_call(
        mark_kernel,
        out_shape=jax.ShapeDtypeStruct((8, LANES), F32),
        in_specs=[HBM] * (1 + len(weights)),
        out_specs=VMEM,
        compiler_params=pltpu.CompilerParams(vmem_limit_bytes=2**20),
        name="mark",
    )(after, *in_hbm(*weights))


def tie_kernel(array, after, out):
    pass


def tie(array, after):
    return pl.pallas_call(
        tie_kernel,
        out_shape=jax.ShapeDtypeStruct(array.shape, array.dtype),
        in_specs=[HBM, HBM],
        out_specs=HBM,
        input_output_aliases={0: 0},
        compiler_params=pltpu.CompilerParams(vmem_limit_bytes=2**20),
        name="tie",
    )(array, after)


def swap(x, axis, distance):
    count = lax.axis_size(axis)
    return lax.ppermute(x, axis, [(i, i ^ distance) for i in range(count)])


def bits(count):
    return [1 << b for b in range(count.bit_length() - 1)]


def per_device(
    residual,
    queries,
    token_keys,
    token_values,
    stored_keys,
    stored_values,
    lengths,
    norm_gain_vector,
    router,
    expert_gate_weight,
    expert_up_weight,
    expert_down_weight,
    adapter_down_map,
    adapter_up_map,
    routes,
    tenants,
):
    rows, features = residual.shape
    expert_devices = lax.axis_size("ep")
    tensor_devices = lax.axis_size("tp")
    state, held = attend(
        (
            lengths,
            tenants,
            routes.T,
            residual,
            queries,
            token_keys,
            token_values,
            stored_keys,
            stored_values,
            norm_gain_vector.reshape(features // LANES, LANES),
            router.T,
            adapter_down_map,
        ),
    )
    replicas = expert_devices // EXPERT_COUNT
    for distance in bits(expert_devices):
        other = swap(held, "ep", distance)
        last = 2 * distance == expert_devices
        beside = mark(held, *((expert_down_weight,) if last else (expert_down_weight, expert_gate_weight, expert_up_weight)))
        if last:
            slots = expert_devices * CAP
            held, place = pack(held, other, replicas, slots, beside, expert_up_weight)
        else:
            held = join(held, other, beside)
    steps = bits(tensor_devices)
    groups = [tuple(k for k in range(tensor_devices) if k & -k == step) for step in steps] + [(0,)]
    early, late = groups[0][-1:], groups[0][1:-1]
    blocks, order, known, sums, parts = [held], [0], 0, None, []
    for distance in reversed(steps):
        others = [swap(block, "tp", distance) for block in blocks]
        for block in blocks[known:]:
            sums, *more = partial(
                block,
                order[known],
                sums,
                expert_gate_weight,
                expert_up_weight,
                expert_down_weight,
                () if known else early,
                () if known else (expert_gate_weight, adapter_up_map),
            )
            parts += more
            known += 1
        blocks = blocks + [tie(block, sums) if distance > 1 else block for block in others]
        order = order + [at ^ distance for at in order]
    sent, active, *parts = experts(
        replicas,
        late,
        groups[1] + (1,),
        tuple(order),
        sums,
        known,
        blocks,
        expert_gate_weight,
        expert_up_weight,
        adapter_up_map,
        parts,
        expert_down_weight,
    )
    received = {k: [] for k in range(tensor_devices)}
    groups[0] = early + late
    for step, group, following in zip(steps, groups[:-1], groups[1:], strict=True):
        arriving = swap(sent, "tp", step)
        more = (1,) if parts else ()
        made = down(following + more, active, parts, expert_down_weight, features, sent)
        if more:
            received[0].append(swap(made[-1:].astype(BF16), "tp", 1)[0])
        parts = []
        for i, k in enumerate(group):
            received[k ^ step].append(arriving[i])
        if following != (0,):
            kept = [
                sum((block.astype(F32) for block in received[k]), made[i])
                for i, k in enumerate(following)
            ]
            sent = jnp.stack([block.astype(BF16) for block in kept])
    kept, sent = unpack(place, made, [block[None] for block in received[0]], rows)
    for distance in bits(expert_devices):
        if distance > 1:
            kept, sent = kept[0::2], kept[1::2].astype(BF16)
        kept = kept + swap(sent, "ep", distance).astype(F32)
    return (state.astype(F32) + kept[0]).astype(BF16)


def solution(mesh):
    placed = (
        P(("groups", "ep"), "tp"),
        P(("groups", "ep"), "tp"),
        P(("groups", "ep"), "tp"),
        P(("groups", "ep"), "tp"),
        P(("groups", "ep"), None, "tp"),
        P(("groups", "ep"), None, "tp"),
        P(("groups", "ep")),
        P("tp"),
        P("tp", None),
        P(None, ("ep", "tp")),
        P(None, ("ep", "tp")),
        P(("ep", "tp"), None),
        P("tp", None),
        P(None, ("ep", "tp")),
        P(("groups", "ep"), None),
        P(("groups", "ep")),
    )
    return jax.shard_map(
        per_device, mesh=mesh, in_specs=placed, out_specs=P(("groups", "ep"), "tp"), check_vma=False
    )
```

```python
import functools

import jax
import jax.numpy as jnp
from jax import lax
from jax.experimental import pallas as pl
from jax.experimental.pallas import tpu as pltpu
from jax.sharding import PartitionSpec as P

HEADS = 24
KVH = 8
HD = 128
EXPERT_COUNT = 4
ADAPTER_RANK = 16
TENANT_COUNT = 8
CAP = 10
LANES = 128
ADAPTER_LANES = EXPERT_COUNT * ADAPTER_RANK
DIFF_HI, DIFF_LO, SQ_HI, SQ_LO, FIRST, SECOND, TENANT = range(ADAPTER_LANES, ADAPTER_LANES + 7)
F32 = jnp.float32
BF16 = jnp.bfloat16
ANY_LANES = (((1,), (1,)), ((), ()))


VMEM = pl.BlockSpec(memory_space=pltpu.VMEM)
HBM = pl.BlockSpec(memory_space=pl.ANY)


def in_hbm(*arrays):
    return [pltpu.with_memory_space_constraint(array, pltpu.HBM) for array in arrays]


def column(values, rows):
    index = lax.broadcasted_iota(jnp.int32, (rows, LANES), 0)
    out = jnp.zeros((rows, LANES), jnp.int32)
    for r in range(rows):
        out = jnp.where(index == r, values(r), out)
    return out


def at_distance(distance, size):
    return pl.ds(pl.multiple_of((lax.axis_index("tp") ^ distance) * size, size), size)


def attend_kernel(*refs):
    count = 12
    sources, outs, buffers, arrived = refs[:count], refs[count : count + 2], refs[count + 2 : -1], refs[-1]
    copies = [
        pltpu.make_async_copy(source, buffer, arrived.at[i])
        for i, (source, buffer) in enumerate(zip(sources, buffers, strict=True))
    ]
    for i in (7, 4, 0, 5, 8, 6, 3, 9, 1, 2, 10, 11):
        copies[i].start()
    attend_body(*buffers, *outs, wait=lambda *which: [copies[i].wait() for i in which])


def attend_body(
    lengths,
    tenants,
    routes,
    residual,
    queries,
    token_keys,
    token_values,
    stored_keys,
    stored_values,
    gain,
    router,
    adapter_down,
    state_out,
    payload_out,
    *,
    wait,
):
    rows, features = residual.shape
    kv_local = token_keys.shape[1] // HD
    cache = stored_keys.shape[1]
    group = HEADS // KVH
    scale = HD ** (-0.5)
    wait(0, 4, 7)
    heads = kv_local * group
    together = 2 if rows % 2 == 0 else 1
    length_column = column(lambda r: lengths[r], rows)
    stacked_length = jnp.concatenate([length_column[:, :1]] * heads, axis=0)
    stacked_row = lax.rem(
        lax.broadcasted_iota(jnp.int32, (heads * rows, cache), 0), jnp.int32(rows)
    )
    visible = lax.broadcasted_iota(jnp.int32, (heads * rows, cache), 1) < stacked_length

    def stacked(get):
        return jnp.concatenate([get(g, j) for g in range(kv_local) for j in range(group)], axis=0)

    def head_lanes(g, j=None):
        h = g if j is None else g * group + j
        return slice(h * HD, (h + 1) * HD)

    query = stacked(lambda g, j: queries[:, head_lanes(g, j)])
    wide = jnp.concatenate([query] * kv_local, axis=1)
    lane_head = lax.broadcasted_iota(jnp.int32, wide.shape, 1) // HD
    row_head = lax.broadcasted_iota(jnp.int32, wide.shape, 0) // (group * rows)
    wide = jnp.where(lane_head == row_head, wide.astype(F32), 0.0).astype(BF16)
    scores = jnp.zeros((heads * rows, cache), F32)
    for r in range(0, rows, together):
        keys = stored_keys[r : r + together].reshape(together * cache, kv_local * HD)
        every = lax.dot_general(wide, keys, ANY_LANES, preferred_element_type=F32)
        for i in range(together):
            scores = jnp.where(
                stacked_row == r + i, every[:, i * cache : (i + 1) * cache], scores
            )
    scores = jnp.where(visible, scores * scale, -jnp.inf)
    wait(5)
    fresh_key = stacked(lambda g, j: token_keys[:, head_lanes(g)].astype(F32))
    fresh = jnp.sum(query.astype(F32) * fresh_key, axis=1, keepdims=True) * scale
    largest = jnp.maximum(jnp.max(scores, axis=1, keepdims=True), fresh)
    cache_exp = jnp.exp(scores - largest)
    fresh_exp = jnp.exp(fresh - largest)
    denominator = jnp.sum(cache_exp, axis=1, keepdims=True) + fresh_exp
    probs = cache_exp / denominator
    fresh_prob = (fresh_exp / denominator).astype(BF16).astype(F32)
    wait(8)
    every = jnp.zeros((heads * rows, kv_local * HD), F32)
    for r in range(0, rows, together):
        values = stored_values[r : r + together].reshape(together * cache, kv_local * HD)
        own = [jnp.where(stacked_row == r + i, probs, 0.0).astype(BF16) for i in range(together)]
        every = every + jnp.dot(
            jnp.concatenate(own, axis=1), values, preferred_element_type=F32
        )
    wait(3, 6, 9)
    squares = jnp.zeros((rows, 1), F32)
    for g in range(kv_local):
        fresh_value = token_values[:, head_lanes(g)].astype(F32)
        for j in range(group):
            lanes = head_lanes(g, j)
            place = slice((g * group + j) * rows, (g * group + j + 1) * rows)
            attended = every[place, head_lanes(g)] + fresh_prob[place] * fresh_value
            state = (residual[:, lanes].astype(F32) + attended).astype(BF16)
            state_out[:, lanes] = state
            state = state.astype(F32)
            squares = squares + jnp.sum(state * state, axis=1, keepdims=True)
            payload_out[:, lanes] = (
                state * gain[lanes.start // LANES : lanes.start // LANES + 1, :]
            ).astype(BF16)
    wait(1, 2, 10, 11)
    scaled = payload_out[:, :features]
    logits = lax.dot_general(scaled, router[...], ANY_LANES, preferred_element_type=F32)
    first = column(lambda r: routes[0, r], rows)
    second = column(lambda r: routes[1, r], rows)
    tenant = column(lambda r: tenants[r], rows)
    expert = lax.broadcasted_iota(jnp.int32, logits.shape, 1)
    chosen = jnp.where(expert == first[:, :EXPERT_COUNT], logits, 0.0) - jnp.where(
        expert == second[:, :EXPERT_COUNT], logits, 0.0
    )
    diff = jnp.sum(chosen, axis=1, keepdims=True)
    adapter = jnp.dot(scaled, adapter_down[...], preferred_element_type=F32)
    lane = lax.broadcasted_iota(jnp.int32, (rows, LANES), 1)
    tail = jnp.zeros((rows, LANES), F32)
    for start in range(0, adapter.shape[1], LANES):
        owner = (lane + start) // ADAPTER_LANES
        tail = tail + jnp.where(owner == tenant, adapter[:, start : start + LANES], 0.0)
    tail = tail + pltpu.roll(tail, ADAPTER_LANES, 1)
    diff_hi = diff.astype(BF16).astype(F32)
    squares_hi = squares.astype(BF16).astype(F32)
    for place, value in (
        (DIFF_HI, diff_hi),
        (DIFF_LO, diff - diff_hi),
        (SQ_HI, squares_hi),
        (SQ_LO, squares - squares_hi),
        (FIRST, first.astype(F32)),
        (SECOND, second.astype(F32)),
        (TENANT, tenant.astype(F32)),
    ):
        tail = jnp.where(lane == place, value, tail)
    payload_out[:, features:] = tail.astype(BF16)


def attend(args):
    rows, features = args[3].shape
    return pl.pallas_call(
        attend_kernel,
        out_shape=(
            jax.ShapeDtypeStruct((rows, features), BF16),
            jax.ShapeDtypeStruct((rows, features + LANES), BF16),
        ),
        in_specs=[HBM] * len(args),
        out_specs=(VMEM,) * 2,
        scratch_shapes=[
            (pltpu.SMEM if i < 3 else pltpu.VMEM)(arg.shape, arg.dtype)
            for i, arg in enumerate(args)
        ]
        + [pltpu.SemaphoreType.DMA((len(args),))],
        compiler_params=pltpu.CompilerParams(vmem_limit_bytes=6 * 2**20),
        cost_estimate=pl.CostEstimate(
            flops=200_000_000, bytes_accessed=3_000_000, transcendentals=20_000
        ),
        name="attend",
    )(*in_hbm(*args))


def fetch(down_weight, distances, parts, arrived):
    copies = [
        pltpu.make_async_copy(
            down_weight.at[:, at_distance(distance, part.shape[1])], part, arrived.at[i]
        )
        for i, (distance, part) in enumerate(zip(distances, parts, strict=True))
    ]
    for copy in copies:
        copy.start()
    return copies


def halves(hidden):
    return hidden // 2 if hidden % (2 * LANES) == 0 else hidden


def partial_kernel(distance, fetched, first, soon, block, gate_weight, up_weight, *refs):
    hidden = gate_weight.shape[1]
    features = block.shape[1] - LANES
    sums, refs = (None, refs) if first else (refs[0], refs[1:])
    down_weight, totals = refs[0], refs[1 + soon]
    copies = fetch(down_weight, fetched, refs[2 + soon : -1], refs[-1])
    tile = halves(hidden)
    depth = at_distance(distance, features)

    def products(n, carry):
        lanes = pl.ds(pl.multiple_of(n * tile, tile), tile)
        for i, weight in enumerate((gate_weight, up_weight)):
            product = jnp.dot(
                block[:, :features], weight[depth, lanes], preferred_element_type=F32
            )
            totals[i, :, lanes] = product if first else sums[i, :, lanes] + product
        return carry

    lax.fori_loop(0, hidden // tile, products, 0)
    for copy in copies:
        copy.wait()


def partial(block, distance, sums, gate_weight, up_weight, down_weight, fetched, soon):
    rows, width = block.shape
    features = width - LANES
    hidden = gate_weight.shape[1]
    first = sums is None
    return pl.pallas_call(
        functools.partial(partial_kernel, distance, fetched, first, len(soon)),
        out_shape=(
            jax.ShapeDtypeStruct((2, rows, hidden), F32),
            *[jax.ShapeDtypeStruct((hidden, features), BF16)] * len(fetched),
        ),
        in_specs=[VMEM] * (3 if first else 4) + [HBM] * (1 + len(soon)),
        out_specs=(VMEM,) * (1 + len(fetched)),
        scratch_shapes=[pltpu.SemaphoreType.DMA((max(1, len(fetched)),))],
        compiler_params=pltpu.CompilerParams(vmem_limit_bytes=3 * 2**20),
        cost_estimate=pl.CostEstimate(
            flops=4 * rows * features * hidden,
            bytes_accessed=2 * features * hidden,
            transcendentals=0,
        ),
        name="partial",
    )(block, gate_weight, up_weight, *(() if first else (sums,)), *in_hbm(down_weight), *soon)


def expert_kernel(replicas, late, following, order, known, early, sums, *refs):
    tensor_devices = len(order)
    blocks, refs = refs[:tensor_devices], refs[tensor_devices:]
    gate_weight, up_weight, adapter_up, refs = *refs[:3], refs[3:]
    early_parts, refs = refs[:early], refs[early:]
    down_weight, out, active, refs = *refs[:3], refs[3:]
    next_parts, late_parts, arrived = refs[: len(following)], refs[len(following) : -1], refs[-1]
    rows, width = blocks[0].shape
    features = width - LANES
    hidden = active.shape[1]
    copies = fetch(down_weight, late + following, (*late_parts, *next_parts), arrived)
    tile = halves(hidden)

    @pl.when(lax.axis_index("tp") >= 0)
    def _():
        expert = lax.axis_index("ep") // replicas
        tail = jnp.zeros((rows, LANES), F32)
        for block in blocks:
            tail = tail + block[:, features:].astype(F32)
        place = lambda k: tail[:, k : k + 1]
        here = blocks[0][:, features:].astype(F32)
        inverse_rms = lax.rsqrt(
            (place(SQ_HI) + place(SQ_LO)) / (features * tensor_devices) + 1e-05
        )
        diff = (place(DIFF_HI) + place(DIFF_LO)) * inverse_rms
        expert_float = expert.astype(F32)
        is_first = here[:, FIRST : FIRST + 1] == expert_float
        is_second = here[:, SECOND : SECOND + 1] == expert_float
        weight = jnp.where(
            is_first, jax.nn.sigmoid(diff), jnp.where(is_second, jax.nn.sigmoid(-diff), 0.0)
        )
        lowrank = (tail * inverse_rms).astype(BF16)
        spread_shape = (LANES, TENANT_COUNT * ADAPTER_RANK)
        source = lax.broadcasted_iota(jnp.int32, spread_shape, 0)
        target = lax.broadcasted_iota(jnp.int32, spread_shape, 1)
        spread = jnp.where(
            source == expert * ADAPTER_RANK + lax.rem(target, jnp.int32(ADAPTER_RANK)), 1.0, 0.0
        ).astype(BF16)
        lane = lax.broadcasted_iota(jnp.int32, (rows, TENANT_COUNT * ADAPTER_RANK), 1)
        own_tenant = (lane // ADAPTER_RANK).astype(F32) == here[:, TENANT : TENANT + 1]
        adapter_rows = jnp.where(
            own_tenant, jnp.dot(lowrank, spread, preferred_element_type=F32), 0.0
        ).astype(BF16)
        for start in range(0, hidden, tile):
            lanes = slice(start, start + tile)
            gate, up = sums[0, :, lanes], sums[1, :, lanes]
            for block, distance in zip(blocks[known:], order[known:], strict=True):
                scaled = block[:, :features]
                depth = at_distance(distance, features)
                gate = gate + jnp.dot(
                    scaled, gate_weight[depth, lanes], preferred_element_type=F32
                )
                up = up + jnp.dot(scaled, up_weight[depth, lanes], preferred_element_type=F32)
            gate = gate * inverse_rms
            up = up * inverse_rms + jnp.dot(
                adapter_rows, adapter_up[:, lanes], preferred_element_type=F32
            )
            active[:, lanes] = (gate * jax.nn.sigmoid(gate) * up * weight).astype(BF16)
        for i, part in enumerate((*early_parts, *late_parts)):
            if i >= early:
                copies[i - early].wait()
            out[i] = jnp.dot(active[...], part[...], preferred_element_type=F32).astype(out.dtype)

    for copy in copies[len(late) :]:
        copy.wait()


def experts(
    replicas, late, following, order, sums, known, blocks, gate_weight, up_weight, adapter_up, parts, down_weight
):
    rows, width = blocks[0].shape
    features, hidden = width - LANES, sums.shape[2]
    count = len(parts) + len(late)
    columns = (hidden, features)
    return pl.pallas_call(
        functools.partial(expert_kernel, replicas, late, following, order, known, len(parts)),
        out_shape=(
            jax.ShapeDtypeStruct((count, rows, features), BF16),
            jax.ShapeDtypeStruct((rows, hidden), BF16),
            *[jax.ShapeDtypeStruct(columns, BF16)] * len(following),
        ),
        in_specs=[VMEM] * (4 + len(blocks) + len(parts)) + [HBM],
        out_specs=(VMEM,) * (2 + len(following)),
        scratch_shapes=[pltpu.VMEM(columns, BF16)] * len(late)
        + [pltpu.SemaphoreType.DMA((len(late) + len(following),))],
        compiler_params=pltpu.CompilerParams(vmem_limit_bytes=5 * 2**20),
        cost_estimate=pl.CostEstimate(
            flops=2 * rows * hidden * features * (2 * (len(blocks) - known) + count),
            bytes_accessed=2 * hidden * features * (len(late) + len(following)),
            transcendentals=0,
        ),
        name="experts",
    )(sums, *blocks, gate_weight, up_weight, adapter_up, *parts, *in_hbm(down_weight))


def down_kernel(active, after, *refs):
    *parts, out = refs
    for i, part in enumerate(parts):
        out[i] = jnp.dot(active[...], part[...], preferred_element_type=F32)


def down_fetching_kernel(targets, active, after, down_weight, out, *refs):
    parts, arrived = refs[:-1], refs[-1]
    for i, copy in enumerate(fetch(down_weight, targets, parts, arrived)):
        copy.wait()
        out[i] = jnp.dot(active[...], parts[i][...], preferred_element_type=F32)


def down(targets, active, parts, down_weight, features, after):
    rows, hidden = active.shape
    count = len(targets)
    columns = pltpu.VMEM((hidden, features), BF16)
    scratch = () if parts else (*[columns] * count, pltpu.SemaphoreType.DMA((count,)))
    return pl.pallas_call(
        down_kernel if parts else functools.partial(down_fetching_kernel, targets),
        out_shape=jax.ShapeDtypeStruct((count, rows, features), F32),
        in_specs=[VMEM, HBM] + ([VMEM] * count if parts else [HBM]),
        out_specs=VMEM,
        scratch_shapes=scratch,
        compiler_params=pltpu.CompilerParams(vmem_limit_bytes=5 * 2**20),
        cost_estimate=pl.CostEstimate(
            flops=2 * rows * hidden * features * count,
            bytes_accessed=2 * hidden * features * count,
            transcendentals=0,
        ),
        name="down",
    )(active, after, *(parts if parts else in_hbm(down_weight)))


def join_kernel(first, second, *refs):
    out = refs[-1]
    count = first.shape[0]
    out[:count] = first[...]
    out[count:] = second[...]


def join(first, second, *after):
    return pl.pallas_call(
        join_kernel,
        out_shape=jax.ShapeDtypeStruct((2 * first.shape[0], *first.shape[1:]), first.dtype),
        in_specs=[VMEM, VMEM] + [HBM] * len(after),
        out_specs=VMEM,
        compiler_params=pltpu.CompilerParams(vmem_limit_bytes=1 * 2**20),
        name="join",
    )(first, second, *after)


def pack_kernel(replicas, first, second, *refs):
    packed, place = refs[-2:]
    rows, slots = place.shape
    half = first.shape[0]
    features = first.shape[1] - LANES
    every = jnp.concatenate([first[...], second[...]], axis=0)
    tail = every[:, features:].astype(F32)
    expert = (lax.axis_index("ep") // replicas).astype(F32)
    named = jnp.where(
        (tail[:, FIRST : FIRST + 1] == expert) | (tail[:, SECOND : SECOND + 1] == expert), 1.0, 0.0
    )
    row = lax.broadcasted_iota(jnp.int32, (rows, rows), 0)
    before = jnp.where(lax.broadcasted_iota(jnp.int32, (rows, rows), 1) < row, 1.0, 0.0)
    named = jnp.broadcast_to(named, (rows, slots))
    slot = jnp.dot(before.astype(BF16), named.astype(BF16), preferred_element_type=F32)
    lane = lax.broadcasted_iota(jnp.int32, (rows, slots), 1).astype(F32)
    at = jnp.where(lane == slot, named, 0.0)
    place[...] = at.astype(BF16)
    packed[...] = lax.dot_general(
        at.astype(BF16), every, (((0,), (0,)), ((), ())), preferred_element_type=F32
    ).astype(BF16)


def pack(first, second, replicas, slots, *after):
    rows, width = 2 * first.shape[0], first.shape[1]
    return pl.pallas_call(
        functools.partial(pack_kernel, replicas),
        out_shape=(
            jax.ShapeDtypeStruct((slots, width), BF16),
            jax.ShapeDtypeStruct((rows, slots), BF16),
        ),
        in_specs=[VMEM, VMEM] + [HBM] * len(after),
        out_specs=(VMEM, VMEM),
        compiler_params=pltpu.CompilerParams(vmem_limit_bytes=4 * 2**20),
        name="pack",
    )(first, second, *after)


def unpack_kernel(place, made, *refs):
    *arrived, kept, sent = refs
    total = made[0]
    for block in arrived:
        total = total + block[0].astype(F32)
    high = total.astype(BF16)
    low = (total - high.astype(F32)).astype(BF16)
    at = place[...]
    full = jnp.dot(at, high, preferred_element_type=F32) + jnp.dot(
        at, low, preferred_element_type=F32
    )
    rows = kept.shape[1]
    for j in range(kept.shape[0]):
        kept[j] = full[2 * j * rows : (2 * j + 1) * rows]
        sent[j] = full[(2 * j + 1) * rows : (2 * j + 2) * rows].astype(BF16)


def unpack(place, made, arrived, rows):
    features = made.shape[2]
    pairs = place.shape[0] // (2 * rows)
    return pl.pallas_call(
        unpack_kernel,
        out_shape=(
            jax.ShapeDtypeStruct((pairs, rows, features), F32),
            jax.ShapeDtypeStruct((pairs, rows, features), BF16),
        ),
        in_specs=[VMEM] * (2 + len(arrived)),
        out_specs=(VMEM, VMEM),
        compiler_params=pltpu.CompilerParams(vmem_limit_bytes=4 * 2**20),
        name="unpack",
    )(place, made, *arrived)


def mark_kernel(after, *refs):
    out = refs[-1]
    out[...] = jnp.zeros_like(out)


def mark(after, *weights):
    return pl.pallas_call(
        mark_kernel,
        out_shape=jax.ShapeDtypeStruct((8, LANES), F32),
        in_specs=[HBM] * (1 + len(weights)),
        out_specs=VMEM,
        compiler_params=pltpu.CompilerParams(vmem_limit_bytes=2**20),
        name="mark",
    )(after, *in_hbm(*weights))


def tie_kernel(array, after, out):
    pass


def tie(array, after):
    return pl.pallas_call(
        tie_kernel,
        out_shape=jax.ShapeDtypeStruct(array.shape, array.dtype),
        in_specs=[HBM, HBM],
        out_specs=HBM,
        input_output_aliases={0: 0},
        compiler_params=pltpu.CompilerParams(vmem_limit_bytes=2**20),
        name="tie",
    )(array, after)


def swap(x, axis, distance):
    count = lax.axis_size(axis)
    return lax.ppermute(x, axis, [(i, i ^ distance) for i in range(count)])


def bits(count):
    return [1 << b for b in range(count.bit_length() - 1)]


def per_device(
    residual,
    queries,
    token_keys,
    token_values,
    stored_keys,
    stored_values,
    lengths,
    norm_gain_vector,
    router,
    expert_gate_weight,
    expert_up_weight,
    expert_down_weight,
    adapter_down_map,
    adapter_up_map,
    routes,
    tenants,
):
    rows, features = residual.shape
    expert_devices = lax.axis_size("ep")
    tensor_devices = lax.axis_size("tp")
    state, held = attend(
        (
            lengths,
            tenants,
            routes.T,
            residual,
            queries,
            token_keys,
            token_values,
            stored_keys,
            stored_values,
            norm_gain_vector.reshape(features // LANES, LANES),
            router.T,
            adapter_down_map,
        ),
    )
    replicas = expert_devices // EXPERT_COUNT
    for distance in bits(expert_devices):
        other = swap(held, "ep", distance)
        last = 2 * distance == expert_devices
        beside = mark(held, *((expert_down_weight,) if last else (expert_down_weight, expert_gate_weight, expert_up_weight)))
        if last:
            slots = expert_devices * CAP
            held, place = pack(held, other, replicas, slots, beside, expert_up_weight)
        else:
            held = join(held, other, beside)
    steps = bits(tensor_devices)
    groups = [tuple(k for k in range(tensor_devices) if k & -k == step) for step in steps] + [(0,)]
    early, late = groups[0][-1:], groups[0][1:-1]
    blocks, order, known, sums, parts = [held], [0], 0, None, []
    for distance in reversed(steps):
        others = [swap(block, "tp", distance) for block in blocks]
        for block in blocks[known:]:
            sums, *more = partial(
                block,
                order[known],
                sums,
                expert_gate_weight,
                expert_up_weight,
                expert_down_weight,
                () if known else early,
                () if known else (expert_gate_weight, adapter_up_map),
            )
            parts += more
            known += 1
        blocks = blocks + [tie(block, sums) if distance > 1 else block for block in others]
        order = order + [at ^ distance for at in order]
    sent, active, *parts = experts(
        replicas,
        late,
        groups[1] + (1,),
        tuple(order),
        sums,
        known,
        blocks,
        expert_gate_weight,
        expert_up_weight,
        adapter_up_map,
        parts,
        expert_down_weight,
    )
    received = {k: [] for k in range(tensor_devices)}
    groups[0], one = early + late, None
    for step, group, following in zip(steps, groups[:-1], groups[1:], strict=True):
        if one is not None:
            sent, one = lax.optimization_barrier((sent, one))
        arriving = swap(sent, "tp", step)
        if one is not None:
            received[0].append(swap(one, "tp", 1)[0])
        one = None
        more = (1,) if parts else ()
        made = down(following + more, active, parts, expert_down_weight, features, sent)
        if more:
            one = made[-1:].astype(BF16)
        parts = []
        for i, k in enumerate(group):
            received[k ^ step].append(arriving[i])
        if following != (0,):
            kept = [
                sum((block.astype(F32) for block in received[k]), made[i])
                for i, k in enumerate(following)
            ]
            sent = jnp.stack([block.astype(BF16) for block in kept])
    kept, sent = unpack(place, made, [block[None] for block in received[0]], rows)
    for distance in bits(expert_devices):
        if distance > 1:
            kept, sent = kept[0::2], kept[1::2].astype(BF16)
        kept = kept + swap(sent, "ep", distance).astype(F32)
    return (state.astype(F32) + kept[0]).astype(BF16)


def solution(mesh):
    placed = (
        P(("groups", "ep"), "tp"),
        P(("groups", "ep"), "tp"),
        P(("groups", "ep"), "tp"),
        P(("groups", "ep"), "tp"),
        P(("groups", "ep"), None, "tp"),
        P(("groups", "ep"), None, "tp"),
        P(("groups", "ep")),
        P("tp"),
        P("tp", None),
        P(None, ("ep", "tp")),
        P(None, ("ep", "tp")),
        P(("ep", "tp"), None),
        P("tp", None),
        P(None, ("ep", "tp")),
        P(("groups", "ep"), None),
        P(("groups", "ep")),
    )
    return jax.shard_map(
        per_device, mesh=mesh, in_specs=placed, out_specs=P(("groups", "ep"), "tp"), check_vma=False
    )
```

```python
import functools

import jax
import jax.numpy as jnp
from jax import lax
from jax.experimental import pallas as pl
from jax.experimental.pallas import tpu as pltpu
from jax.sharding import PartitionSpec as P

HEADS = 24
KVH = 8
HD = 128
EXPERT_COUNT = 4
ADAPTER_RANK = 16
TENANT_COUNT = 8
CAP = 10
LANES = 128
ADAPTER_LANES = EXPERT_COUNT * ADAPTER_RANK
DIFF_HI, DIFF_LO, SQ_HI, SQ_LO, FIRST, SECOND, TENANT = range(ADAPTER_LANES, ADAPTER_LANES + 7)
F32 = jnp.float32
BF16 = jnp.bfloat16
ANY_LANES = (((1,), (1,)), ((), ()))


VMEM = pl.BlockSpec(memory_space=pltpu.VMEM)
HBM = pl.BlockSpec(memory_space=pl.ANY)


def in_hbm(*arrays):
    return [pltpu.with_memory_space_constraint(array, pltpu.HBM) for array in arrays]


def column(values, rows):
    index = lax.broadcasted_iota(jnp.int32, (rows, LANES), 0)
    out = jnp.zeros((rows, LANES), jnp.int32)
    for r in range(rows):
        out = jnp.where(index == r, values(r), out)
    return out


def at_distance(distance, size):
    return pl.ds(pl.multiple_of((lax.axis_index("tp") ^ distance) * size, size), size)


def attend_kernel(*refs):
    count = 12
    sources, outs, buffers, arrived = refs[:count], refs[count : count + 2], refs[count + 2 : -1], refs[-1]
    copies = [
        pltpu.make_async_copy(source, buffer, arrived.at[i])
        for i, (source, buffer) in enumerate(zip(sources, buffers, strict=True))
    ]
    for i in (7, 4, 0, 5, 8, 6, 3, 9, 1, 2, 10, 11):
        copies[i].start()
    attend_body(*buffers, *outs, wait=lambda *which: [copies[i].wait() for i in which])


def attend_body(
    lengths,
    tenants,
    routes,
    residual,
    queries,
    token_keys,
    token_values,
    stored_keys,
    stored_values,
    gain,
    router,
    adapter_down,
    state_out,
    payload_out,
    *,
    wait,
):
    rows, features = residual.shape
    kv_local = token_keys.shape[1] // HD
    cache = stored_keys.shape[1]
    group = HEADS // KVH
    scale = HD ** (-0.5)
    wait(0, 4, 7)
    heads = kv_local * group
    together = 2 if rows % 2 == 0 else 1
    length_column = column(lambda r: lengths[r], rows)
    stacked_length = jnp.concatenate([length_column[:, :1]] * heads, axis=0)
    stacked_row = lax.rem(
        lax.broadcasted_iota(jnp.int32, (heads * rows, cache), 0), jnp.int32(rows)
    )
    visible = lax.broadcasted_iota(jnp.int32, (heads * rows, cache), 1) < stacked_length

    def stacked(get):
        return jnp.concatenate([get(g, j) for g in range(kv_local) for j in range(group)], axis=0)

    def head_lanes(g, j=None):
        h = g if j is None else g * group + j
        return slice(h * HD, (h + 1) * HD)

    query = stacked(lambda g, j: queries[:, head_lanes(g, j)])
    wide = jnp.concatenate([query] * kv_local, axis=1)
    lane_head = lax.broadcasted_iota(jnp.int32, wide.shape, 1) // HD
    row_head = lax.broadcasted_iota(jnp.int32, wide.shape, 0) // (group * rows)
    wide = jnp.where(lane_head == row_head, wide.astype(F32), 0.0).astype(BF16)
    scores = jnp.zeros((heads * rows, cache), F32)
    for r in range(0, rows, together):
        keys = stored_keys[r : r + together].reshape(together * cache, kv_local * HD)
        every = lax.dot_general(wide, keys, ANY_LANES, preferred_element_type=F32)
        for i in range(together):
            scores = jnp.where(
                stacked_row == r + i, every[:, i * cache : (i + 1) * cache], scores
            )
    scores = jnp.where(visible, scores * scale, -jnp.inf)
    wait(5)
    fresh_key = stacked(lambda g, j: token_keys[:, head_lanes(g)].astype(F32))
    fresh = jnp.sum(query.astype(F32) * fresh_key, axis=1, keepdims=True) * scale
    largest = jnp.maximum(jnp.max(scores, axis=1, keepdims=True), fresh)
    cache_exp = jnp.exp(scores - largest)
    fresh_exp = jnp.exp(fresh - largest)
    denominator = jnp.sum(cache_exp, axis=1, keepdims=True) + fresh_exp
    probs = cache_exp / denominator
    fresh_prob = (fresh_exp / denominator).astype(BF16).astype(F32)
    wait(8)
    every = jnp.zeros((heads * rows, kv_local * HD), F32)
    for r in range(0, rows, together):
        values = stored_values[r : r + together].reshape(together * cache, kv_local * HD)
        own = [jnp.where(stacked_row == r + i, probs, 0.0).astype(BF16) for i in range(together)]
        every = every + jnp.dot(
            jnp.concatenate(own, axis=1), values, preferred_element_type=F32
        )
    wait(3, 6, 9)
    squares = jnp.zeros((rows, 1), F32)
    for g in range(kv_local):
        fresh_value = token_values[:, head_lanes(g)].astype(F32)
        for j in range(group):
            lanes = head_lanes(g, j)
            place = slice((g * group + j) * rows, (g * group + j + 1) * rows)
            attended = every[place, head_lanes(g)] + fresh_prob[place] * fresh_value
            state = (residual[:, lanes].astype(F32) + attended).astype(BF16)
            state_out[:, lanes] = state
            state = state.astype(F32)
            squares = squares + jnp.sum(state * state, axis=1, keepdims=True)
            payload_out[:, lanes] = (
                state * gain[lanes.start // LANES : lanes.start // LANES + 1, :]
            ).astype(BF16)
    wait(1, 2, 10, 11)
    scaled = payload_out[:, :features]
    logits = lax.dot_general(scaled, router[...], ANY_LANES, preferred_element_type=F32)
    first = column(lambda r: routes[0, r], rows)
    second = column(lambda r: routes[1, r], rows)
    tenant = column(lambda r: tenants[r], rows)
    expert = lax.broadcasted_iota(jnp.int32, logits.shape, 1)
    chosen = jnp.where(expert == first[:, :EXPERT_COUNT], logits, 0.0) - jnp.where(
        expert == second[:, :EXPERT_COUNT], logits, 0.0
    )
    diff = jnp.sum(chosen, axis=1, keepdims=True)
    adapter = jnp.dot(scaled, adapter_down[...], preferred_element_type=F32)
    lane = lax.broadcasted_iota(jnp.int32, (rows, LANES), 1)
    tail = jnp.zeros((rows, LANES), F32)
    for start in range(0, adapter.shape[1], LANES):
        owner = (lane + start) // ADAPTER_LANES
        tail = tail + jnp.where(owner == tenant, adapter[:, start : start + LANES], 0.0)
    tail = tail + pltpu.roll(tail, ADAPTER_LANES, 1)
    diff_hi = diff.astype(BF16).astype(F32)
    squares_hi = squares.astype(BF16).astype(F32)
    for place, value in (
        (DIFF_HI, diff_hi),
        (DIFF_LO, diff - diff_hi),
        (SQ_HI, squares_hi),
        (SQ_LO, squares - squares_hi),
        (FIRST, first.astype(F32)),
        (SECOND, second.astype(F32)),
        (TENANT, tenant.astype(F32)),
    ):
        tail = jnp.where(lane == place, value, tail)
    payload_out[:, features:] = tail.astype(BF16)


def attend(args):
    rows, features = args[3].shape
    return pl.pallas_call(
        attend_kernel,
        out_shape=(
            jax.ShapeDtypeStruct((rows, features), BF16),
            jax.ShapeDtypeStruct((rows, features + LANES), BF16),
        ),
        in_specs=[HBM] * len(args),
        out_specs=(VMEM,) * 2,
        scratch_shapes=[
            (pltpu.SMEM if i < 3 else pltpu.VMEM)(arg.shape, arg.dtype)
            for i, arg in enumerate(args)
        ]
        + [pltpu.SemaphoreType.DMA((len(args),))],
        compiler_params=pltpu.CompilerParams(vmem_limit_bytes=6 * 2**20),
        cost_estimate=pl.CostEstimate(
            flops=200_000_000, bytes_accessed=3_000_000, transcendentals=20_000
        ),
        name="attend",
    )(*in_hbm(*args))


def fetch(down_weight, distances, parts, arrived):
    copies = [
        pltpu.make_async_copy(
            down_weight.at[:, at_distance(distance, part.shape[1])], part, arrived.at[i]
        )
        for i, (distance, part) in enumerate(zip(distances, parts, strict=True))
    ]
    for copy in copies:
        copy.start()
    return copies


def halves(hidden):
    return hidden // 2 if hidden % (2 * LANES) == 0 else hidden


def partial_kernel(distance, fetched, first, soon, block, gate_weight, up_weight, *refs):
    hidden = gate_weight.shape[1]
    features = block.shape[1] - LANES
    sums, refs = (None, refs) if first else (refs[0], refs[1:])
    down_weight, totals = refs[0], refs[1 + soon]
    copies = fetch(down_weight, fetched, refs[2 + soon : -1], refs[-1])
    tile = halves(hidden)
    depth = at_distance(distance, features)

    def products(n, carry):
        lanes = pl.ds(pl.multiple_of(n * tile, tile), tile)
        for i, weight in enumerate((gate_weight, up_weight)):
            product = jnp.dot(
                block[:, :features], weight[depth, lanes], preferred_element_type=F32
            )
            totals[i, :, lanes] = product if first else sums[i, :, lanes] + product
        return carry

    lax.fori_loop(0, hidden // tile, products, 0)
    for copy in copies:
        copy.wait()


def partial(block, distance, sums, gate_weight, up_weight, down_weight, fetched, soon):
    rows, width = block.shape
    features = width - LANES
    hidden = gate_weight.shape[1]
    first = sums is None
    return pl.pallas_call(
        functools.partial(partial_kernel, distance, fetched, first, len(soon)),
        out_shape=(
            jax.ShapeDtypeStruct((2, rows, hidden), F32),
            *[jax.ShapeDtypeStruct((hidden, features), BF16)] * len(fetched),
        ),
        in_specs=[VMEM] * (3 if first else 4) + [HBM] * (1 + len(soon)),
        out_specs=(VMEM,) * (1 + len(fetched)),
        scratch_shapes=[pltpu.SemaphoreType.DMA((max(1, len(fetched)),))],
        compiler_params=pltpu.CompilerParams(vmem_limit_bytes=3 * 2**20),
        cost_estimate=pl.CostEstimate(
            flops=4 * rows * features * hidden,
            bytes_accessed=2 * features * hidden,
            transcendentals=0,
        ),
        name="partial",
    )(block, gate_weight, up_weight, *(() if first else (sums,)), *in_hbm(down_weight), *soon)


def expert_kernel(replicas, late, following, order, known, early, sums, *refs):
    tensor_devices = len(order)
    blocks, refs = refs[:tensor_devices], refs[tensor_devices:]
    gate_weight, up_weight, adapter_up, refs = *refs[:3], refs[3:]
    early_parts, refs = refs[:early], refs[early:]
    down_weight, out, active, refs = *refs[:3], refs[3:]
    next_parts, late_parts, arrived = refs[: len(following)], refs[len(following) : -1], refs[-1]
    rows, width = blocks[0].shape
    features = width - LANES
    hidden = active.shape[1]
    copies = fetch(down_weight, late + following, (*late_parts, *next_parts), arrived)
    tile = halves(hidden)

    @pl.when(lax.axis_index("tp") >= 0)
    def _():
        expert = lax.axis_index("ep") // replicas
        tail = jnp.zeros((rows, LANES), F32)
        for block in blocks:
            tail = tail + block[:, features:].astype(F32)
        place = lambda k: tail[:, k : k + 1]
        here = blocks[0][:, features:].astype(F32)
        inverse_rms = lax.rsqrt(
            (place(SQ_HI) + place(SQ_LO)) / (features * tensor_devices) + 1e-05
        )
        diff = (place(DIFF_HI) + place(DIFF_LO)) * inverse_rms
        expert_float = expert.astype(F32)
        is_first = here[:, FIRST : FIRST + 1] == expert_float
        is_second = here[:, SECOND : SECOND + 1] == expert_float
        weight = jnp.where(
            is_first, jax.nn.sigmoid(diff), jnp.where(is_second, jax.nn.sigmoid(-diff), 0.0)
        )
        lowrank = (tail * inverse_rms).astype(BF16)
        spread_shape = (LANES, TENANT_COUNT * ADAPTER_RANK)
        source = lax.broadcasted_iota(jnp.int32, spread_shape, 0)
        target = lax.broadcasted_iota(jnp.int32, spread_shape, 1)
        spread = jnp.where(
            source == expert * ADAPTER_RANK + lax.rem(target, jnp.int32(ADAPTER_RANK)), 1.0, 0.0
        ).astype(BF16)
        lane = lax.broadcasted_iota(jnp.int32, (rows, TENANT_COUNT * ADAPTER_RANK), 1)
        own_tenant = (lane // ADAPTER_RANK).astype(F32) == here[:, TENANT : TENANT + 1]
        adapter_rows = jnp.where(
            own_tenant, jnp.dot(lowrank, spread, preferred_element_type=F32), 0.0
        ).astype(BF16)
        for start in range(0, hidden, tile):
            lanes = slice(start, start + tile)
            gate, up = sums[0, :, lanes], sums[1, :, lanes]
            for block, distance in zip(blocks[known:], order[known:], strict=True):
                scaled = block[:, :features]
                depth = at_distance(distance, features)
                gate = gate + jnp.dot(
                    scaled, gate_weight[depth, lanes], preferred_element_type=F32
                )
                up = up + jnp.dot(scaled, up_weight[depth, lanes], preferred_element_type=F32)
            gate = gate * inverse_rms
            up = up * inverse_rms + jnp.dot(
                adapter_rows, adapter_up[:, lanes], preferred_element_type=F32
            )
            active[:, lanes] = (gate * jax.nn.sigmoid(gate) * up * weight).astype(BF16)
        for i, part in enumerate((*early_parts, *late_parts)):
            if i >= early:
                copies[i - early].wait()
            out[i] = jnp.dot(active[...], part[...], preferred_element_type=F32).astype(out.dtype)

    for copy in copies[len(late) :]:
        copy.wait()


def experts(
    replicas, late, following, order, sums, known, blocks, gate_weight, up_weight, adapter_up, parts, down_weight
):
    rows, width = blocks[0].shape
    features, hidden = width - LANES, sums.shape[2]
    count = len(parts) + len(late)
    columns = (hidden, features)
    return pl.pallas_call(
        functools.partial(expert_kernel, replicas, late, following, order, known, len(parts)),
        out_shape=(
            jax.ShapeDtypeStruct((count, rows, features), BF16),
            jax.ShapeDtypeStruct((rows, hidden), BF16),
            *[jax.ShapeDtypeStruct(columns, BF16)] * len(following),
        ),
        in_specs=[VMEM] * (4 + len(blocks) + len(parts)) + [HBM],
        out_specs=(VMEM,) * (2 + len(following)),
        scratch_shapes=[pltpu.VMEM(columns, BF16)] * len(late)
        + [pltpu.SemaphoreType.DMA((len(late) + len(following),))],
        compiler_params=pltpu.CompilerParams(vmem_limit_bytes=5 * 2**20),
        cost_estimate=pl.CostEstimate(
            flops=2 * rows * hidden * features * (2 * (len(blocks) - known) + count),
            bytes_accessed=2 * hidden * features * (len(late) + len(following)),
            transcendentals=0,
        ),
        name="experts",
    )(sums, *blocks, gate_weight, up_weight, adapter_up, *parts, *in_hbm(down_weight))


def down_kernel(active, after, *refs):
    *parts, out = refs
    for i, part in enumerate(parts):
        out[i] = jnp.dot(active[...], part[...], preferred_element_type=F32)


def down_fetching_kernel(targets, active, after, down_weight, out, parts, arrived):
    hidden = active.shape[1]
    tile = halves(hidden)
    pieces = [(i, start) for i in range(len(targets)) for start in range(0, hidden, tile)]
    copies = []
    for n, (i, start) in enumerate(pieces):
        lanes = at_distance(targets[i], out.shape[2])
        copies.append(
            pltpu.make_async_copy(
                down_weight.at[pl.ds(start, tile), lanes],
                parts.at[i, pl.ds(start, tile), :],
                arrived.at[n],
            )
        )
        copies[-1].start()
    for (i, start), copy in zip(pieces, copies, strict=True):
        copy.wait()
        product = jnp.dot(
            active[:, start : start + tile],
            parts[i, start : start + tile, :],
            preferred_element_type=F32,
        )
        out[i] = out[i] + product if start else product


def down(targets, active, parts, down_weight, features, after):
    rows, hidden = active.shape
    count = len(targets)
    scratch = (
        pltpu.VMEM((count, hidden, features), BF16),
        pltpu.SemaphoreType.DMA((count * (hidden // halves(hidden)),)),
    )
    return pl.pallas_call(
        down_kernel if parts else functools.partial(down_fetching_kernel, targets),
        out_shape=jax.ShapeDtypeStruct((count, rows, features), F32),
        in_specs=[VMEM, HBM] + ([VMEM] * count if parts else [HBM]),
        out_specs=VMEM,
        scratch_shapes=() if parts else scratch,
        compiler_params=pltpu.CompilerParams(vmem_limit_bytes=5 * 2**20),
        cost_estimate=pl.CostEstimate(
            flops=2 * rows * hidden * features * count,
            bytes_accessed=2 * hidden * features * count,
            transcendentals=0,
        ),
        name="down",
    )(active, after, *(parts if parts else in_hbm(down_weight)))


def join_kernel(first, second, *refs):
    out = refs[-1]
    count = first.shape[0]
    out[:count] = first[...]
    out[count:] = second[...]


def join(first, second, *after):
    return pl.pallas_call(
        join_kernel,
        out_shape=jax.ShapeDtypeStruct((2 * first.shape[0], *first.shape[1:]), first.dtype),
        in_specs=[VMEM, VMEM] + [HBM] * len(after),
        out_specs=VMEM,
        compiler_params=pltpu.CompilerParams(vmem_limit_bytes=1 * 2**20),
        name="join",
    )(first, second, *after)


def pack_kernel(replicas, first, second, *refs):
    packed, place = refs[-2:]
    rows, slots = place.shape
    half = first.shape[0]
    features = first.shape[1] - LANES
    every = jnp.concatenate([first[...], second[...]], axis=0)
    tail = every[:, features:].astype(F32)
    expert = (lax.axis_index("ep") // replicas).astype(F32)
    named = jnp.where(
        (tail[:, FIRST : FIRST + 1] == expert) | (tail[:, SECOND : SECOND + 1] == expert), 1.0, 0.0
    )
    row = lax.broadcasted_iota(jnp.int32, (rows, rows), 0)
    before = jnp.where(lax.broadcasted_iota(jnp.int32, (rows, rows), 1) < row, 1.0, 0.0)
    named = jnp.broadcast_to(named, (rows, slots))
    slot = jnp.dot(before.astype(BF16), named.astype(BF16), preferred_element_type=F32)
    lane = lax.broadcasted_iota(jnp.int32, (rows, slots), 1).astype(F32)
    at = jnp.where(lane == slot, named, 0.0)
    place[...] = at.astype(BF16)
    packed[...] = lax.dot_general(
        at.astype(BF16), every, (((0,), (0,)), ((), ())), preferred_element_type=F32
    ).astype(BF16)


def pack(first, second, replicas, slots, *after):
    rows, width = 2 * first.shape[0], first.shape[1]
    return pl.pallas_call(
        functools.partial(pack_kernel, replicas),
        out_shape=(
            jax.ShapeDtypeStruct((slots, width), BF16),
            jax.ShapeDtypeStruct((rows, slots), BF16),
        ),
        in_specs=[VMEM, VMEM] + [HBM] * len(after),
        out_specs=(VMEM, VMEM),
        compiler_params=pltpu.CompilerParams(vmem_limit_bytes=4 * 2**20),
        name="pack",
    )(first, second, *after)


def unpack_kernel(place, made, *refs):
    *arrived, kept, sent = refs
    total = made[0]
    for block in arrived:
        total = total + block[0].astype(F32)
    high = total.astype(BF16)
    low = (total - high.astype(F32)).astype(BF16)
    at = place[...]
    full = jnp.dot(at, high, preferred_element_type=F32) + jnp.dot(
        at, low, preferred_element_type=F32
    )
    rows = kept.shape[1]
    for j in range(kept.shape[0]):
        kept[j] = full[2 * j * rows : (2 * j + 1) * rows]
        sent[j] = full[(2 * j + 1) * rows : (2 * j + 2) * rows].astype(BF16)


def unpack(place, made, arrived, rows):
    features = made.shape[2]
    pairs = place.shape[0] // (2 * rows)
    return pl.pallas_call(
        unpack_kernel,
        out_shape=(
            jax.ShapeDtypeStruct((pairs, rows, features), F32),
            jax.ShapeDtypeStruct((pairs, rows, features), BF16),
        ),
        in_specs=[VMEM] * (2 + len(arrived)),
        out_specs=(VMEM, VMEM),
        compiler_params=pltpu.CompilerParams(vmem_limit_bytes=4 * 2**20),
        name="unpack",
    )(place, made, *arrived)


def mark_kernel(after, *refs):
    out = refs[-1]
    out[...] = jnp.zeros_like(out)


def mark(after, *weights):
    return pl.pallas_call(
        mark_kernel,
        out_shape=jax.ShapeDtypeStruct((8, LANES), F32),
        in_specs=[HBM] * (1 + len(weights)),
        out_specs=VMEM,
        compiler_params=pltpu.CompilerParams(vmem_limit_bytes=2**20),
        name="mark",
    )(after, *in_hbm(*weights))


def tie_kernel(array, after, out):
    pass


def tie(array, after):
    return pl.pallas_call(
        tie_kernel,
        out_shape=jax.ShapeDtypeStruct(array.shape, array.dtype),
        in_specs=[HBM, HBM],
        out_specs=HBM,
        input_output_aliases={0: 0},
        compiler_params=pltpu.CompilerParams(vmem_limit_bytes=2**20),
        name="tie",
    )(array, after)


def swap(x, axis, distance):
    count = lax.axis_size(axis)
    return lax.ppermute(x, axis, [(i, i ^ distance) for i in range(count)])


def bits(count):
    return [1 << b for b in range(count.bit_length() - 1)]


def per_device(
    residual,
    queries,
    token_keys,
    token_values,
    stored_keys,
    stored_values,
    lengths,
    norm_gain_vector,
    router,
    expert_gate_weight,
    expert_up_weight,
    expert_down_weight,
    adapter_down_map,
    adapter_up_map,
    routes,
    tenants,
):
    rows, features = residual.shape
    expert_devices = lax.axis_size("ep")
    tensor_devices = lax.axis_size("tp")
    state, held = attend(
        (
            lengths,
            tenants,
            routes.T,
            residual,
            queries,
            token_keys,
            token_values,
            stored_keys,
            stored_values,
            norm_gain_vector.reshape(features // LANES, LANES),
            router.T,
            adapter_down_map,
        ),
    )
    replicas = expert_devices // EXPERT_COUNT
    for distance in bits(expert_devices):
        other = swap(held, "ep", distance)
        last = 2 * distance == expert_devices
        beside = mark(held, *((expert_down_weight,) if last else (expert_down_weight, expert_gate_weight, expert_up_weight)))
        if last:
            slots = expert_devices * CAP
            held, place = pack(held, other, replicas, slots, beside, expert_up_weight)
        else:
            held = join(held, other, beside)
    steps = bits(tensor_devices)
    groups = [tuple(k for k in range(tensor_devices) if k & -k == step) for step in steps] + [(0,)]
    early, late = groups[0][-1:], groups[0][1:-1]
    blocks, order, known, sums, parts = [held], [0], 0, None, []
    for distance in reversed(steps):
        others = [swap(block, "tp", distance) for block in blocks]
        for block in blocks[known:]:
            sums, *more = partial(
                block,
                order[known],
                sums,
                expert_gate_weight,
                expert_up_weight,
                expert_down_weight,
                () if known else early,
                () if known else (expert_gate_weight, adapter_up_map),
            )
            parts += more
            known += 1
        blocks = blocks + [tie(block, sums) if distance > 1 else block for block in others]
        order = order + [at ^ distance for at in order]
    sent, active, *parts = experts(
        replicas,
        late,
        groups[1] + (1,),
        tuple(order),
        sums,
        known,
        blocks,
        expert_gate_weight,
        expert_up_weight,
        adapter_up_map,
        parts,
        expert_down_weight,
    )
    received = {k: [] for k in range(tensor_devices)}
    groups[0] = early + late
    for step, group, following in zip(steps, groups[:-1], groups[1:], strict=True):
        arriving = swap(sent, "tp", step)
        more = (1,) if parts else ()
        made = down(following + more, active, parts, expert_down_weight, features, sent)
        if more:
            received[0].append(swap(made[-1:].astype(BF16), "tp", 1)[0])
        parts = []
        for i, k in enumerate(group):
            received[k ^ step].append(arriving[i])
        if following != (0,):
            kept = [
                sum((block.astype(F32) for block in received[k]), made[i])
                for i, k in enumerate(following)
            ]
            sent = jnp.stack([block.astype(BF16) for block in kept])
    kept, sent = unpack(place, made, [block[None] for block in received[0]], rows)
    for distance in bits(expert_devices):
        if distance > 1:
            kept, sent = kept[0::2], kept[1::2].astype(BF16)
        kept = kept + swap(sent, "ep", distance).astype(F32)
    return (state.astype(F32) + kept[0]).astype(BF16)


def solution(mesh):
    placed = (
        P(("groups", "ep"), "tp"),
        P(("groups", "ep"), "tp"),
        P(("groups", "ep"), "tp"),
        P(("groups", "ep"), "tp"),
        P(("groups", "ep"), None, "tp"),
        P(("groups", "ep"), None, "tp"),
        P(("groups", "ep")),
        P("tp"),
        P("tp", None),
        P(None, ("ep", "tp")),
        P(None, ("ep", "tp")),
        P(("ep", "tp"), None),
        P("tp", None),
        P(None, ("ep", "tp")),
        P(("groups", "ep"), None),
        P(("groups", "ep")),
    )
    return jax.shard_map(
        per_device, mesh=mesh, in_specs=placed, out_specs=P(("groups", "ep"), "tp"), check_vma=False
    )
```
